32 devices in a mesh: ctx: 8 (over z, x), wshard: 4 (over y, core).
Axes of the slice: x: 2, y: 2, z: 4, core: 2. Of those that a mesh axis runs over, the one named last changes fastest.
Arguments:
- inputs: bfloat16 [4096, 2048], P(('ctx', 'wshard')), may hold values from -6 to 6
- span_order: int32 [64], replicated, may hold values from 0 to 63, each once
- attn_gain: bfloat16 [2048], P('wshard'), may hold values from 0.5 to 1.5
- query_weight: bfloat16 [2048, 2048], P('wshard'), may hold values from -0.125 to 0.125
- key_weight: bfloat16 [2048, 512], P('wshard'), may hold values from -0.125 to 0.125
- value_weight: bfloat16 [2048, 512], P('wshard'), may hold values from -0.125 to 0.125
- output_weight: bfloat16 [2048, 2048], P('wshard'), as said below
- ffn_gain: bfloat16 [2048], P('wshard'), may hold values from 0.5 to 1.5
- gate_weight: bfloat16 [2048, 8192], P('wshard'), may hold values from -0.125 to 0.125
- up_weight: bfloat16 [2048, 8192], P('wshard'), may hold values from -0.125 to 0.125
- down_weight: bfloat16 [8192, 2048], P('wshard'), may hold values from -0.0625 to 0.0625
- cotangent: bfloat16 [4096, 2048], P(('ctx', 'wshard')), may hold values from -6 to 6
Outputs:
- outputs: bfloat16 [4096, 2048], P(('ctx', 'wshard'))
- input_grad: float32 [4096, 2048], P(('ctx', 'wshard'))
- attn_gain_grad: float32 [2048], P('wshard')
- query_grad: float32 [2048, 2048], P('wshard')
- key_grad: float32 [2048, 512], P('wshard')
- value_grad: float32 [2048, 512], P('wshard')
- output_grad: float32 [2048, 2048], P('wshard')
- ffn_gain_grad: float32 [2048], P('wshard')
- gate_grad: float32 [2048, 8192], P('wshard')
- up_grad: float32 [2048, 8192], P('wshard')
- down_grad: float32 [8192, 2048], P('wshard')
The draws below stay inside these ranges and needn't reach their ends.
Inputs may be any that keep to these rules, and one draw needn't show every extreme that they name: `span_order`: every number of 0 to 63 appears once. `output_weight`: independent entries of mean zero.
All inputs are finite; a program needn't handle non-finite values.
Results may differ from the reference program's by a relative error of at most 0.02.
Values may be sent and summed in bfloat16 or wider, within the bound.
No kernel may reach another device: no remote copies, remote signals or barrier semaphores. Data moves between devices by JAX's collectives and lax.ppermute only.
A program may use at most 448 MiB of HBM per device.

```python
import math
import jax
import jax.numpy as jnp
from jax import lax

D = 2048
H = 32
KVH = 8
HD = 64
FF = 8192
TOK_DEV = 128
SPANS = 64
TOKENS = 4096


def draw_output_weight(key, part):
    key = jax.random.fold_in(key, 7)
    spread = math.sqrt(TOKENS / (4.0 * H * HD))
    entries = jax.random.truncated_normal(key, -6.0, 6.0, (H * HD, D), jnp.float32)
    return (entries * spread).astype(jnp.bfloat16)


def level_of(own_key, shape, shards, low, high):
    gain = 1.0
    for position, parts in shards:
        draws = jax.random.uniform(jax.random.fold_in(jax.random.fold_in(own_key, 6), position), (parts,), jnp.float32, low / len(shards), high / len(shards))
        gain = gain * jnp.repeat(jnp.exp(draws), shape[position] // parts).reshape((-1,) + (1,) * (len(shape) - 1 - position))
    return gain


def noise(own_key, dims, scale, most, cuts=(), kind=jnp.bfloat16):
    drawn = scale * jax.random.normal(own_key, dims, jnp.float32)
    if cuts:
        drawn = drawn * level_of(own_key, dims, cuts, -0.22, 0.18)
    return jnp.clip(drawn, -most, most).astype(kind)


def setup_inputs(seed: int = 0) -> dict:
    key_list = jax.random.split(jax.random.key(seed), 13)
    inputs = noise(key_list[0], (TOKENS, D), 1.0, 6.0, ((0, 32),))
    span_order = jax.random.permutation(key_list[1], SPANS).astype(jnp.int32)
    attn_gain = jnp.clip(1.0 + 0.1 * jax.random.normal(key_list[2], (D,), jnp.float32), 0.5, 1.5).astype(jnp.bfloat16)
    query_weight = noise(key_list[3], (D, H * HD), D ** -0.5, 0.125, ((0, 4),))
    key_weight = noise(key_list[4], (D, KVH * HD), D ** -0.5, 0.125, ((0, 4),))
    value_weight = noise(key_list[5], (D, KVH * HD), D ** -0.5, 0.125, ((0, 4),))
    output_weight = draw_output_weight(jax.random.fold_in(key_list[12], 71), 0)
    ffn_gain = jnp.clip(1.0 + 0.1 * jax.random.normal(key_list[7], (D,), jnp.float32), 0.5, 1.5).astype(jnp.bfloat16)
    gate_weight = noise(key_list[8], (D, FF), D ** -0.5, 0.125, ((0, 4),))
    up_weight = noise(key_list[9], (D, FF), D ** -0.5, 0.125, ((0, 4),))
    down_weight = noise(key_list[10], (FF, D), FF ** -0.5, 0.0625, ((0, 4),))
    cotangent = noise(key_list[11], (TOKENS, D), 1.0, 6.0, ((0, 32),))
    return {"inputs": inputs, "span_order": span_order, "attn_gain": attn_gain, "query_weight": query_weight, "key_weight": key_weight, "value_weight": value_weight, "output_weight": output_weight, "ffn_gain": ffn_gain, "gate_weight": gate_weight, "up_weight": up_weight, "down_weight": down_weight, "cotangent": cotangent}


@jax.custom_vjp
def low(v):
    return lax.optimization_barrier(v.astype(jnp.bfloat16)).astype(jnp.float32)

@jax.custom_vjp
def low_back(v):
    return v

def low_keep(v):
    return (low(v), None)

def low_pass(kept, grad):
    return (grad,)

def back_keep(v):
    return (v, None)

def back_low(kept, grad):
    return (low(grad),)
low.defvjp(low_keep, low_pass)
low_back.defvjp(back_keep, back_low)
epsilon = 1e-05
rope_base = 500000.0
masked_score = -1e+30

def product(left, right):
    return jnp.dot(left, right, precision=lax.Precision.HIGHEST)

def rms_scale(vector, scale_gain):
    return vector * lax.rsqrt(lax.optimization_barrier(jnp.mean(vector * vector, axis=-1, keepdims=True)) + epsilon) * scale_gain

def rotary_tables(positions, width):
    half_width = width // 2
    frequency = jnp.power(rope_base, -jnp.arange(half_width, dtype=jnp.float32) * 2.0 / width)
    angles = positions.astype(jnp.float32)[:, None] * frequency[None, :]
    return (jnp.cos(angles), jnp.sin(angles))

def rotate(vector, cosine, sine):
    half_width = vector.shape[-1] // 2
    first = vector[..., :half_width]
    second = vector[..., half_width:]
    cos_part = cosine[:, None, :]
    sin_part = sine[:, None, :]
    return jnp.concatenate([first * cos_part - second * sin_part, second * cos_part + first * sin_part], axis=-1)

def attention(queries, key_rows, value_rows, positions):
    row_count = math.gcd(TOKENS, 512)
    group = H // KVH
    scale = HD ** (-0.5)

    def one_block(counter):
        block_number = counter // KVH
        head_number = counter % KVH
        query_block = lax.dynamic_slice(queries, (block_number * row_count, head_number * group, jnp.int32(0)), (row_count, group, HD))
        key_head = lax.dynamic_slice_in_dim(key_rows, head_number, 1, 1)[:, 0, :]
        value_head = lax.dynamic_slice_in_dim(value_rows, head_number, 1, 1)[:, 0, :]
        query_pos = lax.dynamic_slice_in_dim(positions, block_number * row_count, row_count, 0)
        raw = jnp.einsum('qgd,kd->gqk', query_block, key_head, precision=lax.Precision.HIGHEST)
        scores = low_back(raw * scale)
        allowed = positions[None, :] <= query_pos[:, None]
        row_max = lax.optimization_barrier(jnp.max(jnp.where(allowed, scores, masked_score), axis=-1, keepdims=True))
        weights = jnp.where(allowed, jnp.exp(scores - row_max), 0.0)
        probs = low(weights / lax.optimization_barrier(jnp.sum(weights, axis=-1, keepdims=True)))
        return jnp.einsum('gqk,kd->qgd', probs, value_head, precision=lax.Precision.HIGHEST)
    counters = jnp.arange(TOKENS // row_count * KVH, dtype=jnp.int32)
    blocks = lax.map(jax.checkpoint(one_block), counters)
    blocks = blocks.reshape(TOKENS // row_count, KVH, row_count, group, HD)
    return blocks.transpose(0, 2, 1, 3, 4).reshape(TOKENS, H * HD)

def reference(inputs, span_order, attn_gain, query_weight, key_weight, value_weight, output_weight, ffn_gain, gate_weight, up_weight, down_weight, cotangent):
    span_len = TOK_DEV // 2
    positions = (span_order[:, None] * span_len + jnp.arange(span_len, dtype=jnp.int32)[None, :]).reshape(TOKENS).astype(jnp.int32)
    cosine, sine = rotary_tables(positions, HD)

    def forward(floats_in, gain_one, query_full, key_full, value_full, output_full, gain_two, gate_full, up_full, down_full):
        normed_one = low(rms_scale(floats_in, gain_one))
        queries = low(rotate(low_back(product(normed_one, query_full)).reshape(TOKENS, H, HD), cosine, sine))
        key_rows = low(rotate(low_back(product(normed_one, key_full)).reshape(TOKENS, KVH, HD), cosine, sine))
        value_rows = low(low_back(product(normed_one, value_full))).reshape(TOKENS, KVH, HD)
        attended = low(low_back(attention(queries, key_rows, value_rows, positions)))
        residual = floats_in + low_back(product(attended, output_full))
        normed_two = low(rms_scale(residual, gain_two))
        gate_pre = low_back(product(normed_two, gate_full))
        up_pre = low_back(product(normed_two, up_full))
        hidden = low(jax.nn.silu(gate_pre) * up_pre)
        return residual + low_back(product(hidden, down_full))
    floats = (inputs.astype(jnp.float32), attn_gain.astype(jnp.float32), query_weight.astype(jnp.float32), key_weight.astype(jnp.float32), value_weight.astype(jnp.float32), output_weight.astype(jnp.float32), ffn_gain.astype(jnp.float32), gate_weight.astype(jnp.float32), up_weight.astype(jnp.float32), down_weight.astype(jnp.float32))
    result, pullback = jax.vjp(forward, *floats)
    grads = pullback(cotangent.astype(jnp.float32))
    return (result.astype(jnp.bfloat16), grads[0], grads[1], grads[2], grads[3], grads[4], grads[5], grads[6], grads[7], grads[8], grads[9])
```

```python
import functools

import jax
import jax.numpy as jnp
from jax import lax
from jax.experimental import pallas as pl
from jax.experimental.pallas import tpu as pltpu
from jax.sharding import Mesh
from jax.sharding import PartitionSpec as P

H = 32
KVH = 8
HD = 64
GROUP = H // KVH

epsilon = 1e-05
rope_base = 500000.0
masked_score = -1e30
f32 = jnp.float32
bf16 = jnp.bfloat16


def rotary_tables(positions, width):
    half_width = width // 2
    frequency = jnp.power(rope_base, -jnp.arange(half_width, dtype=f32) * 2.0 / width)
    angles = frequency[:, None] * positions.astype(f32)[None, :]
    return (jnp.cos(angles), jnp.sin(angles))


def rotate(vector, cosine, sine):
    half_width = vector.shape[-2] // 2
    first = vector[..., :half_width, :]
    second = vector[..., half_width:, :]
    return jnp.concatenate(
        [first * cosine - second * sine, second * cosine + first * sine], axis=-2
    )


def contract(left, right, left_dim, right_dim):
    return lax.dot_general(
        left, right, (((left_dim,), (right_dim,)), ((), ())), preferred_element_type=f32
    )


SLAB = ("xpart", "wshard")


def swap(value, flip):
    return lax.ppermute(value, SLAB, [(i, i ^ flip) for i in range(KVH)])


FLIPS = (0, 2, 4, 6, 1, 3, 5, 7)


def slab_gather(block):
    half = block.shape[0] // 2
    row = swap(block, 2)
    column = swap(block, 4)
    far = jnp.concatenate([swap(row[:half], 4), swap(column[half:], 2)], axis=0)
    near = [block, row, column, far]
    return jnp.concatenate(near + [swap(v, 1) for v in near], axis=0)


def slab_reduce(partial):
    rows = partial.shape[0] // KVH
    half = partial.shape[1] // 2
    partial = partial.reshape(KVH, rows, 2 * half)
    own = partial[:4] + swap(partial[4:].astype(bf16), 1).astype(f32)
    left, right = own[..., :half], own[..., half:]
    left = left[:2] + swap(left[2:].astype(bf16), 4).astype(f32)
    right = right[0::2] + swap(right[1::2].astype(bf16), 2).astype(f32)
    left = left[0] + swap(left[1].astype(bf16), 2).astype(f32)
    right = right[0] + swap(right[1].astype(bf16), 4).astype(f32)
    return jnp.concatenate([left, right], axis=1)


def line_reduce(parts):
    count = parts.shape[0]
    place = lax.axis_index("line")

    def pick(index):
        return lax.dynamic_index_in_dim(
            parts, jnp.clip(index, 0, count - 1), 0, keepdims=False
        )

    up = pick(place * 0 + count - 1)
    down = pick(place * 0)
    for step in range(1, count):
        up_got = lax.ppermute(up, "line", [(i, i + 1) for i in range(step)])
        down_got = lax.ppermute(
            down, "line", [(count - 1 - i, count - 2 - i) for i in range(step)]
        )
        if step < count - 1:
            up = (pick(count - 1 - step + place).astype(f32) + up_got.astype(f32)).astype(bf16)
            down = (pick(place - (count - 1 - step)).astype(f32) + down_got.astype(f32)).astype(
                bf16
            )
    return pick(place).astype(f32) + (up_got.astype(f32) + down_got.astype(f32))


def line_gather(own):
    count = lax.axis_size("line")
    place = lax.axis_index("line")
    ups, downs = [own], [own]
    for step in range(1, count):
        ups.append(lax.ppermute(ups[-1], "line", [(i, i + 1) for i in range(step - 1, count - 1)]))
        downs.append(
            lax.ppermute(downs[-1], "line", [(i + 1, i) for i in range(0, count - step)])
        )
    return [own] + [
        jnp.where(place + k < count, downs[k], ups[count - k]) for k in range(1, count)
    ]


def place_kernel(spots_ref, *refs):
    out_ref = refs[-1]
    halves = spots_ref.shape[0] - 1
    columns = refs[0].shape[-1]
    for turn in range(halves):
        for spot in range(halves):

            @pl.when(spots_ref[1 + turn] == spot)
            def put(turn=turn, spot=spot):
                out_ref[:, spot * columns : (spot + 1) * columns] = refs[turn][0].astype(f32)


def place_columns(total, pieces, spot, sides, count):
    shards, rows, columns = pieces[0].shape
    halves = len(pieces)
    operands = [jnp.stack([spot] + sides).astype(jnp.int32)] + list(pieces)
    specs = [pl.BlockSpec((1, rows, columns), lambda w, spots: (w, 0, 0))] * halves
    aliases = {}
    if total is not None:
        aliases = {len(operands): 0}
        operands.append(total)
        specs.append(pl.BlockSpec(memory_space=pl.ANY))
    return pl.pallas_call(
        place_kernel,
        grid_spec=pltpu.PrefetchScalarGridSpec(
            num_scalar_prefetch=1,
            grid=(shards,),
            in_specs=specs,
            out_specs=pl.BlockSpec((rows, halves * columns), lambda w, spots: (spots[0], w)),
        ),
        out_shape=jax.ShapeDtypeStruct((count * rows, shards * halves * columns), f32),
        input_output_aliases=aliases,
        compiler_params=pltpu.CompilerParams(vmem_limit_bytes=32 * 1024 * 1024),
        cost_estimate=pl.CostEstimate(
            flops=0, transcendentals=0, bytes_accessed=6 * halves * shards * rows * columns
        ),
        name="place_columns",
    )(*operands)


def place_rows(total, pieces, spot, sides, count):
    rows, columns = pieces[0].shape
    halves = len(pieces)
    for piece, side in zip(pieces, sides):
        operands = [jnp.stack([side * count + spot, side * 0]).astype(jnp.int32), piece[None]]
        width = min(columns, 1024)
        specs = [pl.BlockSpec((1, rows, width), lambda w, spots: (0, 0, w))]
        aliases = {}
        if total is not None:
            aliases = {2: 0}
            operands.append(total)
            specs.append(pl.BlockSpec(memory_space=pl.ANY))
        total = pl.pallas_call(
            place_kernel,
            grid_spec=pltpu.PrefetchScalarGridSpec(
                num_scalar_prefetch=1,
                grid=(columns // width,),
                in_specs=specs,
                out_specs=pl.BlockSpec((rows, width), lambda w, spots: (spots[0], w)),
            ),
            out_shape=jax.ShapeDtypeStruct((halves * count * rows, columns), f32),
            input_output_aliases=aliases,
            compiler_params=pltpu.CompilerParams(vmem_limit_bytes=32 * 1024 * 1024),
            cost_estimate=pl.CostEstimate(
                flops=0, transcendentals=0, bytes_accessed=6 * rows * columns
            ),
            name="place_rows",
        )(*operands)
    return total


def place_narrow(total, pieces, spot, sides, count):
    shards, rows, columns = pieces[0].shape
    halves = len(pieces)
    ordered = [pieces[0]]
    if halves == 2:
        ordered = [jnp.where(sides[0] == t, pieces[0], pieces[1]) for t in range(2)]
    block = jnp.concatenate(
        [ordered[t][w] for w in range(shards) for t in range(halves)], axis=1
    ).astype(f32)
    if total is None:
        total = jnp.zeros((count * rows, block.shape[1]), f32)
    return lax.dynamic_update_slice(total, block, (spot * rows, 0))


def spread(own, places):
    count, halves = lax.axis_size("line"), lax.axis_size("xpart")
    place, side = lax.axis_index("line"), lax.axis_index("xpart")
    totals = [None] * len(places)
    sides = [lax.rem(side + halves - turn, halves) for turn in range(halves)]
    for k, block in enumerate(line_gather(own)):
        spot = lax.rem(place + k, count)
        pieces = [block] + [
            lax.ppermute(block, "xpart", [(i, (i + turn) % halves) for i in range(halves)])
            for turn in range(1, halves)
        ]
        totals = [
            put(total, [part(piece) for piece in pieces], spot, sides, count)
            for total, (put, part) in zip(totals, places)
        ]
    return totals


def whole_block(block):
    return block


def spread_rows(reduced):
    return spread(reduced.astype(bf16), [(place_rows, whole_block)])[0]


def spread_columns(reduced, places):
    return spread(lax.all_to_all(reduced.astype(bf16), "wshard", 0, 0, tiled=True), places)


def line_parts(partial):
    count = lax.axis_size("line")
    *lead, rows, columns = partial.shape
    cut = partial.astype(bf16).reshape(*lead, count, rows // count, columns)
    return jnp.moveaxis(cut, -3, 0)


def move_spans(load, store, order_ref, tiles, span):
    lane = lax.broadcasted_iota(jnp.int32, (1, 2 * span), 1)

    def step(t, unused):
        first, second = order_ref[2 * t], order_ref[2 * t + 1]
        left = load(first // 2).astype(f32)
        right = load(second // 2).astype(f32)
        left = jnp.where(first % 2 == 1, pltpu.roll(left, span, 1), left)
        right = jnp.where(second % 2 == 0, pltpu.roll(right, span, 1), right)
        store(t, jnp.where(lane < span, left, right))
        return unused

    lax.fori_loop(0, tiles, step, 0)


def tile_at(index, tile):
    return pl.ds(pl.multiple_of(index * tile, tile), tile)


def block_mask(size):
    return lax.broadcasted_iota(jnp.int32, (size, size), 0) <= lax.broadcasted_iota(
        jnp.int32, (size, size), 1
    )


def forward_kernel(
    size, span, sort_ref, back_ref, range_ref, blocks_ref, out_ref, sorted_ref, float_ref, log_ref, keys_ref
):
    count, unused, width = blocks_ref.shape
    tile = 2 * span
    per = width // tile
    tiles = count * per

    def load(t):
        return blocks_ref[t // per, :, tile_at(t % per, tile)]

    def store(t, value):
        sorted_ref[:, tile_at(t, tile)] = value.astype(bf16)
        keys_ref[tile_at(t, tile), :] = jnp.transpose(value[HD : 2 * HD, :]).astype(bf16)

    move_spans(load, store, sort_ref, tiles, span)
    allowed = block_mask(size)

    def query_block(i, unused):
        here = tile_at(i, size)
        queries = sorted_ref[0:HD, here]

        def part(j, carried, masked):
            accum, running_max, running_sum = carried
            there = tile_at(j, size)
            scores = jnp.dot(keys_ref[there, :], queries, preferred_element_type=f32)
            if masked:
                scores = jnp.where(allowed, scores, masked_score)
            new_max = jnp.maximum(running_max, jnp.max(scores, axis=0, keepdims=True))
            weights = jnp.exp(scores - new_max)
            shrink = jnp.exp(running_max - new_max)
            running_sum = running_sum * shrink + jnp.sum(weights, axis=0, keepdims=True)
            accum = accum * shrink + jnp.dot(
                sorted_ref[2 * HD : 3 * HD, there],
                weights.astype(bf16),
                preferred_element_type=f32,
            )
            return (accum, new_max, running_sum)

        carried = (
            jnp.zeros((HD, size), f32),
            jnp.full((1, size), masked_score, f32),
            jnp.zeros((1, size), f32),
        )
        carried = lax.fori_loop(0, i, functools.partial(part, masked=False), carried)
        accum, running_max, running_sum = part(i, carried, True)
        float_ref[:, here] = accum / running_sum
        log_ref[:, here] = running_max + jnp.log(running_sum)
        return unused

    float_ref[...] = jnp.zeros_like(float_ref)
    log_ref[...] = jnp.zeros_like(log_ref)
    lax.fori_loop(range_ref[0], range_ref[1], query_block, 0)

    def store_back(t, value):
        out_ref[t // per, :, tile_at(t % per, tile)] = value.astype(bf16)

    move_spans(lambda t: float_ref[:, tile_at(t, tile)], store_back, back_ref, tiles, span)


def backward_kernel(
    size,
    span,
    sort_ref,
    back_ref,
    range_ref,
    sorted_ref,
    float_ref,
    log_ref,
    blocks_ref,
    out_ref,
    keys_ref,
    values_ref,
    given_ref,
    delta_ref,
    grads_ref,
):
    count, unused, width = blocks_ref.shape
    tile = 2 * span
    per = width // tile
    tiles = count * per

    def load(t):
        return blocks_ref[t // per, :, tile_at(t % per, tile)]

    def store(t, value):
        here = tile_at(t, tile)
        given_ref[:, here] = value.astype(bf16)
        delta_ref[:, here] = jnp.sum(value * float_ref[:, here], axis=0, keepdims=True)
        keys_ref[here, :] = jnp.transpose(sorted_ref[HD : 2 * HD, here].astype(f32)).astype(bf16)
        values_ref[here, :] = jnp.transpose(sorted_ref[2 * HD :, here].astype(f32)).astype(bf16)

    move_spans(load, store, sort_ref, tiles, span)
    allowed = block_mask(size)
    grads_ref[...] = jnp.zeros_like(grads_ref)

    def key_block(j, unused):
        there = tile_at(j, size)
        keys = keys_ref[there, :]
        values = values_ref[there, :]
        keys_across = sorted_ref[HD : 2 * HD, there]

        def part(i, carried, masked):
            key_acc, value_acc = carried
            here = tile_at(i, size)
            queries = sorted_ref[0:HD, here]
            given = given_ref[:, here]
            scores = jnp.dot(keys, queries, preferred_element_type=f32)
            probs = jnp.exp(scores - log_ref[:, here])
            if masked:
                probs = jnp.where(allowed, probs, 0.0)
            probs_grad = jnp.dot(values, given, preferred_element_type=f32)
            score_low = (probs * (probs_grad - delta_ref[:, here])).astype(bf16)
            value_acc = value_acc + contract(given, probs.astype(bf16), 1, 1)
            key_acc = key_acc + contract(queries, score_low, 1, 1)
            grads_ref[0:HD, here] += jnp.dot(
                keys_across, score_low, preferred_element_type=f32
            ) * (HD**-0.5)
            return (key_acc, value_acc)

        carried = (jnp.zeros((HD, size), f32), jnp.zeros((HD, size), f32))
        first, last = range_ref[0], range_ref[1]
        carried = lax.cond(
            jnp.logical_and(j >= first, j < last),
            lambda c: part(j, c, True),
            lambda c: c,
            carried,
        )
        carried = lax.fori_loop(
            jnp.maximum(j + 1, first), last, functools.partial(part, masked=False), carried
        )
        grads_ref[HD : 2 * HD, there] = carried[0]
        grads_ref[2 * HD :, there] = carried[1]
        return unused

    lax.fori_loop(0, range_ref[1], key_block, 0)

    def store_back(t, value):
        out_ref[t // per, :, tile_at(t % per, tile)] = value.astype(bf16)

    move_spans(lambda t: grads_ref[:, tile_at(t, tile)], store_back, back_ref, tiles, span)


def attend_forward(blocks, sort_order, back_order, query_range, span, size):
    count, unused, width = blocks.shape
    total = count * width
    smem = pl.BlockSpec(memory_space=pltpu.SMEM)
    vmem = pl.BlockSpec(memory_space=pltpu.VMEM)
    return pl.pallas_call(
        functools.partial(forward_kernel, size, span),
        out_shape=(
            jax.ShapeDtypeStruct((count, HD, width), bf16),
            jax.ShapeDtypeStruct((3 * HD, total), bf16),
            jax.ShapeDtypeStruct((HD, total), f32),
            jax.ShapeDtypeStruct((1, total), f32),
        ),
        in_specs=[smem, smem, smem, vmem],
        out_specs=(vmem, vmem, vmem, vmem),
        scratch_shapes=[pltpu.VMEM((total, HD), bf16)],
        compiler_params=pltpu.CompilerParams(vmem_limit_bytes=56 * 1024 * 1024),
        cost_estimate=pl.CostEstimate(
            flops=30 * 10**9, transcendentals=0, bytes_accessed=8 * 10**6
        ),
        name="attend_forward",
    )(sort_order, back_order, query_range, blocks)


def attend_backward(
    ordered, floats, logs, blocks, sort_order, back_order, query_range, span, size
):
    count, unused, width = blocks.shape
    total = count * width
    smem = pl.BlockSpec(memory_space=pltpu.SMEM)
    vmem = pl.BlockSpec(memory_space=pltpu.VMEM)
    return pl.pallas_call(
        functools.partial(backward_kernel, size, span),
        out_shape=jax.ShapeDtypeStruct((count, 3 * HD, width), bf16),
        in_specs=[smem, smem, smem, vmem, vmem, vmem, vmem],
        out_specs=vmem,
        scratch_shapes=[
            pltpu.VMEM((total, HD), bf16),
            pltpu.VMEM((total, HD), bf16),
            pltpu.VMEM((HD, total), bf16),
            pltpu.VMEM((1, total), f32),
            pltpu.VMEM((3 * HD, total), f32),
        ],
        compiler_params=pltpu.CompilerParams(vmem_limit_bytes=56 * 1024 * 1024),
        cost_estimate=pl.CostEstimate(
            flops=36 * 10**9, transcendentals=0, bytes_accessed=8 * 10**6
        ),
        name="attend_backward",
    )(sort_order, back_order, query_range, ordered, floats, logs, blocks)


def norm_parts(vector):
    inverse = lax.rsqrt(jnp.mean(vector * vector, axis=-1, keepdims=True) + epsilon)
    return inverse, vector * inverse


def norm_back(vector, scale_gain, gradient):
    inverse, normed = norm_parts(vector)
    gain_term = jnp.sum(gradient * normed, axis=0)
    scaled = gradient * scale_gain
    return (
        inverse * (scaled - normed * jnp.mean(scaled * normed, axis=-1, keepdims=True)),
        gain_term,
    )


def local(
    inputs,
    span_order,
    attn_gain,
    query_weight,
    key_weight,
    value_weight,
    output_weight,
    ffn_gain,
    gate_weight,
    up_weight,
    down_weight,
    cotangent,
):
    tok_dev, width = inputs.shape
    span = tok_dev // 2
    tokens = KVH * tok_dev
    line = lax.axis_size("line")
    halves = lax.axis_size("xpart")
    shards = lax.axis_size("wshard")
    place = lax.axis_index("line")
    side = lax.axis_index("xpart")
    slab_place = side * shards + lax.axis_index("wshard")
    copies = line // GROUP
    rows = width // shards

    flips = jnp.array(FLIPS, jnp.int32)
    devices = jnp.arange(line, dtype=jnp.int32)[:, None] * KVH + (flips ^ slab_place)[None, :]
    slots = (2 * devices[..., None] + jnp.arange(2, dtype=jnp.int32)).reshape(-1)
    spans = span_order.shape[0]
    numbers = jnp.arange(spans, dtype=jnp.int32)
    back_order = jnp.sum(
        jnp.where(slots[:, None] == numbers[None, :], span_order[None, :], 0), axis=1
    )
    sort_order = jnp.sum(
        jnp.where(back_order[None, :] == numbers[:, None], numbers[None, :], 0), axis=1
    )
    total = line * tokens
    size = min(512, total // copies)
    blocks_each = total // size // copies
    first_block = (place // GROUP) * blocks_each
    query_range = jnp.stack([first_block, first_block + blocks_each]).astype(jnp.int32)
    slab_spans = lax.dynamic_slice_in_dim(back_order, place * 2 * KVH, 2 * KVH, 0)
    positions = (slab_spans[:, None] * span + jnp.arange(span, dtype=jnp.int32)).reshape(-1)
    cosine, sine = rotary_tables(positions, HD)

    def own_columns(weight):
        units = weight.shape[1] // KVH
        if units % 128 == 0 or halves == 1:
            cuts = [
                lax.dynamic_slice_in_dim(weight, (w * halves + side) * units, units, 1)
                for w in range(shards)
            ]
        else:
            cuts = [
                jnp.where(
                    side == 0,
                    weight[:, 2 * w * units : (2 * w + 1) * units],
                    weight[:, (2 * w + 1) * units : (2 * w + 2) * units],
                )
                for w in range(shards)
            ]
        return jnp.stack(cuts)

    def gather_rows(columns):
        return lax.all_to_all(columns, "wshard", 0, 0, tiled=True).reshape(width, -1)

    gains = jnp.broadcast_to(jnp.stack([attn_gain, ffn_gain])[None], (shards, 2, rows))
    gains = lax.all_to_all(gains, "wshard", 0, 0, tiled=True).astype(f32)
    gain_one = gains[:, 0].reshape(width)
    gain_two = gains[:, 1].reshape(width)
    attn_weight = gather_rows(
        jnp.concatenate(
            [own_columns(query_weight), own_columns(key_weight), own_columns(value_weight)], axis=-1
        )
    )
    heads = query_weight.shape[1] // KVH
    slab_inputs = slab_gather(inputs)
    normed_one = (norm_parts(slab_inputs.astype(f32))[1] * gain_one).astype(bf16)
    slab_cotangent = slab_gather(cotangent)

    projected = contract(attn_weight, normed_one, 0, 1)
    queries = rotate(projected[:heads].reshape(GROUP, HD, tokens), cosine, sine).astype(bf16)
    queries = queries * jnp.asarray(HD**-0.5, bf16)
    keys = rotate(projected[heads : heads + HD], cosine, sine).astype(bf16)
    values = projected[heads + HD :].astype(bf16)
    blocks = jnp.concatenate(
        [queries, jnp.broadcast_to(jnp.concatenate([keys, values]), (GROUP, 2 * HD, tokens))],
        axis=1,
    )
    blocks = lax.all_to_all(jnp.tile(blocks, (copies, 1, 1)), "line", 0, 0, tiled=True)
    attended, ordered, floats, logs = attend_forward(
        blocks, sort_order, back_order, query_range, span, size
    )

    def from_heads(blocks):
        got = lax.all_to_all(blocks, "line", 0, 0, tiled=True)
        return got.reshape((copies, GROUP) + got.shape[1:])

    def add_copies(got):
        return got[0] if copies == 1 else jnp.sum(got.astype(f32), axis=0).astype(bf16)

    attended = add_copies(from_heads(attended)).reshape(heads, tokens)
    own_output = lax.dynamic_slice_in_dim(output_weight, side * heads, heads, 0)
    residual = inputs.astype(f32) + slab_reduce(contract(attended, own_output, 0, 0))

    gate_full = gather_rows(own_columns(gate_weight))
    up_full = gather_rows(own_columns(up_weight))
    units = gate_full.shape[1]
    own_down = lax.dynamic_slice_in_dim(down_weight, side * units, units, 0)
    normed_two = slab_gather((norm_parts(residual)[1] * gain_two).astype(bf16))
    gate_pre = contract(normed_two, gate_full, 1, 0)
    up_pre = contract(normed_two, up_full, 1, 0)
    sigmoid_gate = jax.nn.sigmoid(gate_pre)
    hidden = (gate_pre * sigmoid_gate * up_pre).astype(bf16)
    hidden_grad = contract(slab_cotangent, own_down, 1, 1)
    gate_low = (
        hidden_grad * up_pre * sigmoid_gate * (1.0 + gate_pre * (1.0 - sigmoid_gate))
    ).astype(bf16)
    up_low = (hidden_grad * gate_pre * sigmoid_gate).astype(bf16)
    normed_two_grad = slab_reduce(
        contract(gate_low, gate_full, 1, 1) + contract(up_low, up_full, 1, 1)
    )
    down_share = line_reduce(line_parts(contract(hidden, slab_cotangent, 0, 0)))
    gate_share = line_reduce(
        line_parts(contract(normed_two, gate_low, 0, 0).reshape(shards, rows, units))
    )
    up_share = line_reduce(
        line_parts(contract(normed_two, up_low, 0, 0).reshape(shards, rows, units))
    )
    residual_part, ffn_gain_term = norm_back(residual, gain_two, normed_two_grad)
    residual_grad = cotangent.astype(f32) + residual_part
    branch_low = slab_gather(residual_grad.astype(bf16))

    attended_grad = contract(own_output, branch_low, 1, 1).astype(bf16)
    given = jnp.tile(attended_grad.reshape(GROUP, HD, tokens), (copies, 1, 1))
    given = lax.all_to_all(given, "line", 0, 0, tiled=True)
    raw = attend_backward(
        ordered, floats, logs, given, sort_order, back_order, query_range, span, size
    )
    raw = from_heads(raw)
    query_low = rotate(add_copies(raw[:, :, :HD]).astype(f32), cosine, -sine).astype(bf16)
    pair_raw = jnp.sum(raw[:, :, HD:].astype(f32), axis=(0, 1))
    key_low = rotate(pair_raw[:HD], cosine, -sine).astype(bf16)
    value_low = pair_raw[HD:].astype(bf16)
    low = jnp.concatenate([query_low.reshape(heads, tokens), key_low, value_low], axis=0)
    normed_one_grad = slab_reduce(contract(low, attn_weight, 0, 1))
    input_part, attn_gain_term = norm_back(inputs.astype(f32), gain_one, normed_one_grad)
    input_grad = residual_grad + input_part

    output_share = line_reduce(line_parts(contract(attended, branch_low, 1, 0)))
    attn_share = line_reduce(
        line_parts(contract(normed_one, low, 0, 1).reshape(shards, rows, heads + 2 * HD))
    )

    outputs = (residual + slab_reduce(contract(hidden, own_down, 1, 0))).astype(bf16)

    down_grad = spread_rows(down_share)
    (gate_grad,) = spread_columns(gate_share, [(place_columns, whole_block)])
    (up_grad,) = spread_columns(up_share, [(place_columns, whole_block)])
    output_grad = spread_rows(output_share)
    query_grad, key_grad, value_grad = spread_columns(
        attn_share,
        [
            (place_columns, lambda block: block[..., :heads]),
            (place_narrow, lambda block: block[..., heads : heads + HD]),
            (place_narrow, lambda block: block[..., heads + HD :]),
        ],
    )
    gain_terms = lax.psum(jnp.stack([attn_gain_term, ffn_gain_term]), ("line",) + SLAB)
    gain_terms = lax.dynamic_slice_in_dim(
        gain_terms, lax.axis_index("wshard") * rows, rows, 1
    )
    return (
        outputs,
        input_grad,
        gain_terms[0],
        query_grad,
        key_grad,
        value_grad,
        output_grad,
        gain_terms[1],
        gate_grad,
        up_grad,
        down_grad,
    )


def solution(mesh):
    shards = mesh.shape["wshard"]
    halves = KVH // shards
    fine = Mesh(
        mesh.devices.reshape(mesh.shape["ctx"] // halves, halves, shards),
        ("line", "xpart", "wshard"),
    )
    every = ("line", "xpart", "wshard")
    in_specs = (
        P(every, None),
        P(),
        P("wshard"),
        P("wshard", None),
        P("wshard", None),
        P("wshard", None),
        P("wshard", None),
        P("wshard"),
        P("wshard", None),
        P("wshard", None),
        P("wshard", None),
        P(every, None),
    )
    out_specs = (
        P(every, None),
        P(every, None),
        P("wshard"),
        P("wshard", None),
        P("wshard", None),
        P("wshard", None),
        P("wshard", None),
        P("wshard"),
        P("wshard", None),
        P("wshard", None),
        P("wshard", None),
    )
    return jax.shard_map(local, mesh=fine, in_specs=in_specs, out_specs=out_specs, check_vma=False)
```

```python
import functools

import jax
import jax.numpy as jnp
from jax import lax
from jax.experimental import pallas as pl
from jax.experimental.pallas import tpu as pltpu
from jax.sharding import Mesh
from jax.sharding import PartitionSpec as P

H = 32
KVH = 8
HD = 64
GROUP = H // KVH

epsilon = 1e-05
rope_base = 500000.0
masked_score = -1e30
f32 = jnp.float32
bf16 = jnp.bfloat16


def rotary_tables(positions, width):
    half_width = width // 2
    frequency = jnp.power(rope_base, -jnp.arange(half_width, dtype=f32) * 2.0 / width)
    angles = frequency[:, None] * positions.astype(f32)[None, :]
    return (jnp.cos(angles), jnp.sin(angles))


def rotate(vector, cosine, sine):
    half_width = vector.shape[-2] // 2
    first = vector[..., :half_width, :]
    second = vector[..., half_width:, :]
    return jnp.concatenate(
        [first * cosine - second * sine, second * cosine + first * sine], axis=-2
    )


def contract(left, right, left_dim, right_dim):
    return lax.dot_general(
        left, right, (((left_dim,), (right_dim,)), ((), ())), preferred_element_type=f32
    )


SLAB = ("xpart", "wshard")


def swap(value, flip):
    return lax.ppermute(value, SLAB, [(i, i ^ flip) for i in range(KVH)])


FLIPS = (0, 2, 4, 6, 1, 3, 5, 7)


def slab_gather(block):
    rows = block.shape[0]
    half = rows // 2
    total = jnp.zeros((KVH * rows,) + block.shape[1:], block.dtype)

    def put(total, pieces):
        for index, piece in pieces:
            total = lax.dynamic_update_slice(total, piece, (index * half,) + (0,) * (block.ndim - 1))
        return total

    total = put(total, [(0, block)])
    row, column, other = yield [swap(block, 2), swap(block, 4), swap(block, 1)]
    total = put(total, [(2, row), (4, column), (8, other)])
    far_low, far_high, other_row, other_column = yield [
        swap(row[:half], 4),
        swap(column[half:], 2),
        swap(row, 1),
        swap(column, 1),
    ]
    total = put(total, [(6, far_low), (7, far_high), (10, other_row), (12, other_column)])
    far_low, far_high, total = yield [swap(far_low, 1), swap(far_high, 1), total]
    return put(total, [(14, far_low), (15, far_high)])


def slab_reduce(partial):
    rows = partial.shape[0] // KVH
    half = partial.shape[1] // 2
    partial = partial.reshape(KVH, rows, 2 * half)
    (got,) = yield [swap(partial[4:].astype(bf16), 1)]
    own = partial[:4] + got.astype(f32)
    left, right = own[..., :half], own[..., half:]
    left_got, right_got = yield [
        swap(left[2:].astype(bf16), 4),
        swap(right[1::2].astype(bf16), 2),
    ]
    left = left[:2] + left_got.astype(f32)
    right = right[0::2] + right_got.astype(f32)
    left_got, right_got = yield [
        swap(left[1].astype(bf16), 2),
        swap(right[1].astype(bf16), 4),
    ]
    return jnp.concatenate(
        [left[0] + left_got.astype(f32), right[0] + right_got.astype(f32)], axis=1
    )


def alone(task):
    try:
        transfers = next(task)
        while True:
            transfers = task.send(transfers)
    except StopIteration as stop:
        return stop.value


def after(value, *others):
    return lax.optimization_barrier((value,) + others)[0]


def run_tasks(tasks, box):
    running, stage, last = {}, 0, ()
    tasks = list(tasks)
    while tasks or running:
        for entry in list(tasks):
            name, ready, make, *turn = entry
            if ready(stage, box) and turn in ([], [stage % 2]):
                tasks.remove(entry)
                running[name] = (make(last), None, turn)
        moving = {}
        for name, (task, got, turn) in list(running.items()):
            if turn in ([], [stage % 2]):
                try:
                    moving[name] = task.send(got)
                except StopIteration as stop:
                    del running[name]
                    box[name] = stop.value
        held = lax.optimization_barrier(tuple(v for values in moving.values() for v in values))
        last = held[:1] or last
        box["now"] = last
        done = 0
        for name, values in moving.items():
            task, unused, turn = running[name]
            running[name] = (task, held[done : done + len(values)], turn)
            done += len(values)
        stage += 1


def stream(chunks, placed):
    count, halves = lax.axis_size("line"), lax.axis_size("xpart")
    place, side = lax.axis_index("line"), lax.axis_index("xpart")
    sides = [lax.rem(side + halves - turn, halves) for turn in range(halves)]
    outer = jnp.logical_or(place == 0, place == count - 1)
    inward, outward, across = [(0, 1), (3, 2)], [(1, 0), (2, 3)], [(1, 2), (2, 1)]
    last = len(chunks)
    parts, sums, totals, owns = {}, {}, {}, {}
    for stage in range(last + 3):
        moves = {}
        going, coming = stage, stage - 2
        if going < last:
            parts[going] = chunks[going][0]()
        if count != 4:
            if going < last:
                moves["all"] = lax.psum(parts.pop(going), "line")
        else:
            if going < last and coming in totals and parts[going].shape == totals[coming].shape:
                both = jnp.where(outer, parts[going], totals[coming])
                moves["in"] = moves["out"] = lax.ppermute(both, "line", inward + outward)
            else:
                if going < last:
                    moves["in"] = lax.ppermute(parts[going], "line", inward)
                if coming in totals:
                    moves["out"] = lax.ppermute(totals[coming], "line", outward)
            if stage - 1 in sums:
                moves["across"] = lax.ppermute(sums[stage - 1], "line", across)
        if stage - 3 in owns:
            for turn in range(1, halves):
                moves[turn] = lax.ppermute(
                    owns[stage - 3], "xpart", [(i, (i + turn) % halves) for i in range(halves)]
                )
        values = []
        for value in moves.values():
            if all(value is not other for other in values):
                values.append(value)
        got = yield values
        new = {id(value): new_value for value, new_value in zip(values, got)}
        moves = {key: new[id(value)] for key, value in moves.items()}
        if "all" in moves:
            totals[going] = moves["all"]
        if "across" in moves:
            kept = sums.pop(stage - 1)
            totals[stage - 1] = (kept.astype(f32) + moves["across"].astype(f32)).astype(bf16)
        if "in" in moves:
            part = parts.pop(going)
            sums[going] = (part.astype(f32) + moves["in"].astype(f32)).astype(bf16)
        if "out" in moves:
            owns[coming] = jnp.where(outer, moves["out"], totals.pop(coming))
        elif coming in totals:
            owns[coming] = totals.pop(coming)
        if stage - 3 in owns:
            pieces = [owns.pop(stage - 3)] + [moves[turn] for turn in range(1, halves)]
            chunks[stage - 3][1](placed, pieces, sides)
    return None


def place_kernel(spots_ref, *refs):
    out_ref = refs[-1]
    halves = spots_ref.shape[0] - 1
    columns = refs[0].shape[-1]
    for turn in range(halves):
        for spot in range(halves):

            @pl.when(spots_ref[1 + turn] == spot)
            def put(turn=turn, spot=spot):
                out_ref[:, spot * columns : (spot + 1) * columns] = refs[turn][0].astype(f32)


def place_columns(total, pieces, spot, sides, count):
    shards, rows, columns = pieces[0].shape
    halves = len(pieces)
    operands = [jnp.stack([spot] + sides).astype(jnp.int32)] + list(pieces)
    specs = [pl.BlockSpec((1, rows, columns), lambda w, spots: (w, 0, 0))] * halves
    aliases = {}
    if total is not None:
        aliases = {len(operands): 0}
        operands.append(total)
        specs.append(pl.BlockSpec(memory_space=pl.ANY))
    return pl.pallas_call(
        place_kernel,
        grid_spec=pltpu.PrefetchScalarGridSpec(
            num_scalar_prefetch=1,
            grid=(shards,),
            in_specs=specs,
            out_specs=pl.BlockSpec((rows, halves * columns), lambda w, spots: (spots[0], w)),
        ),
        out_shape=jax.ShapeDtypeStruct((count * rows, shards * halves * columns), f32),
        input_output_aliases=aliases,
        compiler_params=pltpu.CompilerParams(vmem_limit_bytes=32 * 1024 * 1024),
        cost_estimate=pl.CostEstimate(
            flops=0, transcendentals=0, bytes_accessed=6 * halves * shards * rows * columns
        ),
        name="place_columns",
    )(*operands)


def blocks_kernel(sides_ref, *refs):
    out_ref = refs[-1]
    for turn in range(sides_ref.shape[0]):

        @pl.when(pl.program_id(0) == turn)
        def put(turn=turn):
            out_ref[...] = refs[turn][...].astype(f32)


def place_blocks(total, pieces, sides, shape, block, spot):
    halves = len(pieces)
    steps = pieces[0].shape[0] // block[0]

    def source(turn):
        def index(t, i, sides_ref):
            return (jnp.where(t == turn, i, jnp.where(t < turn, 0, steps - 1)), 0)

        return pl.BlockSpec(block, index)

    operands = [jnp.stack(sides).astype(jnp.int32)] + list(pieces)
    specs = [source(turn) for turn in range(halves)]
    aliases = {}
    if total is not None:
        aliases = {len(operands): 0}
        operands.append(total)
        specs.append(pl.BlockSpec(memory_space=pl.ANY))
    return pl.pallas_call(
        blocks_kernel,
        grid_spec=pltpu.PrefetchScalarGridSpec(
            num_scalar_prefetch=1,
            grid=(halves, steps),
            in_specs=specs,
            out_specs=pl.BlockSpec(block, lambda t, i, sides_ref: spot(sides_ref[t], i)),
        ),
        out_shape=jax.ShapeDtypeStruct(shape, f32),
        input_output_aliases=aliases,
        compiler_params=pltpu.CompilerParams(vmem_limit_bytes=32 * 1024 * 1024),
        cost_estimate=pl.CostEstimate(
            flops=0, transcendentals=0, bytes_accessed=6 * halves * pieces[0].size
        ),
        name="place_blocks",
    )(*operands)


def place_narrow(total, pieces, spot, sides, count):
    shards, rows, columns = pieces[0].shape
    halves = len(pieces)
    ordered = [pieces[0]]
    if halves == 2:
        ordered = [jnp.where(sides[0] == t, pieces[0], pieces[1]) for t in range(2)]
    block = jnp.concatenate(
        [ordered[t][w] for w in range(shards) for t in range(halves)], axis=1
    ).astype(f32)
    if total is None:
        total = jnp.zeros((count * rows, block.shape[1]), f32)
    return lax.dynamic_update_slice(total, block, (spot * rows, 0))


def sum_everywhere(vector):
    for flip in (1, 2, 4):
        (got,) = yield [swap(vector, flip)]
        vector = vector + got
    count = lax.axis_size("line")
    flip = 1
    while flip < count:
        (got,) = yield [lax.ppermute(vector, "line", [(i, i ^ flip) for i in range(count)])]
        vector = vector + got
        flip *= 2
    return vector


def move_spans(load, store, order_ref, tiles, span):
    lane = lax.broadcasted_iota(jnp.int32, (1, 2 * span), 1)

    def step(t, unused):
        first, second = order_ref[2 * t], order_ref[2 * t + 1]
        left = load(first // 2).astype(f32)
        right = load(second // 2).astype(f32)
        left = jnp.where(first % 2 == 1, pltpu.roll(left, span, 1), left)
        right = jnp.where(second % 2 == 0, pltpu.roll(right, span, 1), right)
        store(t, jnp.where(lane < span, left, right))
        return unused

    lax.fori_loop(0, tiles, step, 0)


def tile_at(index, tile):
    return pl.ds(pl.multiple_of(index * tile, tile), tile)


def block_mask(size):
    return lax.broadcasted_iota(jnp.int32, (size, size), 0) <= lax.broadcasted_iota(
        jnp.int32, (size, size), 1
    )


def forward_kernel(
    size, span, sort_ref, back_ref, range_ref, blocks_ref, out_ref, sorted_ref, float_ref, log_ref, keys_ref
):
    count, unused, width = blocks_ref.shape
    tile = 2 * span
    per = width // tile
    tiles = count * per

    def load(t):
        return blocks_ref[t // per, :, tile_at(t % per, tile)]

    def store(t, value):
        sorted_ref[:, tile_at(t, tile)] = value.astype(bf16)
        keys_ref[tile_at(t, tile), :] = jnp.transpose(value[HD : 2 * HD, :]).astype(bf16)

    move_spans(load, store, sort_ref, tiles, span)
    allowed = block_mask(size)

    def query_block(i, unused):
        here = tile_at(i, size)
        queries = sorted_ref[0:HD, here]

        def part(j, carried, masked):
            accum, running_max, running_sum = carried
            there = tile_at(j, size)
            scores = jnp.dot(keys_ref[there, :], queries, preferred_element_type=f32)
            if masked:
                scores = jnp.where(allowed, scores, masked_score)
            new_max = jnp.maximum(running_max, jnp.max(scores, axis=0, keepdims=True))
            weights = jnp.exp(scores - new_max)
            shrink = jnp.exp(running_max - new_max)
            running_sum = running_sum * shrink + jnp.sum(weights, axis=0, keepdims=True)
            accum = accum * shrink + jnp.dot(
                sorted_ref[2 * HD : 3 * HD, there],
                weights.astype(bf16),
                preferred_element_type=f32,
            )
            return (accum, new_max, running_sum)

        carried = (
            jnp.zeros((HD, size), f32),
            jnp.full((1, size), masked_score, f32),
            jnp.zeros((1, size), f32),
        )
        carried = lax.fori_loop(0, i, functools.partial(part, masked=False), carried)
        accum, running_max, running_sum = part(i, carried, True)
        float_ref[:, here] = accum / running_sum
        log_ref[:, here] = running_max + jnp.log(running_sum)
        return unused

    float_ref[...] = jnp.zeros_like(float_ref)
    log_ref[...] = jnp.zeros_like(log_ref)
    lax.fori_loop(range_ref[0], range_ref[1], query_block, 0)

    def store_back(t, value):
        out_ref[t // per, :, tile_at(t % per, tile)] = value.astype(bf16)

    move_spans(lambda t: float_ref[:, tile_at(t, tile)], store_back, back_ref, tiles, span)


def backward_kernel(
    size,
    span,
    sort_ref,
    back_ref,
    range_ref,
    sorted_ref,
    float_ref,
    log_ref,
    blocks_ref,
    out_ref,
    keys_ref,
    values_ref,
    given_ref,
    delta_ref,
    grads_ref,
):
    count, unused, width = blocks_ref.shape
    tile = 2 * span
    per = width // tile
    tiles = count * per

    def load(t):
        return blocks_ref[t // per, :, tile_at(t % per, tile)]

    def store(t, value):
        here = tile_at(t, tile)
        given_ref[:, here] = value.astype(bf16)
        delta_ref[:, here] = jnp.sum(value * float_ref[:, here], axis=0, keepdims=True)
        keys_ref[here, :] = jnp.transpose(sorted_ref[HD : 2 * HD, here].astype(f32)).astype(bf16)
        values_ref[here, :] = jnp.transpose(sorted_ref[2 * HD :, here].astype(f32)).astype(bf16)

    move_spans(load, store, sort_ref, tiles, span)
    allowed = block_mask(size)
    grads_ref[...] = jnp.zeros_like(grads_ref)

    def key_block(j, unused):
        there = tile_at(j, size)
        keys = keys_ref[there, :]
        values = values_ref[there, :]
        keys_across = sorted_ref[HD : 2 * HD, there]

        def part(i, carried, masked):
            key_acc, value_acc = carried
            here = tile_at(i, size)
            queries = sorted_ref[0:HD, here]
            given = given_ref[:, here]
            scores = jnp.dot(keys, queries, preferred_element_type=f32)
            probs = jnp.exp(scores - log_ref[:, here])
            if masked:
                probs = jnp.where(allowed, probs, 0.0)
            probs_grad = jnp.dot(values, given, preferred_element_type=f32)
            score_low = (probs * (probs_grad - delta_ref[:, here])).astype(bf16)
            value_acc = value_acc + contract(given, probs.astype(bf16), 1, 1)
            key_acc = key_acc + contract(queries, score_low, 1, 1)
            grads_ref[0:HD, here] += jnp.dot(
                keys_across, score_low, preferred_element_type=f32
            ) * (HD**-0.5)
            return (key_acc, value_acc)

        carried = (jnp.zeros((HD, size), f32), jnp.zeros((HD, size), f32))
        first, last = range_ref[0], range_ref[1]
        carried = lax.cond(
            jnp.logical_and(j >= first, j < last),
            lambda c: part(j, c, True),
            lambda c: c,
            carried,
        )
        carried = lax.fori_loop(
            jnp.maximum(j + 1, first), last, functools.partial(part, masked=False), carried
        )
        grads_ref[HD : 2 * HD, there] = carried[0]
        grads_ref[2 * HD :, there] = carried[1]
        return unused

    lax.fori_loop(0, range_ref[1], key_block, 0)

    def store_back(t, value):
        out_ref[t // per, :, tile_at(t % per, tile)] = value.astype(bf16)

    move_spans(lambda t: grads_ref[:, tile_at(t, tile)], store_back, back_ref, tiles, span)


def attend_forward(blocks, sort_order, back_order, query_range, span, size):
    count, unused, width = blocks.shape
    total = count * width
    smem = pl.BlockSpec(memory_space=pltpu.SMEM)
    vmem = pl.BlockSpec(memory_space=pltpu.VMEM)
    return pl.pallas_call(
        functools.partial(forward_kernel, size, span),
        out_shape=(
            jax.ShapeDtypeStruct((count, HD, width), bf16),
            jax.ShapeDtypeStruct((3 * HD, total), bf16),
            jax.ShapeDtypeStruct((HD, total), f32),
            jax.ShapeDtypeStruct((1, total), f32),
        ),
        in_specs=[smem, smem, smem, vmem],
        out_specs=(vmem, vmem, vmem, vmem),
        scratch_shapes=[pltpu.VMEM((total, HD), bf16)],
        compiler_params=pltpu.CompilerParams(vmem_limit_bytes=56 * 1024 * 1024),
        cost_estimate=pl.CostEstimate(
            flops=30 * 10**9, transcendentals=0, bytes_accessed=8 * 10**6
        ),
        name="attend_forward",
    )(sort_order, back_order, query_range, blocks)


def attend_backward(
    ordered, floats, logs, blocks, sort_order, back_order, query_range, span, size
):
    count, unused, width = blocks.shape
    total = count * width
    smem = pl.BlockSpec(memory_space=pltpu.SMEM)
    vmem = pl.BlockSpec(memory_space=pltpu.VMEM)
    return pl.pallas_call(
        functools.partial(backward_kernel, size, span),
        out_shape=jax.ShapeDtypeStruct((count, 3 * HD, width), bf16),
        in_specs=[smem, smem, smem, vmem, vmem, vmem, vmem],
        out_specs=vmem,
        scratch_shapes=[
            pltpu.VMEM((total, HD), bf16),
            pltpu.VMEM((total, HD), bf16),
            pltpu.VMEM((HD, total), bf16),
            pltpu.VMEM((1, total), f32),
            pltpu.VMEM((3 * HD, total), f32),
        ],
        compiler_params=pltpu.CompilerParams(vmem_limit_bytes=56 * 1024 * 1024),
        cost_estimate=pl.CostEstimate(
            flops=36 * 10**9, transcendentals=0, bytes_accessed=8 * 10**6
        ),
        name="attend_backward",
    )(sort_order, back_order, query_range, ordered, floats, logs, blocks)


def norm_parts(vector):
    inverse = lax.rsqrt(jnp.mean(vector * vector, axis=-1, keepdims=True) + epsilon)
    return inverse, vector * inverse


def norm_back(vector, scale_gain, gradient):
    inverse, normed = norm_parts(vector)
    gain_term = jnp.sum(gradient * normed, axis=0)
    scaled = gradient * scale_gain
    return (
        inverse * (scaled - normed * jnp.mean(scaled * normed, axis=-1, keepdims=True)),
        gain_term,
    )


def local(
    inputs,
    span_order,
    attn_gain,
    query_weight,
    key_weight,
    value_weight,
    output_weight,
    ffn_gain,
    gate_weight,
    up_weight,
    down_weight,
    cotangent,
):
    tok_dev, width = inputs.shape
    span = tok_dev // 2
    tokens = KVH * tok_dev
    line = lax.axis_size("line")
    halves = lax.axis_size("xpart")
    shards = lax.axis_size("wshard")
    place = lax.axis_index("line")
    side = lax.axis_index("xpart")
    slab_place = side * shards + lax.axis_index("wshard")
    copies = line // GROUP
    rows = width // shards

    flips = jnp.array(FLIPS, jnp.int32)
    devices = jnp.arange(line, dtype=jnp.int32)[:, None] * KVH + (flips ^ slab_place)[None, :]
    slots = (2 * devices[..., None] + jnp.arange(2, dtype=jnp.int32)).reshape(-1)
    spans = span_order.shape[0]
    numbers = jnp.arange(spans, dtype=jnp.int32)
    back_order = jnp.sum(
        jnp.where(slots[:, None] == numbers[None, :], span_order[None, :], 0), axis=1
    )
    sort_order = jnp.sum(
        jnp.where(back_order[None, :] == numbers[:, None], numbers[None, :], 0), axis=1
    )
    total = line * tokens
    size = min(512, total // copies)
    blocks_each = total // size // copies
    first_block = (place // GROUP) * blocks_each
    query_range = jnp.stack([first_block, first_block + blocks_each]).astype(jnp.int32)
    slab_spans = lax.dynamic_slice_in_dim(back_order, place * 2 * KVH, 2 * KVH, 0)
    positions = (slab_spans[:, None] * span + jnp.arange(span, dtype=jnp.int32)).reshape(-1)
    cosine, sine = rotary_tables(positions, HD)

    shard = lax.axis_index("wshard")

    def pass_on(block, flip):
        return lax.ppermute(block, "wshard", [(i, i ^ flip) for i in range(shards)])

    def in_order(blocks):
        first = blocks[0]
        total = jnp.zeros((shards,) + first.shape, first.dtype)
        for flip, block in enumerate(blocks):
            total = lax.dynamic_update_slice(
                total, block[None], (shard ^ flip,) + (0,) * first.ndim
            )
        return total

    def side_columns(weight, flip):
        units = weight.shape[1] // KVH
        if units % 128 == 0 or halves == 1:
            start = ((shard ^ flip) * halves + side) * units
            return lax.dynamic_slice_in_dim(weight, start, units, 1)
        pair = lax.dynamic_slice_in_dim(weight, (shard ^ flip) * halves * units, halves * units, 1)
        return jnp.where(side == 0, pair[:, :units], pair[:, units:])

    heads = query_weight.shape[1] // KVH
    units = gate_weight.shape[1] // KVH

    def side_block(weights, flip):
        return jnp.concatenate([side_columns(weight, flip) for weight in weights], axis=1)

    box = {}

    def exchange(weights, flips):
        weights = after(weights, *box["now"])
        return [pass_on(side_block(weights, flip), flip) for flip in flips]

    near, middle, far = (1,), range(2, shards // 2 + 1), range(shards // 2 + 1, shards)
    near, middle, far = (
        [flip for flip in flips if flip < shards] for flips in (near, middle, far)
    )

    projections = (query_weight, key_weight, value_weight)
    ffn_weights = (gate_weight, up_weight)

    def weights_task():
        blocks = [side_block(projections, 0)]
        blocks += yield [pass_on(side_block(projections, flip), flip) for flip in near]
        gains = jnp.stack([attn_gain, ffn_gain])
        gains = after(gains, *box["now"])
        got = yield exchange(projections, middle) + [
            pass_on(gains, flip) for flip in range(1, shards)
        ]
        blocks += got[: len(middle)]
        gains = in_order([gains] + list(got[len(middle) :])).astype(f32)
        blocks += yield exchange(projections, far)
        attn_weight = in_order(blocks).reshape(width, -1)
        return (gains[:, 0].reshape(width), gains[:, 1].reshape(width), attn_weight)

    run_tasks(
        [
            ("inputs", lambda t, b: True, lambda last: slab_gather(inputs)),
            ("weights", lambda t, b: True, lambda last: weights_task()),
        ],
        box,
    )
    gain_one, gain_two, attn_weight = box["weights"]
    normed_one = (norm_parts(box["inputs"].astype(f32))[1] * gain_one).astype(bf16)

    own_down = lax.dynamic_slice_in_dim(down_weight, side * units, units, 0)

    projected = contract(attn_weight, normed_one, 0, 1)
    queries = rotate(projected[:heads].reshape(GROUP, HD, tokens), cosine, sine).astype(bf16)
    queries = queries * jnp.asarray(HD**-0.5, bf16)
    keys = rotate(projected[heads : heads + HD], cosine, sine).astype(bf16)
    values = projected[heads + HD :].astype(bf16)
    blocks = jnp.concatenate(
        [queries, jnp.broadcast_to(jnp.concatenate([keys, values]), (GROUP, 2 * HD, tokens))],
        axis=1,
    )
    blocks = lax.all_to_all(jnp.tile(blocks, (copies, 1, 1)), "line", 0, 0, tiled=True)
    def ffn_pass(flips, parts, *now):
        weights = after([ffn_weights[part] for part in parts], *now)
        return [
            (flip, part, pass_on(side_columns(weight, flip), flip))
            for part, weight in zip(parts, weights)
            for flip in flips
        ]

    def held(moves, *others):
        values = lax.optimization_barrier(tuple(value for f, p, value in moves) + others)
        return [(f, p, v) for (f, p, unused), v in zip(moves, values)], values[len(moves) :]

    ffn_moves, (blocks,) = held(ffn_pass(near + middle, (0, 1), normed_one), blocks)
    late_moves = ffn_pass(far, (0,), ffn_moves[-1][2])
    attended, ordered, floats, logs = attend_forward(
        blocks, sort_order, back_order, query_range, span, size
    )

    def from_heads(blocks):
        got = lax.all_to_all(blocks, "line", 0, 0, tiled=True)
        return got.reshape((copies, GROUP) + got.shape[1:])

    def add_copies(got):
        return got[0] if copies == 1 else jnp.sum(got.astype(f32), axis=0).astype(bf16)

    own_output = lax.dynamic_slice_in_dim(output_weight, side * heads, heads, 0)
    late_moves, (attended,) = held(late_moves, attended)
    last_moves = ffn_pass(far, (1,), attended)
    late_moves, last_moves = late_moves + last_moves, len(late_moves)

    def attended_task():
        (blocks, *moves) = yield [from_heads(attended)] + [
            v for f, p, v in late_moves[last_moves:]
        ]
        box["late_moves"] = late_moves[:last_moves] + [
            (f, p, v) for (f, p, unused), v in zip(late_moves[last_moves:], moves)
        ]
        heads_out = add_copies(blocks).reshape(heads, tokens)
        added = yield from slab_reduce(contract(heads_out, own_output, 0, 0))
        return (heads_out, inputs.astype(f32) + added)

    run_tasks(
        [
            ("attended", lambda t, b: True, lambda last: attended_task()),
            (
                "cotangent",
                lambda t, b: t >= 1,
                lambda last: slab_gather(after(cotangent, *last)),
            ),
        ],
        box,
    )
    attended, residual = box["attended"]
    slab_cotangent = box["cotangent"]

    ffn_full = jnp.zeros((shards, rows, 2 * units), bf16)
    moves = [(0, part, side_columns(ffn_weights[part], 0)) for part in range(2)]
    for flip, part, block in moves + ffn_moves + box["late_moves"]:
        ffn_full = lax.dynamic_update_slice(
            ffn_full, block[None], (shard ^ flip, 0, part * units)
        )
    ffn_full = ffn_full.reshape(width, 2 * units)

    normed_two = alone(
        slab_gather((norm_parts(residual)[1] * gain_two).astype(bf16))
    )
    hidden_grad = contract(slab_cotangent, own_down, 1, 1)
    normed_two, hidden_grad = lax.optimization_barrier((normed_two, hidden_grad))
    ffn_pre = contract(normed_two, ffn_full, 1, 0)
    gate_pre, up_pre = ffn_pre[:, :units], ffn_pre[:, units:]
    sigmoid_gate = jax.nn.sigmoid(gate_pre)
    hidden = (gate_pre * sigmoid_gate * up_pre).astype(bf16)
    down_parts = contract(hidden, slab_cotangent, 0, 0).astype(bf16)
    gate_low = (
        hidden_grad * up_pre * sigmoid_gate * (1.0 + gate_pre * (1.0 - sigmoid_gate))
    ).astype(bf16)
    up_low = (hidden_grad * gate_pre * sigmoid_gate).astype(bf16)

    def to_shards(partial):
        return lax.all_to_all(partial, "wshard", 0, 0, tiled=True)

    gate_partial = contract(normed_two, gate_low, 0, 0).astype(bf16).reshape(shards, rows, units)

    def attention_back(last):
        ffn_low = after(jnp.concatenate([gate_low, up_low], axis=1), gate_partial)
        normed_two_grad = yield from slab_reduce(contract(ffn_low, ffn_full, 1, 1))
        residual_part, box["ffn_gain"] = norm_back(residual, gain_two, normed_two_grad)
        residual_grad = cotangent.astype(f32) + residual_part
        branch_low = yield from slab_gather(residual_grad.astype(bf16))
        attended_grad = contract(own_output, branch_low, 1, 1).astype(bf16)
        given = jnp.tile(attended_grad.reshape(GROUP, HD, tokens), (copies, 1, 1))
        (given,) = yield [lax.all_to_all(given, "line", 0, 0, tiled=True)]
        box["output_parts"] = contract(attended, branch_low, 1, 0).astype(bf16)
        raw = attend_backward(
            ordered, floats, logs, given, sort_order, back_order, query_range, span, size
        )
        raw, box["output_parts"] = yield [raw, box["output_parts"]]
        (pair_raw,) = yield [from_heads(raw[:, HD:])]
        (query_raw,) = yield [from_heads(after(raw[:, :HD], pair_raw))]
        query_low = rotate(add_copies(query_raw).astype(f32), cosine, -sine).astype(bf16)
        pair_raw = jnp.sum(pair_raw.astype(f32), axis=(0, 1))
        key_low = rotate(pair_raw[:HD], cosine, -sine).astype(bf16)
        value_low = pair_raw[HD:].astype(bf16)
        low = jnp.concatenate([query_low.reshape(heads, tokens), key_low, value_low], axis=0)
        attn_partial = contract(normed_one, low, 0, 1).astype(bf16)
        (box["attn"],) = yield [to_shards(attn_partial.reshape(shards, rows, -1))]
        normed_one_grad = yield from slab_reduce(contract(low, attn_weight, 0, 1))
        input_part, attn_gain_term = norm_back(inputs.astype(f32), gain_one, normed_one_grad)
        input_grad = residual_grad + input_part
        gain_terms = yield from sum_everywhere(jnp.stack([attn_gain_term, box["ffn_gain"]]))
        return (input_grad, gain_terms)

    half_rows = rows // 2

    def feed_forward_back(last):
        up_partial = contract(normed_two, after(up_low, gate_partial), 0, 0).astype(bf16)
        up_partial = up_partial.reshape(shards, rows, units)
        yield []
        yield []
        gate = after(gate_partial, *box["now"])
        (box["gate0"], up_partial) = yield [to_shards(gate[:, :half_rows]), up_partial]
        yield []
        yield []
        gate = after(gate_partial, *box["now"])
        (box["gate1"],) = yield [to_shards(gate[:, half_rows:])]
        up_now = after(up_partial, *box["now"])
        (box["up0"],) = yield [to_shards(up_now[:, :half_rows])]
        up_now = after(up_partial, *box["now"])
        (box["up1"],) = yield [to_shards(up_now[:, half_rows:])]
        return None

    def feed_forward_out(last):
        low = after(hidden, *last)
        return (yield from slab_reduce(contract(low, own_down, 1, 0)))

    half_width, half_units = width // 2, units // 2

    def down_chunk(c):
        high, right = c // 2, c % 2

        def make():
            return down_parts[
                high * half_units : (high + 1) * half_units,
                right * half_width : (right + 1) * half_width,
            ]

        def put(placed, pieces, sides):
            step = half_units // 4
            placed["down"] = place_blocks(
                placed.get("down"),
                pieces,
                sides,
                (halves * units, width),
                (step, half_width),
                lambda on, i: (on * 8 + high * 4 + i, right),
            )

        return (make, put)

    def column_chunk(name, c, cut, entries):
        size = rows // cut

        def make():
            if cut == 4:
                source, start = box[name + str(c // 2)], (c % 2) * size
            else:
                source, start = box[name], c * size
            return source[:, start : start + size].reshape(shards * size, -1)

        def put(placed, pieces, sides):
            pieces = [piece.reshape(shards, size, -1) for piece in pieces]
            for key, place_part, columns in entries:
                placed[key] = place_part(
                    placed.get(key), [piece[..., columns] for piece in pieces], c, sides, cut
                )

        return (make, put)

    def output_chunk():
        def make():
            partial = box["output_parts"]
            return jnp.concatenate([partial[:, :half_width], partial[:, half_width:]], axis=0)

        def put(placed, pieces, sides):
            placed["output"] = place_blocks(
                placed.get("output"),
                pieces,
                sides,
                (halves * heads, width),
                (heads, half_width),
                lambda on, i: (on, i),
            )

        return (make, put)

    everything = slice(None)
    chunks = [down_chunk(c) for c in range(4)]
    for name in ("gate", "up"):
        chunks += [
            column_chunk(name, c, 4, [(name, place_columns, everything)]) for c in range(4)
        ]
    chunks += [output_chunk()]
    chunks += [
        column_chunk(
            "attn",
            c,
            2,
            [
                ("query", place_columns, slice(0, heads)),
                ("key", place_narrow, slice(heads, heads + HD)),
                ("value", place_narrow, slice(heads + HD, heads + 2 * HD)),
            ],
        )
        for c in range(2)
    ]
    placed = {}
    run_tasks(
        [
            ("attention", lambda t, b: True, attention_back),
            ("parts", lambda t, b: True, feed_forward_back),
            ("even", lambda t, b: True, lambda last: stream(chunks[0::2], placed), 0),
            ("odd", lambda t, b: True, lambda last: stream(chunks[1::2], placed), 1),
            ("out", lambda t, b: t >= 1, feed_forward_out),
        ],
        box,
    )
    input_grad, gain_terms = box["attention"]
    gain_terms = lax.dynamic_slice_in_dim(gain_terms, shard * rows, rows, 1)
    return (
        (residual + box["out"]).astype(bf16),
        input_grad,
        gain_terms[0],
        placed["query"],
        placed["key"],
        placed["value"],
        placed["output"],
        gain_terms[1],
        placed["gate"],
        placed["up"],
        placed["down"],
    )


def solution(mesh):
    shards = mesh.shape["wshard"]
    halves = KVH // shards
    fine = Mesh(
        mesh.devices.reshape(mesh.shape["ctx"] // halves, halves, shards),
        ("line", "xpart", "wshard"),
    )
    every = ("line", "xpart", "wshard")
    in_specs = (
        P(every, None),
        P(),
        P("wshard"),
        P("wshard", None),
        P("wshard", None),
        P("wshard", None),
        P("wshard", None),
        P("wshard"),
        P("wshard", None),
        P("wshard", None),
        P("wshard", None),
        P(every, None),
    )
    out_specs = (
        P(every, None),
        P(every, None),
        P("wshard"),
        P("wshard", None),
        P("wshard", None),
        P("wshard", None),
        P("wshard", None),
        P("wshard"),
        P("wshard", None),
        P("wshard", None),
        P("wshard", None),
    )
    return jax.shard_map(local, mesh=fine, in_specs=in_specs, out_specs=out_specs, check_vma=False)
```

```python
import functools

import jax
import jax.numpy as jnp
from jax import lax
from jax.experimental import pallas as pl
from jax.experimental.pallas import tpu as pltpu
from jax.sharding import Mesh
from jax.sharding import PartitionSpec as P

H = 32
KVH = 8
HD = 64
GROUP = H // KVH

epsilon = 1e-05
rope_base = 500000.0
masked_score = -1e30
f32 = jnp.float32
bf16 = jnp.bfloat16


def rotary_tables(positions, width):
    half_width = width // 2
    frequency = jnp.power(rope_base, -jnp.arange(half_width, dtype=f32) * 2.0 / width)
    angles = frequency[:, None] * positions.astype(f32)[None, :]
    return (jnp.cos(angles), jnp.sin(angles))


def rotate(vector, cosine, sine):
    half_width = vector.shape[-2] // 2
    first = vector[..., :half_width, :]
    second = vector[..., half_width:, :]
    return jnp.concatenate(
        [first * cosine - second * sine, second * cosine + first * sine], axis=-2
    )


def contract(left, right, left_dim, right_dim):
    return lax.dot_general(
        left, right, (((left_dim,), (right_dim,)), ((), ())), preferred_element_type=f32
    )


SLAB = ("xpart", "wshard")


def swap(value, flip):
    return lax.ppermute(value, SLAB, [(i, i ^ flip) for i in range(KVH)])


FLIPS = (0, 2, 4, 6, 1, 3, 5, 7)


def slab_gather(block, turns=False):
    rows = block.shape[0]
    half = rows // 2
    total = jnp.zeros((KVH * rows,) + block.shape[1:], block.dtype)

    def put(total, pieces):
        for index, piece in pieces:
            total = lax.dynamic_update_slice(total, piece, (index * half,) + (0,) * (block.ndim - 1))
        return total

    total = put(total, [(0, block)])
    row, column, other = yield [swap(block, 2), swap(block, 4), swap(block, 1)]
    total = put(total, [(2, row), (4, column), (8, other)])
    if turns:
        far, other_row, other_column = yield [swap(row, 4), swap(row, 1), swap(column, 1)]
        total = put(total, [(6, far), (10, other_row), (12, other_column)])
        far, total = yield [swap(far, 1), total]
        return put(total, [(14, far)])
    far_low, far_high, other_row, other_column = yield [
        swap(row[:half], 4),
        swap(column[half:], 2),
        swap(row, 1),
        swap(column, 1),
    ]
    total = put(total, [(6, far_low), (7, far_high), (10, other_row), (12, other_column)])
    far_low, far_high, total = yield [swap(far_low, 1), swap(far_high, 1), total]
    return put(total, [(14, far_low), (15, far_high)])


def slab_reduce(rows_of, rows):
    (got,) = yield [swap(rows_of(4 * rows, 8 * rows).astype(bf16), 1)]
    own = (rows_of(0, 4 * rows) + got.astype(f32)).reshape(4, rows, -1)
    half = own.shape[-1] // 2
    left, right = own[..., :half], own[..., half:]
    left_got, right_got = yield [
        swap(left[2:].astype(bf16), 4),
        swap(right[1::2].astype(bf16), 2),
    ]
    left = left[:2] + left_got.astype(f32)
    right = right[0::2] + right_got.astype(f32)
    left_got, right_got = yield [
        swap(left[1].astype(bf16), 2),
        swap(right[1].astype(bf16), 4),
    ]
    return jnp.concatenate(
        [left[0] + left_got.astype(f32), right[0] + right_got.astype(f32)], axis=1
    )


def alone(task):
    try:
        transfers = next(task)
        while True:
            transfers = task.send(transfers)
    except StopIteration as stop:
        return stop.value


def after(value, *others):
    return lax.optimization_barrier((value,) + others)[0]


def run_tasks(tasks, box):
    running, stage, last = {}, 0, ()
    tasks = list(tasks)
    while tasks or running:
        for entry in list(tasks):
            name, ready, make, *turn = entry
            if ready(stage, box) and turn in ([], [stage % 2]):
                tasks.remove(entry)
                running[name] = (make(last), None, turn)
        moving = {}
        for name, (task, got, turn) in list(running.items()):
            if turn in ([], [stage % 2]):
                try:
                    moving[name] = task.send(got)
                except StopIteration as stop:
                    del running[name]
                    box[name] = stop.value
        held = lax.optimization_barrier(tuple(v for values in moving.values() for v in values))
        last = held[:1] or last
        box["now"] = last
        done = 0
        for name, values in moving.items():
            task, unused, turn = running[name]
            running[name] = (task, held[done : done + len(values)], turn)
            done += len(values)
        stage += 1


def mix_kernel(names, block, flag_ref, *refs):
    refs = dict(zip(names, refs))

    def read(name):
        return refs[name][...].reshape(block)

    @pl.when(flag_ref[0] == 0)
    def middle():
        if "sum" in refs:
            refs["sum"][...] = (read("now").astype(f32) + read("got").astype(f32)).astype(bf16)
        if "outer" in refs and "kept" in refs:
            refs["outer"][...] = (read("kept").astype(f32) + read("across").astype(f32)).astype(
                bf16
            )
        if "own" in refs:
            refs["own"][...] = read("before")

    @pl.when(flag_ref[0] == 1)
    def end():
        if "outer" in refs and "next" in refs:
            refs["outer"][...] = read("next")
        if "own" in refs:
            refs["own"][...] = read("got")


def mix(outer, sources, arrays, results, steps, block):
    at_end = {"now": 0, "next": 1, "got": None, "kept": 0, "across": 0, "before": 0}
    names, operands, specs = [], [], []
    for name in at_end:
        if name in sources:
            array, shape, index = sources[name]
        elif name in arrays:
            array, shape, index = arrays[name], block, lambda i: (i, 0)
        else:
            continue
        if name == "got" and "sum" not in results:
            used = 1
        elif name == "got" and "own" not in results:
            used = 0
        else:
            used = at_end[name]

        def where(i, flag, index=index, used=used):
            return index(i if used is None else jnp.where(flag[0] == used, i, 0))

        names.append(name)
        operands.append(array)
        specs.append(pl.BlockSpec(shape, where))
    got = pl.pallas_call(
        functools.partial(mix_kernel, tuple(names) + tuple(results), block),
        grid_spec=pltpu.PrefetchScalarGridSpec(
            num_scalar_prefetch=1,
            grid=(steps,),
            in_specs=specs,
            out_specs=[pl.BlockSpec(block, lambda i, flag: (i, 0)) for name in results],
        ),
        out_shape=[
            jax.ShapeDtypeStruct((steps * block[0], block[1]), bf16) for name in results
        ],
        compiler_params=pltpu.CompilerParams(vmem_limit_bytes=32 * 1024 * 1024),
        cost_estimate=pl.CostEstimate(
            flops=0, transcendentals=0, bytes_accessed=10 * steps * block[0] * block[1]
        ),
        name="mix",
    )(outer, *operands)
    return dict(zip(results, got))


def finish(task, sent):
    try:
        while True:
            sent = task.send(lax.optimization_barrier(tuple(sent)))
    except StopIteration:
        pass


def stream(chunks, placed, box, steps, block):
    count, halves = lax.axis_size("line"), lax.axis_size("xpart")
    place, side = lax.axis_index("line"), lax.axis_index("xpart")
    sides = [lax.rem(side + halves - turn, halves) for turn in range(halves)]
    split = count == 4
    outer = jnp.logical_and(split, jnp.logical_or(place == 0, place == count - 1))
    outer = outer.astype(jnp.int32).reshape(1)
    inward, outward, across = [(0, 1), (3, 2)], [(1, 0), (2, 3)], [(1, 2), (2, 1)]
    last = len(chunks)

    def is_chunk(number):
        return 0 <= number < last

    def first(number):
        return mix(outer * 0 + 1, {"next": chunks[number][0]()}, {}, ["outer"], steps, block)

    sending = first(0)["outer"]
    sums, owns, fresh = {}, {}, []
    for stage in range(last + 3):
        moves = {}
        if not split:
            if is_chunk(stage):
                moves["all"] = lax.psum(first(stage)["outer"], "line")
        else:
            pairs = (inward if is_chunk(stage) else []) + (outward if is_chunk(stage - 2) else [])
            if pairs:
                moves["got"] = lax.ppermute(sending, "line", pairs)
            if is_chunk(stage - 1):
                moves["across"] = lax.ppermute(sums[stage - 1], "line", across)
        if is_chunk(stage - 3):
            for turn in range(1, halves):
                moves[turn] = lax.ppermute(
                    owns[stage - 3], "xpart", [(i, (i + turn) % halves) for i in range(halves)]
                )
        held = yield list(moves.values()) + [placed[key] for key in fresh]
        moves = dict(zip(moves, held))
        placed.update(zip(fresh, held[len(moves) :]))
        if split:
            sources, arrays, results = {}, {}, []
            if is_chunk(stage):
                sources["now"] = chunks[stage][0]()
                results.append("sum")
            if is_chunk(stage + 1):
                sources["next"] = chunks[stage + 1][0]()
            if is_chunk(stage - 1):
                arrays.update(kept=sums.pop(stage - 1), across=moves["across"])
            if is_chunk(stage + 1) or is_chunk(stage - 1):
                results.append("outer")
            if is_chunk(stage - 2):
                arrays["before"] = sending
                results.append("own")
            if is_chunk(stage) or is_chunk(stage - 2):
                arrays["got"] = moves["got"]
            if results:
                made = mix(outer, sources, arrays, results, steps, block)
                sending = made.get("outer")
                if is_chunk(stage):
                    sums[stage] = made["sum"]
                if is_chunk(stage - 2):
                    owns[stage - 2] = made["own"]
                box["mixed"] = (next(iter(made.values())),)
        elif is_chunk(stage):
            owns[stage] = moves["all"]
        fresh = []
        if is_chunk(stage - 3):
            pieces = [owns.pop(stage - 3)] + [moves[turn] for turn in range(1, halves)]
            before = dict(placed)
            chunks[stage - 3][1](placed, pieces, sides)
            fresh = [key for key in placed if placed[key] is not before.get(key)]
    return None


def place_kernel(spots_ref, *refs):
    out_ref = refs[-1]
    halves = spots_ref.shape[0] - 1
    columns = refs[0].shape[-1]
    for turn in range(halves):
        for spot in range(halves):

            @pl.when(spots_ref[1 + turn] == spot)
            def put(turn=turn, spot=spot):
                out_ref[:, spot * columns : (spot + 1) * columns] = refs[turn][0].astype(f32)


def place_columns(total, pieces, spot, sides, count):
    shards, rows, columns = pieces[0].shape
    halves = len(pieces)
    operands = [jnp.stack([spot] + sides).astype(jnp.int32)] + list(pieces)
    specs = [pl.BlockSpec((1, rows, columns), lambda w, spots: (w, 0, 0))] * halves
    aliases = {}
    if total is not None:
        aliases = {len(operands): 0}
        operands.append(total)
        specs.append(pl.BlockSpec(memory_space=pl.ANY))
    return pl.pallas_call(
        place_kernel,
        grid_spec=pltpu.PrefetchScalarGridSpec(
            num_scalar_prefetch=1,
            grid=(shards,),
            in_specs=specs,
            out_specs=pl.BlockSpec((rows, halves * columns), lambda w, spots: (spots[0], w)),
        ),
        out_shape=jax.ShapeDtypeStruct((count * rows, shards * halves * columns), f32),
        input_output_aliases=aliases,
        compiler_params=pltpu.CompilerParams(vmem_limit_bytes=32 * 1024 * 1024),
        cost_estimate=pl.CostEstimate(
            flops=0, transcendentals=0, bytes_accessed=6 * halves * shards * rows * columns
        ),
        name="place_columns",
    )(*operands)


def blocks_kernel(sides_ref, *refs):
    out_ref = refs[-1]
    for turn in range(sides_ref.shape[0]):

        @pl.when(pl.program_id(0) == turn)
        def put(turn=turn):
            out_ref[...] = refs[turn][...].astype(f32)


def place_blocks(total, pieces, sides, shape, block, spot):
    halves = len(pieces)
    steps = pieces[0].shape[0] // block[0]

    def source(turn):
        def index(t, i, sides_ref):
            return (jnp.where(t == turn, i, jnp.where(t < turn, 0, steps - 1)), 0)

        return pl.BlockSpec(block, index)

    operands = [jnp.stack(sides).astype(jnp.int32)] + list(pieces)
    specs = [source(turn) for turn in range(halves)]
    aliases = {}
    if total is not None:
        aliases = {len(operands): 0}
        operands.append(total)
        specs.append(pl.BlockSpec(memory_space=pl.ANY))
    return pl.pallas_call(
        blocks_kernel,
        grid_spec=pltpu.PrefetchScalarGridSpec(
            num_scalar_prefetch=1,
            grid=(halves, steps),
            in_specs=specs,
            out_specs=pl.BlockSpec(block, lambda t, i, sides_ref: spot(sides_ref[t], i)),
        ),
        out_shape=jax.ShapeDtypeStruct(shape, f32),
        input_output_aliases=aliases,
        compiler_params=pltpu.CompilerParams(vmem_limit_bytes=32 * 1024 * 1024),
        cost_estimate=pl.CostEstimate(
            flops=0, transcendentals=0, bytes_accessed=6 * halves * pieces[0].size
        ),
        name="place_blocks",
    )(*operands)


def place_narrow(total, pieces, spot, sides, count):
    shards, rows, columns = pieces[0].shape
    halves = len(pieces)
    ordered = [pieces[0]]
    if halves == 2:
        ordered = [jnp.where(sides[0] == t, pieces[0], pieces[1]) for t in range(2)]
    block = jnp.concatenate(
        [ordered[t][w] for w in range(shards) for t in range(halves)], axis=1
    ).astype(f32)
    if total is None:
        total = jnp.zeros((count * rows, block.shape[1]), f32)
    return lax.dynamic_update_slice(total, block, (spot * rows, 0))


def sum_everywhere(vector):
    for flip in (1, 2, 4):
        (got,) = yield [swap(vector, flip)]
        vector = vector + got
    count = lax.axis_size("line")
    flip = 1
    while flip < count:
        (got,) = yield [lax.ppermute(vector, "line", [(i, i ^ flip) for i in range(count)])]
        vector = vector + got
        flip *= 2
    return vector


def move_spans(load, store, order_ref, tiles, span):
    lane = lax.broadcasted_iota(jnp.int32, (1, 2 * span), 1)

    def step(t, unused):
        first, second = order_ref[2 * t], order_ref[2 * t + 1]
        left = load(first // 2).astype(f32)
        right = load(second // 2).astype(f32)
        left = jnp.where(first % 2 == 1, pltpu.roll(left, span, 1), left)
        right = jnp.where(second % 2 == 0, pltpu.roll(right, span, 1), right)
        store(t, jnp.where(lane < span, left, right))
        return unused

    lax.fori_loop(0, tiles, step, 0, unroll=min(8, tiles))


def tile_at(index, tile):
    return pl.ds(pl.multiple_of(index * tile, tile), tile)


def rows_at(start, amount, align):
    return pl.ds(pl.multiple_of(start, align), amount)


def causal(scores, offset, other):
    key = lax.broadcasted_iota(jnp.int32, scores.shape, 0)
    query = lax.broadcasted_iota(jnp.int32, scores.shape, 1)
    return jnp.where(key <= query + offset, scores, other)


def forward_kernel(
    size, span, sort_ref, back_ref, range_ref, blocks_ref, out_ref, sorted_ref, float_ref, log_ref, keys_ref
):
    count, unused, width = blocks_ref.shape
    tile = 2 * span
    per = width // tile
    tiles = count * per

    def load(t):
        return blocks_ref[t // per, :, tile_at(t % per, tile)]

    def store(t, value):
        sorted_ref[:, tile_at(t, tile)] = value.astype(bf16)
        keys_ref[tile_at(t, tile), :] = jnp.transpose(value[HD : 2 * HD, :]).astype(bf16)

    move_spans(load, store, sort_ref, tiles, span)
    half = size // 2

    def query_block(i, unused):
        def part(start, amount, key_start, keys, carried, offset=None):
            accum, running_max, running_sum = carried
            there = rows_at(key_start, keys, size)
            queries = sorted_ref[0:HD, rows_at(start, amount, half)]
            scores = jnp.dot(keys_ref[there, :], queries, preferred_element_type=f32)
            if offset is not None:
                scores = causal(scores, offset, masked_score)
            new_max = jnp.maximum(running_max, jnp.max(scores, axis=0, keepdims=True))
            weights = jnp.exp(scores - new_max)
            shrink = jnp.exp(running_max - new_max)
            running_sum = running_sum * shrink + jnp.sum(weights, axis=0, keepdims=True)
            accum = accum * shrink + jnp.dot(
                sorted_ref[2 * HD : 3 * HD, there],
                weights.astype(bf16),
                preferred_element_type=f32,
            )
            return (accum, new_max, running_sum)

        carried = (
            jnp.zeros((HD, size), f32),
            jnp.full((1, size), masked_score, f32),
            jnp.zeros((1, size), f32),
        )
        first = i * size
        carried = lax.fori_loop(
            0, i, lambda j, carried: part(first, size, j * size, size, carried), carried
        )
        for side in range(2):
            start = first + side * half
            own = tuple(c[:, side * half : (side + 1) * half] for c in carried)
            accum, running_max, running_sum = part(
                start, half, first, (side + 1) * half, own, side * half
            )
            here = rows_at(start, half, half)
            float_ref[:, here] = accum / running_sum
            log_ref[:, here] = running_max + jnp.log(running_sum)
        return unused

    float_ref[...] = jnp.zeros_like(float_ref)
    log_ref[...] = jnp.zeros_like(log_ref)
    lax.fori_loop(range_ref[0], range_ref[1], query_block, 0)

    def store_back(t, value):
        out_ref[t // per, :, tile_at(t % per, tile)] = value.astype(bf16)

    move_spans(lambda t: float_ref[:, tile_at(t, tile)], store_back, back_ref, tiles, span)


def backward_kernel(
    size,
    span,
    sort_ref,
    back_ref,
    range_ref,
    sorted_ref,
    float_ref,
    log_ref,
    blocks_ref,
    out_ref,
    keys_ref,
    values_ref,
    given_ref,
    delta_ref,
    grads_ref,
):
    count, unused, width = blocks_ref.shape
    tile = 2 * span
    per = width // tile
    tiles = count * per

    def load(t):
        return blocks_ref[t // per, :, tile_at(t % per, tile)]

    def store(t, value):
        here = tile_at(t, tile)
        given_ref[:, here] = value.astype(bf16)
        delta_ref[:, here] = jnp.sum(value * float_ref[:, here], axis=0, keepdims=True)
        keys_ref[here, :] = jnp.transpose(sorted_ref[HD : 2 * HD, here].astype(f32)).astype(bf16)
        values_ref[here, :] = jnp.transpose(sorted_ref[2 * HD :, here].astype(f32)).astype(bf16)

    move_spans(load, store, sort_ref, tiles, span)
    half = size // 2
    grads_ref[...] = jnp.zeros_like(grads_ref)

    def key_block(j, unused):
        first_key = j * size
        there = rows_at(first_key, size, size)

        def part(start, amount, keys, carried, offset=None):
            key_acc, value_acc = carried
            here = rows_at(start, amount, half)
            near = rows_at(first_key, keys, size)
            queries = sorted_ref[0:HD, here]
            given = given_ref[:, here]
            scores = jnp.dot(keys_ref[near, :], queries, preferred_element_type=f32)
            probs = jnp.exp(scores - log_ref[:, here])
            if offset is not None:
                probs = causal(probs, offset, 0.0)
            probs_grad = jnp.dot(values_ref[near, :], given, preferred_element_type=f32)
            score_low = (probs * (probs_grad - delta_ref[:, here])).astype(bf16)
            value_acc = value_acc + contract(given, probs.astype(bf16), 1, 1)
            key_acc = key_acc + contract(queries, score_low, 1, 1)
            grads_ref[0:HD, here] += jnp.dot(
                sorted_ref[HD : 2 * HD, near], score_low, preferred_element_type=f32
            ) * (HD**-0.5)
            return (key_acc, value_acc)

        def diagonal(carried):
            near = part(first_key, half, half, tuple(c[:, :half] for c in carried), 0)
            carried = tuple(
                jnp.concatenate([n, c[:, half:]], axis=1) for n, c in zip(near, carried)
            )
            return part(first_key + half, half, size, carried, half)

        carried = (jnp.zeros((HD, size), f32), jnp.zeros((HD, size), f32))
        first, last = range_ref[0], range_ref[1]
        carried = lax.cond(
            jnp.logical_and(j >= first, j < last), diagonal, lambda c: c, carried
        )
        carried = lax.fori_loop(
            jnp.maximum(j + 1, first),
            last,
            lambda i, carried: part(i * size, size, size, carried),
            carried,
        )
        grads_ref[HD : 2 * HD, there] = carried[0]
        grads_ref[2 * HD :, there] = carried[1]
        return unused

    lax.fori_loop(0, range_ref[1], key_block, 0)

    def store_back(t, value):
        out_ref[t // per, :, tile_at(t % per, tile)] = value.astype(bf16)

    move_spans(lambda t: grads_ref[:, tile_at(t, tile)], store_back, back_ref, tiles, span)


def attend_forward(blocks, sort_order, back_order, query_range, span, size):
    count, unused, width = blocks.shape
    total = count * width
    smem = pl.BlockSpec(memory_space=pltpu.SMEM)
    vmem = pl.BlockSpec(memory_space=pltpu.VMEM)
    return pl.pallas_call(
        functools.partial(forward_kernel, size, span),
        out_shape=(
            jax.ShapeDtypeStruct((count, HD, width), bf16),
            jax.ShapeDtypeStruct((3 * HD, total), bf16),
            jax.ShapeDtypeStruct((HD, total), f32),
            jax.ShapeDtypeStruct((1, total), f32),
        ),
        in_specs=[smem, smem, smem, vmem],
        out_specs=(vmem, vmem, vmem, vmem),
        scratch_shapes=[pltpu.VMEM((total, HD), bf16)],
        compiler_params=pltpu.CompilerParams(vmem_limit_bytes=56 * 1024 * 1024),
        cost_estimate=pl.CostEstimate(
            flops=30 * 10**9, transcendentals=0, bytes_accessed=8 * 10**6
        ),
        name="attend_forward",
    )(sort_order, back_order, query_range, blocks)


def attend_backward(
    ordered, floats, logs, blocks, sort_order, back_order, query_range, span, size
):
    count, unused, width = blocks.shape
    total = count * width
    smem = pl.BlockSpec(memory_space=pltpu.SMEM)
    vmem = pl.BlockSpec(memory_space=pltpu.VMEM)
    return pl.pallas_call(
        functools.partial(backward_kernel, size, span),
        out_shape=jax.ShapeDtypeStruct((count, 3 * HD, width), bf16),
        in_specs=[smem, smem, smem, vmem, vmem, vmem, vmem],
        out_specs=vmem,
        scratch_shapes=[
            pltpu.VMEM((total, HD), bf16),
            pltpu.VMEM((total, HD), bf16),
            pltpu.VMEM((HD, total), bf16),
            pltpu.VMEM((1, total), f32),
            pltpu.VMEM((3 * HD, total), f32),
        ],
        compiler_params=pltpu.CompilerParams(vmem_limit_bytes=56 * 1024 * 1024),
        cost_estimate=pl.CostEstimate(
            flops=36 * 10**9, transcendentals=0, bytes_accessed=8 * 10**6
        ),
        name="attend_backward",
    )(sort_order, back_order, query_range, ordered, floats, logs, blocks)


def norm_parts(vector):
    inverse = lax.rsqrt(jnp.mean(vector * vector, axis=-1, keepdims=True) + epsilon)
    return inverse, vector * inverse


def norm_back(vector, scale_gain, gradient):
    inverse, normed = norm_parts(vector)
    gain_term = jnp.sum(gradient * normed, axis=0)
    scaled = gradient * scale_gain
    return (
        inverse * (scaled - normed * jnp.mean(scaled * normed, axis=-1, keepdims=True)),
        gain_term,
    )


def local(
    inputs,
    span_order,
    attn_gain,
    query_weight,
    key_weight,
    value_weight,
    output_weight,
    ffn_gain,
    gate_weight,
    up_weight,
    down_weight,
    cotangent,
):
    tok_dev, width = inputs.shape
    span = tok_dev // 2
    tokens = KVH * tok_dev
    line = lax.axis_size("line")
    halves = lax.axis_size("xpart")
    shards = lax.axis_size("wshard")
    place = lax.axis_index("line")
    side = lax.axis_index("xpart")
    slab_place = side * shards + lax.axis_index("wshard")
    copies = line // GROUP
    rows = width // shards

    flips = jnp.array(FLIPS, jnp.int32)
    devices = jnp.arange(line, dtype=jnp.int32)[:, None] * KVH + (flips ^ slab_place)[None, :]
    slots = (2 * devices[..., None] + jnp.arange(2, dtype=jnp.int32)).reshape(-1)
    spans = span_order.shape[0]
    numbers = jnp.arange(spans, dtype=jnp.int32)
    back_order = jnp.sum(
        jnp.where(slots[:, None] == numbers[None, :], span_order[None, :], 0), axis=1
    )
    sort_order = jnp.sum(
        jnp.where(back_order[None, :] == numbers[:, None], numbers[None, :], 0), axis=1
    )
    total = line * tokens
    size = min(1024, total // copies)
    blocks_each = total // size // copies
    first_block = (place // GROUP) * blocks_each
    query_range = jnp.stack([first_block, first_block + blocks_each]).astype(jnp.int32)
    slab_spans = lax.dynamic_slice_in_dim(back_order, place * 2 * KVH, 2 * KVH, 0)
    positions = (slab_spans[:, None] * span + jnp.arange(span, dtype=jnp.int32)).reshape(-1)
    cosine, sine = rotary_tables(positions, HD)

    shard = lax.axis_index("wshard")

    def pass_on(block, flip):
        return lax.ppermute(block, "wshard", [(i, i ^ flip) for i in range(shards)])

    def in_order(blocks):
        first = blocks[0]
        total = jnp.zeros((shards,) + first.shape, first.dtype)
        for flip, block in enumerate(blocks):
            total = lax.dynamic_update_slice(
                total, block[None], (shard ^ flip,) + (0,) * first.ndim
            )
        return total

    def side_columns(weight, flip):
        units = weight.shape[1] // KVH
        if units % 128 == 0 or halves == 1:
            start = ((shard ^ flip) * halves + side) * units
            return lax.dynamic_slice_in_dim(weight, start, units, 1)
        pair = lax.dynamic_slice_in_dim(weight, (shard ^ flip) * halves * units, halves * units, 1)
        return jnp.where(side == 0, pair[:, :units], pair[:, units:])

    heads = query_weight.shape[1] // KVH
    units = gate_weight.shape[1] // KVH

    def side_block(weights, flip):
        return jnp.concatenate([side_columns(weight, flip) for weight in weights], axis=1)

    box = {}

    def exchange(weights, flips):
        weights = after(weights, *box["now"])
        return [pass_on(side_block(weights, flip), flip) for flip in flips]

    near, middle, far = (1,), range(2, shards // 2 + 1), range(shards // 2 + 1, shards)
    near, middle, far = (
        [flip for flip in flips if flip < shards] for flips in (near, middle, far)
    )

    projections = (query_weight, key_weight, value_weight)
    ffn_weights = (gate_weight, up_weight)

    def weights_task():
        blocks = [side_block(projections, 0)]
        blocks += yield [pass_on(side_block(projections, flip), flip) for flip in near]
        gains = jnp.stack([attn_gain, ffn_gain])
        gains = after(gains, *box["now"])
        got = yield exchange(projections, middle) + [
            pass_on(gains, flip) for flip in range(1, shards)
        ]
        blocks += got[: len(middle)]
        gains = in_order([gains] + list(got[len(middle) :])).astype(f32)
        blocks += yield exchange(projections, far)
        attn_weight = in_order(blocks).reshape(width, -1)
        return (gains[:, 0].reshape(width), gains[:, 1].reshape(width), attn_weight)

    run_tasks(
        [
            ("inputs", lambda t, b: True, lambda last: slab_gather(inputs)),
            ("weights", lambda t, b: True, lambda last: weights_task()),
        ],
        box,
    )
    gain_one, gain_two, attn_weight = box["weights"]
    normed_one = (norm_parts(box["inputs"].astype(f32))[1] * gain_one).astype(bf16)

    own_down = lax.dynamic_slice_in_dim(down_weight, side * units, units, 0)

    projected = contract(attn_weight, normed_one, 0, 1)
    queries = rotate(projected[:heads].reshape(GROUP, HD, tokens), cosine, sine).astype(bf16)
    queries = queries * jnp.asarray(HD**-0.5, bf16)
    keys = rotate(projected[heads : heads + HD], cosine, sine).astype(bf16)
    values = projected[heads + HD :].astype(bf16)
    blocks = jnp.concatenate(
        [queries, jnp.broadcast_to(jnp.concatenate([keys, values]), (GROUP, 2 * HD, tokens))],
        axis=1,
    )
    blocks = lax.all_to_all(jnp.tile(blocks, (copies, 1, 1)), "line", 0, 0, tiled=True)
    def ffn_pass(flips, parts, *now):
        weights = after([ffn_weights[part] for part in parts], *now)
        return [
            (flip, part, pass_on(side_columns(weight, flip), flip))
            for part, weight in zip(parts, weights)
            for flip in flips
        ]

    def held(moves, *others):
        values = lax.optimization_barrier(tuple(value for f, p, value in moves) + others)
        return [(f, p, v) for (f, p, unused), v in zip(moves, values)], values[len(moves) :]

    gathering = slab_gather(after(cotangent, *box["now"]), True)
    first = next(gathering)
    ffn_moves = ffn_pass(near + middle, (0,), first[0])
    ffn_moves, (blocks, *first) = held(ffn_moves, blocks, *first)
    late_moves = ffn_pass(near + middle, (1,), ffn_moves[-1][2])
    second = gathering.send(first)
    attended, ordered, floats, logs = attend_forward(
        blocks, sort_order, back_order, query_range, span, size
    )

    def from_heads(blocks):
        got = lax.all_to_all(blocks, "line", 0, 0, tiled=True)
        return got.reshape((copies, GROUP) + got.shape[1:])

    def add_copies(got):
        return got[0] if copies == 1 else jnp.sum(got.astype(f32), axis=0).astype(bf16)

    own_output = lax.dynamic_slice_in_dim(output_weight, side * heads, heads, 0)
    late_moves, (attended, *second) = held(late_moves, attended, *second)
    ffn_moves += late_moves
    third = gathering.send(second)
    late_moves = ffn_pass(far, (0,), attended)

    def attended_task():
        (blocks,) = yield [from_heads(attended)]
        heads_out = add_copies(blocks).reshape(heads, tokens)
        added = yield from slab_reduce(
            lambda start, stop: contract(heads_out[:, start:stop], own_output, 0, 0), tok_dev
        )
        return (heads_out, inputs.astype(f32) + added)

    def rest_task():
        got = yield [v for f, p, v in late_moves] + third
        moves = [(f, p, v) for (f, p, unused), v in zip(late_moves, got)]
        try:
            gathering.send(got[len(late_moves) :])
        except StopIteration as stop:
            box["cotangent"] = stop.value
        more = ffn_pass(far, (1,), *box["now"])
        yield []
        got = yield [v for f, p, v in more]
        return moves + [(f, p, v) for (f, p, unused), v in zip(more, got)]

    run_tasks(
        [
            ("attended", lambda t, b: True, lambda last: attended_task()),
            ("moves", lambda t, b: True, lambda last: rest_task()),
        ],
        box,
    )
    attended, residual = box["attended"]
    slab_cotangent = box["cotangent"]

    ffn_full = jnp.zeros((shards, rows, 2 * units), bf16)
    moves = [(0, part, side_columns(ffn_weights[part], 0)) for part in range(2)]
    for flip, part, block in moves + ffn_moves + box["moves"]:
        ffn_full = lax.dynamic_update_slice(
            ffn_full, block[None], (shard ^ flip, 0, part * units)
        )
    ffn_full = ffn_full.reshape(width, 2 * units)

    normed_two = alone(
        slab_gather((norm_parts(residual)[1] * gain_two).astype(bf16))
    )
    hidden_grad = contract(slab_cotangent, own_down, 1, 1)
    normed_two, hidden_grad = lax.optimization_barrier((normed_two, hidden_grad))
    ffn_pre = contract(normed_two, ffn_full, 1, 0)
    gate_pre, up_pre = ffn_pre[:, :units], ffn_pre[:, units:]
    sigmoid_gate = jax.nn.sigmoid(gate_pre)
    hidden = (gate_pre * sigmoid_gate * up_pre).astype(bf16)
    down_parts = contract(hidden, slab_cotangent, 0, 0).astype(bf16)
    gate_low = (
        hidden_grad * up_pre * sigmoid_gate * (1.0 + gate_pre * (1.0 - sigmoid_gate))
    ).astype(bf16)
    up_low = (hidden_grad * gate_pre * sigmoid_gate).astype(bf16)

    def to_shards(partial):
        return lax.all_to_all(partial, "wshard", 0, 0, tiled=True)

    gate_partial = contract(normed_two, gate_low, 0, 0).astype(bf16).reshape(shards, rows, units)

    def attention_back(last):
        ffn_low = after(jnp.concatenate([gate_low, up_low], axis=1), gate_partial, *box.get("mixed", ()))
        normed_two_grad = yield from slab_reduce(
            lambda start, stop: contract(ffn_low[start:stop], ffn_full, 1, 1), tok_dev
        )
        residual_part, box["ffn_gain"] = norm_back(residual, gain_two, normed_two_grad)
        residual_grad = cotangent.astype(f32) + residual_part
        branch_low = yield from slab_gather(residual_grad.astype(bf16))
        attended_grad = contract(own_output, branch_low, 1, 1).astype(bf16)
        given = jnp.tile(attended_grad.reshape(GROUP, HD, tokens), (copies, 1, 1))
        (given,) = yield [lax.all_to_all(given, "line", 0, 0, tiled=True)]
        box["output_parts"] = contract(attended, branch_low, 1, 0).astype(bf16)
        raw = attend_backward(
            ordered, floats, logs, given, sort_order, back_order, query_range, span, size
        )
        raw, box["output_parts"] = yield [raw, box["output_parts"]]
        (pair_raw,) = yield [from_heads(raw[:, HD:])]
        (query_raw,) = yield [from_heads(after(raw[:, :HD], pair_raw))]
        query_low = rotate(add_copies(query_raw).astype(f32), cosine, -sine).astype(bf16)
        pair_raw = jnp.sum(pair_raw.astype(f32), axis=(0, 1))
        key_low = rotate(pair_raw[:HD], cosine, -sine).astype(bf16)
        value_low = pair_raw[HD:].astype(bf16)
        low = jnp.concatenate([query_low.reshape(heads, tokens), key_low, value_low], axis=0)
        attn_partial = contract(normed_one, low, 0, 1).astype(bf16)
        (box["attn"],) = yield [to_shards(attn_partial.reshape(shards, rows, -1))]
        normed_one_grad = yield from slab_reduce(
            lambda start, stop: contract(low[:, start:stop], attn_weight, 0, 1), tok_dev
        )
        input_part, attn_gain_term = norm_back(inputs.astype(f32), gain_one, normed_one_grad)
        input_grad = residual_grad + input_part
        gain_terms = yield from sum_everywhere(jnp.stack([attn_gain_term, box["ffn_gain"]]))
        return (input_grad, gain_terms)

    half_rows = rows // 2

    def feed_forward_back(last):
        (box["gate0"],) = yield [to_shards(gate_partial[:, :half_rows])]
        up_partial = contract(normed_two, after(up_low, *box["now"]), 0, 0).astype(bf16)
        (up_partial,) = yield [up_partial.reshape(shards, rows, units)]
        yield []
        yield []
        gate = after(gate_partial, *box["now"])
        (box["gate1"],) = yield [to_shards(gate[:, half_rows:])]
        yield []
        up_now = after(up_partial, *box["now"])
        (box["up0"],) = yield [to_shards(up_now[:, :half_rows])]
        up_now = after(up_partial, *box["now"])
        (box["up1"],) = yield [to_shards(up_now[:, half_rows:])]
        return None

    def feed_forward_out(last):
        low = after(hidden, *last)
        return (
            yield from slab_reduce(
                lambda start, stop: contract(low[start:stop], own_down, 1, 0), tok_dev
            )
        )

    half_width, half_units = width // 2, units // 2

    steps, block = 4, (half_units // 4, half_width)

    def down_chunk(c):
        high, right = c // 2, c % 2

        def source():
            return down_parts, block, lambda i: (high * steps + i, right)

        def put(placed, pieces, sides):
            placed["down"] = place_blocks(
                placed.get("down"),
                pieces,
                sides,
                (halves * units, width),
                (half_units // 2, half_width),
                lambda on, i: (on * 4 + high * 2 + i, right),
            )

        return (source, put)

    def column_chunk(name, c):
        size = rows // 4
        each = shards // steps

        def source():
            return (
                box[name + str(c // 2)],
                (each, size, units),
                lambda i: (i, c % 2, 0),
            )

        def put(placed, pieces, sides):
            pieces = [piece.reshape(shards, size, units) for piece in pieces]
            placed[name] = place_columns(placed.get(name), pieces, c, sides, 4)

        return (source, put)

    def output_chunk():
        def source():
            return box["output_parts"], block, lambda i: (i % 2, i // 2)

        def put(placed, pieces, sides):
            placed["output"] = place_blocks(
                placed.get("output"),
                pieces,
                sides,
                (halves * heads, width),
                (heads, half_width),
                lambda on, i: (on, i),
            )

        return (source, put)

    def attn_chunk(c):
        size, columns = rows // 2, heads + 2 * HD
        beside = 2
        over = shards // beside

        def source():
            part = box["attn"][:, c * size : (c + 1) * size].reshape(over, beside, size, columns)
            part = part.swapaxes(1, 2).reshape(over * size, beside * columns)
            part = jnp.pad(part, ((0, 0), (0, half_width - beside * columns)))
            return part, block, lambda i: (i, 0)

        def put(placed, pieces, sides):
            cut = [
                piece[:, : beside * columns]
                .reshape(over, size, beside, columns)
                .swapaxes(1, 2)
                .reshape(shards, size, columns)
                for piece in pieces
            ]
            for key, place_part, start, stop in (
                ("query", place_columns, 0, heads),
                ("key", place_narrow, heads, heads + HD),
                ("value", place_narrow, heads + HD, columns),
            ):
                placed[key] = place_part(
                    placed.get(key), [piece[..., start:stop] for piece in cut], c, sides, 2
                )

        return (source, put)

    chunks = [down_chunk(c) for c in range(4)]
    chunks += [column_chunk(name, c) for name in ("gate", "up") for c in range(4)]
    chunks += [output_chunk()] + [attn_chunk(c) for c in range(2)]
    placed = {}
    gradients = stream(chunks, placed, box, steps, block)
    sent = gradients.send(lax.optimization_barrier(tuple(next(gradients))))
    run_tasks(
        [
            ("attention", lambda t, b: True, attention_back),
            ("parts", lambda t, b: True, feed_forward_back),
            ("out", lambda t, b: t >= 1, feed_forward_out),
        ],
        box,
    )
    finish(gradients, sent)
    input_grad, gain_terms = box["attention"]
    gain_terms = lax.dynamic_slice_in_dim(gain_terms, shard * rows, rows, 1)
    return (
        (residual + box["out"]).astype(bf16),
        input_grad,
        gain_terms[0],
        placed["query"],
        placed["key"],
        placed["value"],
        placed["output"],
        gain_terms[1],
        placed["gate"],
        placed["up"],
        placed["down"],
    )


def solution(mesh):
    shards = mesh.shape["wshard"]
    halves = KVH // shards
    fine = Mesh(
        mesh.devices.reshape(mesh.shape["ctx"] // halves, halves, shards),
        ("line", "xpart", "wshard"),
    )
    every = ("line", "xpart", "wshard")
    in_specs = (
        P(every, None),
        P(),
        P("wshard"),
        P("wshard", None),
        P("wshard", None),
        P("wshard", None),
        P("wshard", None),
        P("wshard"),
        P("wshard", None),
        P("wshard", None),
        P("wshard", None),
        P(every, None),
    )
    out_specs = (
        P(every, None),
        P(every, None),
        P("wshard"),
        P("wshard", None),
        P("wshard", None),
        P("wshard", None),
        P("wshard", None),
        P("wshard"),
        P("wshard", None),
        P("wshard", None),
        P("wshard", None),
    )
    return jax.shard_map(local, mesh=fine, in_specs=in_specs, out_specs=out_specs, check_vma=False)
```

```python
import functools

import jax
import jax.numpy as jnp
from jax import lax
from jax.experimental import pallas as pl
from jax.experimental.pallas import tpu as pltpu
from jax.sharding import Mesh
from jax.sharding import PartitionSpec as P

H = 32
KVH = 8
HD = 64
GROUP = H // KVH

epsilon = 1e-05
rope_base = 500000.0
masked_score = -1e30
f32 = jnp.float32
bf16 = jnp.bfloat16


def rotary_tables(positions, width):
    half_width = width // 2
    frequency = jnp.power(rope_base, -jnp.arange(half_width, dtype=f32) * 2.0 / width)
    angles = frequency[:, None] * positions.astype(f32)[None, :]
    return (jnp.cos(angles), jnp.sin(angles))


def rotate(vector, cosine, sine):
    half_width = vector.shape[-2] // 2
    first = vector[..., :half_width, :]
    second = vector[..., half_width:, :]
    return jnp.concatenate(
        [first * cosine - second * sine, second * cosine + first * sine], axis=-2
    )


def contract(left, right, left_dim, right_dim):
    return lax.dot_general(
        left, right, (((left_dim,), (right_dim,)), ((), ())), preferred_element_type=f32
    )


SLAB = ("xpart", "wshard")


def swap(value, flip):
    return lax.ppermute(value, SLAB, [(i, i ^ flip) for i in range(KVH)])


FLIPS = (0, 2, 4, 6, 1, 3, 5, 7)


def slab_gather(block, turns=False):
    rows = block.shape[0]
    half = rows // 2
    total = jnp.zeros((KVH * rows,) + block.shape[1:], block.dtype)

    def put(total, pieces):
        for index, piece in pieces:
            total = lax.dynamic_update_slice(total, piece, (index * half,) + (0,) * (block.ndim - 1))
        return total

    total = put(total, [(0, block)])
    row, column, other = yield [swap(block, 2), swap(block, 4), swap(block, 1)]
    total = put(total, [(2, row), (4, column), (8, other)])
    if turns:
        far, other_row, other_column = yield [swap(row, 4), swap(row, 1), swap(column, 1)]
        total = put(total, [(6, far), (10, other_row), (12, other_column)])
        far, total = yield [swap(far, 1), total]
        return put(total, [(14, far)])
    far_low, far_high, other_row, other_column = yield [
        swap(row[:half], 4),
        swap(column[half:], 2),
        swap(row, 1),
        swap(column, 1),
    ]
    total = put(total, [(6, far_low), (7, far_high), (10, other_row), (12, other_column)])
    far_low, far_high, total = yield [swap(far_low, 1), swap(far_high, 1), total]
    return put(total, [(14, far_low), (15, far_high)])


def slab_reduce(rows_of, rows):
    (got,) = yield [swap(rows_of(4 * rows, 8 * rows).astype(bf16), 1)]
    own = (rows_of(0, 4 * rows) + got.astype(f32)).reshape(4, rows, -1)
    half = own.shape[-1] // 2
    left, right = own[..., :half], own[..., half:]
    left_got, right_got = yield [
        swap(left[2:].astype(bf16), 4),
        swap(right[1::2].astype(bf16), 2),
    ]
    left = left[:2] + left_got.astype(f32)
    right = right[0::2] + right_got.astype(f32)
    left_got, right_got = yield [
        swap(left[1].astype(bf16), 2),
        swap(right[1].astype(bf16), 4),
    ]
    return jnp.concatenate(
        [left[0] + left_got.astype(f32), right[0] + right_got.astype(f32)], axis=1
    )


def alone(task):
    try:
        transfers = next(task)
        while True:
            transfers = task.send(transfers)
    except StopIteration as stop:
        return stop.value


def after(value, *others):
    return lax.optimization_barrier((value,) + others)[0]


def run_tasks(tasks, box):
    running, stage, last = {}, 0, ()
    tasks = list(tasks)
    while tasks or running:
        for entry in list(tasks):
            name, ready, make, *turn = entry
            if ready(stage, box) and turn in ([], [stage % 2]):
                tasks.remove(entry)
                running[name] = (make(last), None, turn)
        moving = {}
        for name, (task, got, turn) in list(running.items()):
            if turn in ([], [stage % 2]):
                try:
                    moving[name] = task.send(got)
                except StopIteration as stop:
                    del running[name]
                    box[name] = stop.value
        held = lax.optimization_barrier(tuple(v for values in moving.values() for v in values))
        last = held[:1] or last
        box["now"] = last
        box["stage", stage] = last
        done = 0
        for name, values in moving.items():
            task, unused, turn = running[name]
            running[name] = (task, held[done : done + len(values)], turn)
            done += len(values)
        stage += 1


def mix_kernel(names, block, flag_ref, *refs):
    refs = dict(zip(names, refs))

    def read(name):
        return refs[name][...].reshape(block)

    @pl.when(flag_ref[0] == 0)
    def middle():
        if "sum" in refs:
            refs["sum"][...] = (read("now").astype(f32) + read("got").astype(f32)).astype(bf16)
        if "outer" in refs and "kept" in refs:
            refs["outer"][...] = (read("kept").astype(f32) + read("across").astype(f32)).astype(
                bf16
            )
        if "own" in refs:
            refs["own"][...] = read("before")

    @pl.when(flag_ref[0] == 1)
    def end():
        if "outer" in refs and "next" in refs:
            refs["outer"][...] = read("next")
        if "own" in refs:
            refs["own"][...] = read("got")


def mix(outer, sources, arrays, results, block):
    at_end = {"now": 0, "next": 1, "got": None, "kept": 0, "across": 0, "before": 0}
    names, operands, specs = [], [], []
    for name in at_end:
        if name in sources:
            array, shape, index, blocks = sources[name]
        elif name in arrays:
            array, blocks = arrays[name]
            shape, index = block, lambda i: (i, 0)
        else:
            continue
        if name == "got" and "sum" not in results:
            used = 1
        elif name == "got" and "own" not in results:
            used = 0
        else:
            used = at_end[name]

        def where(i, flag, index=index, used=used, blocks=blocks):
            i = jnp.minimum(i, blocks - 1)
            return index(i if used is None else jnp.where(flag[0] == used, i, 0))

        names.append(name)
        operands.append(array)
        specs.append(pl.BlockSpec(shape, where))
    got = pl.pallas_call(
        functools.partial(mix_kernel, tuple(names) + tuple(results), block),
        grid_spec=pltpu.PrefetchScalarGridSpec(
            num_scalar_prefetch=1,
            grid=(max(results.values()),),
            in_specs=specs,
            out_specs=[
                pl.BlockSpec(block, lambda i, flag, blocks=blocks: (jnp.minimum(i, blocks - 1), 0))
                for blocks in results.values()
            ],
        ),
        out_shape=[
            jax.ShapeDtypeStruct((blocks * block[0], block[1]), bf16)
            for blocks in results.values()
        ],
        compiler_params=pltpu.CompilerParams(vmem_limit_bytes=32 * 1024 * 1024),
        cost_estimate=pl.CostEstimate(
            flops=0,
            transcendentals=0,
            bytes_accessed=10 * max(results.values()) * block[0] * block[1],
        ),
        name="mix",
    )(outer, *operands)
    return dict(zip(results, got))


def finish(tasks):
    results, running = [None] * len(tasks), dict(enumerate(tasks))
    while running:
        held = lax.optimization_barrier(
            tuple(value for task, sent in running.values() for value in sent)
        )
        done = 0
        for number, (task, sent) in list(running.items()):
            try:
                running[number] = (task, task.send(held[done : done + len(sent)]))
            except StopIteration as stop:
                del running[number]
                results[number] = stop.value
            done += len(sent)
    return results


def stream(chunks, placed, box, block):
    count, halves = lax.axis_size("line"), lax.axis_size("xpart")
    place, side = lax.axis_index("line"), lax.axis_index("xpart")
    sides = [lax.rem(side + halves - turn, halves) for turn in range(halves)]
    split = count == 4
    outer = jnp.logical_and(split, jnp.logical_or(place == 0, place == count - 1))
    outer = outer.astype(jnp.int32).reshape(1)
    inward, outward, across = [(0, 1), (3, 2)], [(1, 0), (2, 3)], [(1, 2), (2, 1)]
    last = len(chunks)
    sizes = [blocks for source, put, blocks in chunks]

    def is_chunk(number):
        return 0 <= number < last

    def chunk(number):
        return chunks[number][0]() + (sizes[number],)

    def first(number):
        return mix(
            outer * 0 + 1, {"next": chunk(number)}, {}, {"outer": sizes[number]}, block
        )

    sending, width = first(0)["outer"], sizes[0]
    sums, owns, fresh = {}, {}, []
    for stage in range(last + 3):
        moves = {}
        if not split:
            if is_chunk(stage):
                moves["all"] = lax.psum(first(stage)["outer"], "line")
        else:
            pairs = (inward if is_chunk(stage) else []) + (outward if is_chunk(stage - 2) else [])
            if pairs:
                moves["got"] = lax.ppermute(sending, "line", pairs)
            if is_chunk(stage - 1):
                moves["across"] = lax.ppermute(sums[stage - 1], "line", across)
        if is_chunk(stage - 3):
            for turn in range(1, halves):
                moves[turn] = lax.ppermute(
                    owns[stage - 3], "xpart", [(i, (i + turn) % halves) for i in range(halves)]
                )
        held = yield list(moves.values()) + [placed[key] for key in fresh]
        moves = dict(zip(moves, held))
        placed.update(zip(fresh, held[len(moves) :]))
        if split:
            sources, arrays, results = {}, {}, {}
            if is_chunk(stage):
                sources["now"] = chunk(stage)
                results["sum"] = sizes[stage]
            if is_chunk(stage + 1):
                sources["next"] = chunk(stage + 1)
            if is_chunk(stage - 1):
                arrays["kept"] = (sums.pop(stage - 1), sizes[stage - 1])
                arrays["across"] = (moves["across"], sizes[stage - 1])
            if is_chunk(stage + 1) or is_chunk(stage - 1):
                results["outer"] = max(sizes[n] for n in (stage - 1, stage + 1) if is_chunk(n))
            if is_chunk(stage - 2):
                arrays["before"] = (sending, sizes[stage - 2])
                results["own"] = sizes[stage - 2]
            if is_chunk(stage) or is_chunk(stage - 2):
                arrays["got"] = (moves["got"], width)
            if results:
                made = mix(outer, sources, arrays, results, block)
                sending, width = made.get("outer"), results.get("outer")
                if is_chunk(stage):
                    sums[stage] = made["sum"]
                if is_chunk(stage - 2):
                    owns[stage - 2] = made["own"]
                box["mixed"] = (next(iter(made.values())),)
        elif is_chunk(stage):
            owns[stage] = moves["all"]
        fresh = []
        if is_chunk(stage - 3):
            pieces = [owns.pop(stage - 3)] + [moves[turn] for turn in range(1, halves)]
            before = dict(placed)
            chunks[stage - 3][1](placed, pieces, sides)
            fresh = [key for key in placed if placed[key] is not before.get(key)]
    return None


def place_kernel(spots_ref, *refs):
    out_ref = refs[-1]
    halves = spots_ref.shape[0] - 1
    columns = refs[0].shape[-1]
    for turn in range(halves):
        for spot in range(halves):

            @pl.when(spots_ref[1 + turn] == spot)
            def put(turn=turn, spot=spot):
                out_ref[:, spot * columns : (spot + 1) * columns] = refs[turn][0].astype(f32)


def place_columns(total, pieces, spot, sides, count):
    shards, rows, columns = pieces[0].shape
    halves = len(pieces)
    operands = [jnp.stack([spot] + sides).astype(jnp.int32)] + list(pieces)
    specs = [pl.BlockSpec((1, rows, columns), lambda w, spots: (w, 0, 0))] * halves
    aliases = {}
    if total is not None:
        aliases = {len(operands): 0}
        operands.append(total)
        specs.append(pl.BlockSpec(memory_space=pl.ANY))
    return pl.pallas_call(
        place_kernel,
        grid_spec=pltpu.PrefetchScalarGridSpec(
            num_scalar_prefetch=1,
            grid=(shards,),
            in_specs=specs,
            out_specs=pl.BlockSpec((rows, halves * columns), lambda w, spots: (spots[0], w)),
        ),
        out_shape=jax.ShapeDtypeStruct((count * rows, shards * halves * columns), f32),
        input_output_aliases=aliases,
        compiler_params=pltpu.CompilerParams(vmem_limit_bytes=32 * 1024 * 1024),
        cost_estimate=pl.CostEstimate(
            flops=0, transcendentals=0, bytes_accessed=6 * halves * shards * rows * columns
        ),
        name="place_columns",
    )(*operands)


def blocks_kernel(sides_ref, *refs):
    out_ref = refs[-1]
    for turn in range(sides_ref.shape[0]):

        @pl.when(pl.program_id(0) == turn)
        def put(turn=turn):
            out_ref[...] = refs[turn][...].astype(f32)


def place_blocks(total, pieces, sides, shape, block, spot):
    halves = len(pieces)
    steps = pieces[0].shape[0] // block[0]

    def source(turn):
        def index(t, i, sides_ref):
            return (jnp.where(t == turn, i, jnp.where(t < turn, 0, steps - 1)), 0)

        return pl.BlockSpec(block, index)

    operands = [jnp.stack(sides).astype(jnp.int32)] + list(pieces)
    specs = [source(turn) for turn in range(halves)]
    aliases = {}
    if total is not None:
        aliases = {len(operands): 0}
        operands.append(total)
        specs.append(pl.BlockSpec(memory_space=pl.ANY))
    return pl.pallas_call(
        blocks_kernel,
        grid_spec=pltpu.PrefetchScalarGridSpec(
            num_scalar_prefetch=1,
            grid=(halves, steps),
            in_specs=specs,
            out_specs=pl.BlockSpec(block, lambda t, i, sides_ref: spot(sides_ref[t], i)),
        ),
        out_shape=jax.ShapeDtypeStruct(shape, f32),
        input_output_aliases=aliases,
        compiler_params=pltpu.CompilerParams(vmem_limit_bytes=32 * 1024 * 1024),
        cost_estimate=pl.CostEstimate(
            flops=0, transcendentals=0, bytes_accessed=6 * halves * pieces[0].size
        ),
        name="place_blocks",
    )(*operands)


def attn_kernel(deep, heads, sides_ref, *refs):
    *others, query_ref, key_ref, value_ref = refs
    halves = sides_ref.shape[0]
    pieces = others[:halves]
    across = pieces[0].shape[1] // 128
    kinds = heads // 128
    count = query_ref.shape[1] // heads
    first = lax.broadcasted_iota(jnp.int32, (1, 128), 1) < HD

    def square(order, number, kind, high):
        spot = ((number // halves) * (kinds + 1) + kind) * deep + high
        down, right = spot // across * 128, spot % across * 128
        piece = pieces[order[number % halves]]
        return piece[down : down + 128, right : right + 128].astype(f32)

    for turn in range(halves):

        @pl.when(sides_ref[0] == turn)
        def put(turn=turn):
            order = [(side + turn) % halves for side in range(halves)]
            for high in range(deep):
                rows = slice(high * 128, (high + 1) * 128)
                for number in range(count):
                    for kind in range(kinds):
                        left = number * heads + kind * 128
                        query_ref[rows, left : left + 128] = square(order, number, kind, high)
                for pair in range(count // 2):
                    even = square(order, 2 * pair, kinds, high)
                    odd = square(order, 2 * pair + 1, kinds, high)
                    here = slice(pair * 128, (pair + 1) * 128)
                    key_ref[rows, here] = jnp.where(first, even, pltpu.roll(odd, HD, 1))
                    value_ref[rows, here] = jnp.where(first, pltpu.roll(even, HD, 1), odd)


def place_attn(totals, pieces, spot, sides, size, heads, shards, count):
    halves = len(pieces)
    columns = [shards * halves * width for width in (heads, HD, HD)]
    operands = [jnp.stack(sides).astype(jnp.int32)] + list(pieces)
    specs = [pl.BlockSpec(memory_space=pltpu.VMEM)] * halves
    aliases = {}
    if totals is not None:
        aliases = {len(operands) + i: i for i in range(3)}
        operands += totals
        specs += [pl.BlockSpec(memory_space=pl.ANY)] * 3

    def kernel(sides_ref, *refs):
        attn_kernel(size // 128, heads, sides_ref, *refs[:halves], *refs[-3:])

    return pl.pallas_call(
        kernel,
        grid_spec=pltpu.PrefetchScalarGridSpec(
            num_scalar_prefetch=1,
            grid=(1,),
            in_specs=specs,
            out_specs=[
                pl.BlockSpec((size, width), lambda i, sides_ref: (spot, 0)) for width in columns
            ],
        ),
        out_shape=[jax.ShapeDtypeStruct((count * size, width), f32) for width in columns],
        input_output_aliases=aliases,
        compiler_params=pltpu.CompilerParams(vmem_limit_bytes=32 * 1024 * 1024),
        cost_estimate=pl.CostEstimate(
            flops=0, transcendentals=0, bytes_accessed=6 * size * sum(columns)
        ),
        name="place_attn",
    )(*operands)


def sum_everywhere(vector, stages):
    for unused in range(stages):
        yield []
    got = yield [swap(vector, flip) for flip in range(1, KVH)]
    vector = sum(got, vector)
    count = lax.axis_size("line")
    got = yield [
        lax.ppermute(vector, "line", [(i, (i + turn) % count) for i in range(count)])
        for turn in range(1, count)
    ]
    return sum(got, vector)


def move_spans(load, store, order_ref, tiles, span):
    lane = lax.broadcasted_iota(jnp.int32, (1, 2 * span), 1)

    def step(t, unused):
        first, second = order_ref[2 * t], order_ref[2 * t + 1]
        left = load(first // 2).astype(f32)
        right = load(second // 2).astype(f32)
        left = jnp.where(first % 2 == 1, pltpu.roll(left, span, 1), left)
        right = jnp.where(second % 2 == 0, pltpu.roll(right, span, 1), right)
        store(t, jnp.where(lane < span, left, right))
        return unused

    lax.fori_loop(0, tiles, step, 0, unroll=min(8, tiles))


def tile_at(index, tile):
    return pl.ds(pl.multiple_of(index * tile, tile), tile)


def rows_at(start, amount, align):
    return pl.ds(pl.multiple_of(start, align), amount)


def causal(scores, offset, other):
    key = lax.broadcasted_iota(jnp.int32, scores.shape, 0)
    query = lax.broadcasted_iota(jnp.int32, scores.shape, 1)
    return jnp.where(key <= query + offset, scores, other)


def forward_kernel(
    size, span, sort_ref, back_ref, range_ref, blocks_ref, out_ref, sorted_ref, float_ref, log_ref, keys_ref
):
    count, unused, width = blocks_ref.shape
    tile = 2 * span
    per = width // tile
    tiles = count * per

    def load(t):
        return blocks_ref[t // per, :, tile_at(t % per, tile)]

    def store(t, value):
        sorted_ref[:, tile_at(t, tile)] = value.astype(bf16)
        keys_ref[tile_at(t, tile), :] = jnp.transpose(value[HD : 2 * HD, :]).astype(bf16)

    move_spans(load, store, sort_ref, tiles, span)
    half = size // 2

    def query_block(i, unused):
        def part(start, amount, key_start, keys, carried, offset=None):
            accum, running_max, running_sum = carried
            there = rows_at(key_start, keys, size)
            queries = sorted_ref[0:HD, rows_at(start, amount, half)]
            scores = jnp.dot(keys_ref[there, :], queries, preferred_element_type=f32)
            if offset is not None:
                scores = causal(scores, offset, masked_score)
            new_max = jnp.maximum(running_max, jnp.max(scores, axis=0, keepdims=True))
            weights = jnp.exp(scores - new_max)
            shrink = jnp.exp(running_max - new_max)
            running_sum = running_sum * shrink + jnp.sum(weights, axis=0, keepdims=True)
            accum = accum * shrink + jnp.dot(
                sorted_ref[2 * HD : 3 * HD, there],
                weights.astype(bf16),
                preferred_element_type=f32,
            )
            return (accum, new_max, running_sum)

        carried = (
            jnp.zeros((HD, size), f32),
            jnp.full((1, size), masked_score, f32),
            jnp.zeros((1, size), f32),
        )
        first = i * size
        carried = lax.fori_loop(
            0, i, lambda j, carried: part(first, size, j * size, size, carried), carried
        )
        for side in range(2):
            start = first + side * half
            own = tuple(c[:, side * half : (side + 1) * half] for c in carried)
            accum, running_max, running_sum = part(
                start, half, first, (side + 1) * half, own, side * half
            )
            here = rows_at(start, half, half)
            float_ref[:, here] = accum / running_sum
            log_ref[:, here] = running_max + jnp.log(running_sum)
        return unused

    float_ref[...] = jnp.zeros_like(float_ref)
    log_ref[...] = jnp.zeros_like(log_ref)
    lax.fori_loop(range_ref[0], range_ref[1], query_block, 0)

    def store_back(t, value):
        out_ref[t // per, :, tile_at(t % per, tile)] = value.astype(bf16)

    move_spans(lambda t: float_ref[:, tile_at(t, tile)], store_back, back_ref, tiles, span)


def backward_kernel(
    size,
    span,
    sort_ref,
    back_ref,
    range_ref,
    sorted_ref,
    float_ref,
    log_ref,
    blocks_ref,
    out_ref,
    keys_ref,
    values_ref,
    given_ref,
    delta_ref,
    grads_ref,
):
    count, unused, width = blocks_ref.shape
    tile = 2 * span
    per = width // tile
    tiles = count * per

    def load(t):
        return blocks_ref[t // per, :, tile_at(t % per, tile)]

    def store(t, value):
        here = tile_at(t, tile)
        given_ref[:, here] = value.astype(bf16)
        delta_ref[:, here] = jnp.sum(value * float_ref[:, here], axis=0, keepdims=True)
        keys_ref[here, :] = jnp.transpose(sorted_ref[HD : 2 * HD, here].astype(f32)).astype(bf16)
        values_ref[here, :] = jnp.transpose(sorted_ref[2 * HD :, here].astype(f32)).astype(bf16)

    move_spans(load, store, sort_ref, tiles, span)
    half = size // 2
    grads_ref[...] = jnp.zeros_like(grads_ref)

    def key_block(j, unused):
        first_key = j * size
        there = rows_at(first_key, size, size)

        def part(start, amount, keys, carried, offset=None):
            key_acc, value_acc = carried
            here = rows_at(start, amount, half)
            near = rows_at(first_key, keys, size)
            queries = sorted_ref[0:HD, here]
            given = given_ref[:, here]
            scores = jnp.dot(keys_ref[near, :], queries, preferred_element_type=f32)
            probs = jnp.exp(scores - log_ref[:, here])
            if offset is not None:
                probs = causal(probs, offset, 0.0)
            probs_grad = jnp.dot(values_ref[near, :], given, preferred_element_type=f32)
            score_low = (probs * (probs_grad - delta_ref[:, here])).astype(bf16)
            value_acc = value_acc + contract(given, probs.astype(bf16), 1, 1)
            key_acc = key_acc + contract(queries, score_low, 1, 1)
            grads_ref[0:HD, here] += jnp.dot(
                sorted_ref[HD : 2 * HD, near], score_low, preferred_element_type=f32
            ) * (HD**-0.5)
            return (key_acc, value_acc)

        def diagonal(carried):
            near = part(first_key, half, half, tuple(c[:, :half] for c in carried), 0)
            carried = tuple(
                jnp.concatenate([n, c[:, half:]], axis=1) for n, c in zip(near, carried)
            )
            return part(first_key + half, half, size, carried, half)

        carried = (jnp.zeros((HD, size), f32), jnp.zeros((HD, size), f32))
        first, last = range_ref[0], range_ref[1]
        carried = lax.cond(
            jnp.logical_and(j >= first, j < last), diagonal, lambda c: c, carried
        )
        carried = lax.fori_loop(
            jnp.maximum(j + 1, first),
            last,
            lambda i, carried: part(i * size, size, size, carried),
            carried,
        )
        grads_ref[HD : 2 * HD, there] = carried[0]
        grads_ref[2 * HD :, there] = carried[1]
        return unused

    lax.fori_loop(0, range_ref[1], key_block, 0)

    def store_back(t, value):
        out_ref[t // per, :, tile_at(t % per, tile)] = value.astype(bf16)

    move_spans(lambda t: grads_ref[:, tile_at(t, tile)], store_back, back_ref, tiles, span)


def attend_forward(blocks, sort_order, back_order, query_range, span, size):
    count, unused, width = blocks.shape
    total = count * width
    smem = pl.BlockSpec(memory_space=pltpu.SMEM)
    vmem = pl.BlockSpec(memory_space=pltpu.VMEM)
    return pl.pallas_call(
        functools.partial(forward_kernel, size, span),
        out_shape=(
            jax.ShapeDtypeStruct((count, HD, width), bf16),
            jax.ShapeDtypeStruct((3 * HD, total), bf16),
            jax.ShapeDtypeStruct((HD, total), f32),
            jax.ShapeDtypeStruct((1, total), f32),
        ),
        in_specs=[smem, smem, smem, vmem],
        out_specs=(vmem, vmem, vmem, vmem),
        scratch_shapes=[pltpu.VMEM((total, HD), bf16)],
        compiler_params=pltpu.CompilerParams(vmem_limit_bytes=56 * 1024 * 1024),
        cost_estimate=pl.CostEstimate(
            flops=30 * 10**9, transcendentals=0, bytes_accessed=8 * 10**6
        ),
        name="attend_forward",
    )(sort_order, back_order, query_range, blocks)


def attend_backward(
    ordered, floats, logs, blocks, sort_order, back_order, query_range, span, size
):
    count, unused, width = blocks.shape
    total = count * width
    smem = pl.BlockSpec(memory_space=pltpu.SMEM)
    vmem = pl.BlockSpec(memory_space=pltpu.VMEM)
    return pl.pallas_call(
        functools.partial(backward_kernel, size, span),
        out_shape=jax.ShapeDtypeStruct((count, 3 * HD, width), bf16),
        in_specs=[smem, smem, smem, vmem, vmem, vmem, vmem],
        out_specs=vmem,
        scratch_shapes=[
            pltpu.VMEM((total, HD), bf16),
            pltpu.VMEM((total, HD), bf16),
            pltpu.VMEM((HD, total), bf16),
            pltpu.VMEM((1, total), f32),
            pltpu.VMEM((3 * HD, total), f32),
        ],
        compiler_params=pltpu.CompilerParams(vmem_limit_bytes=56 * 1024 * 1024),
        cost_estimate=pl.CostEstimate(
            flops=36 * 10**9, transcendentals=0, bytes_accessed=8 * 10**6
        ),
        name="attend_backward",
    )(sort_order, back_order, query_range, ordered, floats, logs, blocks)


def norm_parts(vector):
    inverse = lax.rsqrt(jnp.mean(vector * vector, axis=-1, keepdims=True) + epsilon)
    return inverse, vector * inverse


def norm_back(vector, scale_gain, gradient):
    inverse, normed = norm_parts(vector)
    gain_term = jnp.sum(gradient * normed, axis=0)
    scaled = gradient * scale_gain
    return (
        inverse * (scaled - normed * jnp.mean(scaled * normed, axis=-1, keepdims=True)),
        gain_term,
    )


def local(
    inputs,
    span_order,
    attn_gain,
    query_weight,
    key_weight,
    value_weight,
    output_weight,
    ffn_gain,
    gate_weight,
    up_weight,
    down_weight,
    cotangent,
):
    tok_dev, width = inputs.shape
    span = tok_dev // 2
    tokens = KVH * tok_dev
    line = lax.axis_size("line")
    halves = lax.axis_size("xpart")
    shards = lax.axis_size("wshard")
    place = lax.axis_index("line")
    side = lax.axis_index("xpart")
    slab_place = side * shards + lax.axis_index("wshard")
    copies = line // GROUP
    rows = width // shards

    flips = jnp.array(FLIPS, jnp.int32)
    devices = jnp.arange(line, dtype=jnp.int32)[:, None] * KVH + (flips ^ slab_place)[None, :]
    slots = (2 * devices[..., None] + jnp.arange(2, dtype=jnp.int32)).reshape(-1)
    spans = span_order.shape[0]
    numbers = jnp.arange(spans, dtype=jnp.int32)
    back_order = jnp.sum(
        jnp.where(slots[:, None] == numbers[None, :], span_order[None, :], 0), axis=1
    )
    sort_order = jnp.sum(
        jnp.where(back_order[None, :] == numbers[:, None], numbers[None, :], 0), axis=1
    )
    total = line * tokens
    size = min(1024, total // copies)
    blocks_each = total // size // copies
    first_block = (place // GROUP) * blocks_each
    query_range = jnp.stack([first_block, first_block + blocks_each]).astype(jnp.int32)
    slab_spans = lax.dynamic_slice_in_dim(back_order, place * 2 * KVH, 2 * KVH, 0)
    positions = (slab_spans[:, None] * span + jnp.arange(span, dtype=jnp.int32)).reshape(-1)
    cosine, sine = rotary_tables(positions, HD)

    shard = lax.axis_index("wshard")

    def pass_on(block, flip):
        return lax.ppermute(block, "wshard", [(i, i ^ flip) for i in range(shards)])

    def in_order(blocks):
        first = blocks[0]
        total = jnp.zeros((shards,) + first.shape, first.dtype)
        for flip, block in enumerate(blocks):
            total = lax.dynamic_update_slice(
                total, block[None], (shard ^ flip,) + (0,) * first.ndim
            )
        return total

    def side_columns(weight, flip):
        units = weight.shape[1] // KVH
        if units % 128 == 0 or halves == 1:
            start = ((shard ^ flip) * halves + side) * units
            return lax.dynamic_slice_in_dim(weight, start, units, 1)
        pair = lax.dynamic_slice_in_dim(weight, (shard ^ flip) * halves * units, halves * units, 1)
        return jnp.where(side == 0, pair[:, :units], pair[:, units:])

    heads = query_weight.shape[1] // KVH
    units = gate_weight.shape[1] // KVH

    def side_block(weights, flip):
        return jnp.concatenate([side_columns(weight, flip) for weight in weights], axis=1)

    box = {}

    def exchange(weights, flips):
        weights = after(weights, *box["now"])
        return [pass_on(side_block(weights, flip), flip) for flip in flips]

    near, middle, far = (1,), range(2, shards // 2 + 1), range(shards // 2 + 1, shards)
    near, middle, far = (
        [flip for flip in flips if flip < shards] for flips in (near, middle, far)
    )

    projections = (query_weight, key_weight, value_weight)
    ffn_weights = (gate_weight, up_weight)

    def weights_task():
        blocks = [side_block(projections, 0)]
        blocks += yield [pass_on(side_block(projections, flip), flip) for flip in near]
        gains = jnp.stack([attn_gain, ffn_gain])
        gains = after(gains, *box["now"])
        got = yield exchange(projections, middle) + [
            pass_on(gains, flip) for flip in range(1, shards)
        ]
        blocks += got[: len(middle)]
        gains = in_order([gains] + list(got[len(middle) :])).astype(f32)
        blocks += yield exchange(projections, far)
        attn_weight = in_order(blocks).reshape(width, -1)
        return (gains[:, 0].reshape(width), gains[:, 1].reshape(width), attn_weight)

    run_tasks(
        [
            ("inputs", lambda t, b: True, lambda last: slab_gather(inputs)),
            ("weights", lambda t, b: True, lambda last: weights_task()),
        ],
        box,
    )
    gain_one, gain_two, attn_weight = box["weights"]
    normed_one = (norm_parts(box["inputs"].astype(f32))[1] * gain_one).astype(bf16)

    own_down = lax.dynamic_slice_in_dim(down_weight, side * units, units, 0)

    projected = contract(attn_weight, normed_one, 0, 1)
    queries = rotate(projected[:heads].reshape(GROUP, HD, tokens), cosine, sine).astype(bf16)
    queries = queries * jnp.asarray(HD**-0.5, bf16)
    keys = rotate(projected[heads : heads + HD], cosine, sine).astype(bf16)
    values = projected[heads + HD :].astype(bf16)
    blocks = jnp.concatenate(
        [queries, jnp.broadcast_to(jnp.concatenate([keys, values]), (GROUP, 2 * HD, tokens))],
        axis=1,
    )
    blocks = lax.all_to_all(jnp.tile(blocks, (copies, 1, 1)), "line", 0, 0, tiled=True)
    def ffn_pass(flips, parts, *now):
        weights = after([ffn_weights[part] for part in parts], *now)
        return [
            (flip, part, pass_on(side_columns(weight, flip), flip))
            for part, weight in zip(parts, weights)
            for flip in flips
        ]

    def held(moves, *others):
        values = lax.optimization_barrier(tuple(value for f, p, value in moves) + others)
        return [(f, p, v) for (f, p, unused), v in zip(moves, values)], values[len(moves) :]

    gathering = slab_gather(after(cotangent, *box["now"]), True)
    first = next(gathering)
    ffn_moves = ffn_pass(near + middle, (0,), first[0])
    ffn_moves, (blocks, *first) = held(ffn_moves, blocks, *first)
    late_moves = ffn_pass(near + middle, (1,), ffn_moves[-1][2])
    second = gathering.send(first)
    attended, ordered, floats, logs = attend_forward(
        blocks, sort_order, back_order, query_range, span, size
    )

    def from_heads(blocks):
        got = lax.all_to_all(blocks, "line", 0, 0, tiled=True)
        return got.reshape((copies, GROUP) + got.shape[1:])

    def add_copies(got):
        return got[0] if copies == 1 else jnp.sum(got.astype(f32), axis=0).astype(bf16)

    own_output = lax.dynamic_slice_in_dim(output_weight, side * heads, heads, 0)
    late_moves, (attended, *second) = held(late_moves, attended, *second)
    ffn_moves += late_moves
    third = gathering.send(second)
    late_moves = ffn_pass(far, (0,), attended)

    def attended_task():
        (blocks,) = yield [from_heads(attended)]
        heads_out = add_copies(blocks).reshape(heads, tokens)
        added = yield from slab_reduce(
            lambda start, stop: contract(heads_out[:, start:stop], own_output, 0, 0), tok_dev
        )
        return (heads_out, inputs.astype(f32) + added)

    def rest_task():
        got = yield [v for f, p, v in late_moves] + third
        moves = [(f, p, v) for (f, p, unused), v in zip(late_moves, got)]
        try:
            gathering.send(got[len(late_moves) :])
        except StopIteration as stop:
            box["cotangent"] = stop.value
        more = ffn_pass(far, (1,), *box["now"])
        yield []
        got = yield [v for f, p, v in more]
        return moves + [(f, p, v) for (f, p, unused), v in zip(more, got)]

    run_tasks(
        [
            ("attended", lambda t, b: True, lambda last: attended_task()),
            ("moves", lambda t, b: True, lambda last: rest_task()),
        ],
        box,
    )
    attended, residual = box["attended"]
    slab_cotangent = box["cotangent"]

    ffn_full = jnp.zeros((shards, rows, 2 * units), bf16)
    moves = [(0, part, side_columns(ffn_weights[part], 0)) for part in range(2)]
    for flip, part, block in moves + ffn_moves + box["moves"]:
        ffn_full = lax.dynamic_update_slice(
            ffn_full, block[None], (shard ^ flip, 0, part * units)
        )
    ffn_full = ffn_full.reshape(width, 2 * units)

    normed_two = alone(
        slab_gather((norm_parts(residual)[1] * gain_two).astype(bf16))
    )
    hidden_grad = contract(slab_cotangent, own_down, 1, 1)
    normed_two, hidden_grad = lax.optimization_barrier((normed_two, hidden_grad))
    ffn_pre = contract(normed_two, ffn_full, 1, 0)
    gate_pre, up_pre = ffn_pre[:, :units], ffn_pre[:, units:]
    sigmoid_gate = jax.nn.sigmoid(gate_pre)
    hidden = (gate_pre * sigmoid_gate * up_pre).astype(bf16)
    down_parts = contract(hidden, slab_cotangent, 0, 0).astype(bf16)
    gate_low = (
        hidden_grad * up_pre * sigmoid_gate * (1.0 + gate_pre * (1.0 - sigmoid_gate))
    ).astype(bf16)
    up_low = (hidden_grad * gate_pre * sigmoid_gate).astype(bf16)

    def to_shards(partial):
        return lax.all_to_all(partial, "wshard", 0, 0, tiled=True)

    gate_partial = contract(normed_two, gate_low, 0, 0).astype(bf16).reshape(shards, rows, units)

    def attention_back(last):
        ffn_low = after(jnp.concatenate([gate_low, up_low], axis=1), gate_partial, *box.get("mixed", ()))
        normed_two_grad = yield from slab_reduce(
            lambda start, stop: contract(ffn_low[start:stop], ffn_full, 1, 1), tok_dev
        )
        residual_part, box["ffn_gain"] = norm_back(residual, gain_two, normed_two_grad)
        residual_grad = cotangent.astype(f32) + residual_part
        branch_low = yield from slab_gather(residual_grad.astype(bf16))
        attended_grad = contract(own_output, branch_low, 1, 1).astype(bf16)
        given = jnp.tile(attended_grad.reshape(GROUP, HD, tokens), (copies, 1, 1))
        (given,) = yield [lax.all_to_all(given, "line", 0, 0, tiled=True)]
        box["output_parts"] = contract(attended, branch_low, 1, 0).astype(bf16)
        raw = attend_backward(
            ordered, floats, logs, given, sort_order, back_order, query_range, span, size
        )
        raw, box["output_parts"] = yield [raw, box["output_parts"]]
        (pair_raw,) = yield [from_heads(raw[:, HD:])]
        (query_raw,) = yield [from_heads(after(raw[:, :HD], pair_raw))]
        query_low = rotate(add_copies(query_raw).astype(f32), cosine, -sine).astype(bf16)
        pair_raw = jnp.sum(pair_raw.astype(f32), axis=(0, 1))
        key_low = rotate(pair_raw[:HD], cosine, -sine).astype(bf16)
        value_low = pair_raw[HD:].astype(bf16)
        low = jnp.concatenate([query_low.reshape(heads, tokens), key_low, value_low], axis=0)
        attn_partial = contract(normed_one, low, 0, 1).astype(bf16)
        (box["attn"],) = yield [to_shards(attn_partial.reshape(shards, rows, -1))]
        normed_one_grad = yield from slab_reduce(
            lambda start, stop: contract(low[:, start:stop], attn_weight, 0, 1), tok_dev
        )
        input_part, attn_gain_term = norm_back(inputs.astype(f32), gain_one, normed_one_grad)
        input_grad = residual_grad + input_part
        return (input_grad, jnp.stack([attn_gain_term, box["ffn_gain"]]))

    half_rows = rows // 2

    def feed_forward_back(last):
        gate0 = to_shards(gate_partial[:, :half_rows])
        yield []
        up_partial = contract(normed_two, after(up_low, *box["now"]), 0, 0).astype(bf16)
        (up_partial,) = yield [up_partial.reshape(shards, rows, units)]
        box["gate0"], gate_now = yield [gate0, gate_partial]
        gate1 = to_shards(gate_now[:, half_rows:])
        yield []
        yield []
        (box["gate1"],) = yield [gate1]
        up_now = after(up_partial, *box["now"])
        (box["up0"],) = yield [to_shards(up_now[:, :half_rows])]
        up_now = after(up_partial, *box["now"])
        (box["up1"],) = yield [to_shards(up_now[:, half_rows:])]
        return None

    def feed_forward_out(last):
        low = after(hidden, *box["stage", 1])
        return (
            yield from slab_reduce(
                lambda start, stop: contract(low[start:stop], own_down, 1, 0), tok_dev
            )
        )

    half_width, half_units = width // 2, units // 2

    steps, block = 4, (half_units // 4, half_width)

    def down_chunk(c):
        high, right = c // 2, c % 2

        def source():
            return down_parts, block, lambda i: (high * steps + i, right)

        def put(placed, pieces, sides):
            placed["down"] = place_blocks(
                placed.get("down"),
                pieces,
                sides,
                (halves * units, width),
                (half_units // 2, half_width),
                lambda on, i: (on * 4 + high * 2 + i, right),
            )

        return (source, put, steps)

    def column_chunk(name, c):
        size = rows // 4
        each = shards // steps

        def source():
            return (
                box[name + str(c // 2)],
                (each, size, units),
                lambda i: (i, c % 2, 0),
            )

        def put(placed, pieces, sides):
            pieces = [piece.reshape(shards, size, units) for piece in pieces]
            placed[name] = place_columns(placed.get(name), pieces, c, sides, 4)

        return (source, put, steps)

    def output_chunk():
        def source():
            return box["output_parts"], block, lambda i: (i % 2, i // 2)

        def put(placed, pieces, sides):
            placed["output"] = place_blocks(
                placed.get("output"),
                pieces,
                sides,
                (halves * heads, width),
                (heads, half_width),
                lambda on, i: (on, i),
            )

        return (source, put, steps)

    def attn_chunk(c):
        size, columns = rows // 2, heads + 2 * HD
        deep, wide, across = size // 128, columns // 128, half_width // 128
        blocks = shards * deep * wide // across

        def source():
            part = box["attn"][:, c * size : (c + 1) * size]
            squares = [
                part[w, h * 128 : (h + 1) * 128, b * 128 : (b + 1) * 128]
                for w in range(shards)
                for b in range(wide)
                for h in range(deep)
            ]
            lines = [
                jnp.concatenate(squares[g * across : (g + 1) * across], axis=1)
                for g in range(blocks)
            ]
            return jnp.concatenate(lines, axis=0), block, lambda i: (i, 0)

        def put(placed, pieces, sides):
            names = ("query", "key", "value")
            totals = [placed[name] for name in names] if "query" in placed else None
            totals = place_attn(totals, pieces, c, sides, size, heads, shards, 2)
            placed.update(zip(names, totals))

        return (source, put, blocks)

    chunks = [down_chunk(c) for c in range(4)]
    chunks += [column_chunk(name, c) for name in ("gate", "up") for c in range(4)]
    chunks += [output_chunk()] + [attn_chunk(c) for c in range(2)]
    placed = {}
    gradients = stream(chunks, placed, box, block)
    sent = gradients.send(lax.optimization_barrier(tuple(next(gradients))))
    run_tasks(
        [
            ("attention", lambda t, b: True, attention_back),
            ("parts", lambda t, b: True, feed_forward_back),
        ],
        box,
    )
    run_tasks([("out", lambda t, b: True, feed_forward_out)], box)
    input_grad, gain_terms = box["attention"]
    gain_sums = sum_everywhere(gain_terms, len(chunks) - 1)
    gain_terms = finish([(gradients, sent), (gain_sums, next(gain_sums))])[1]
    gain_terms = lax.dynamic_slice_in_dim(gain_terms, shard * rows, rows, 1)
    return (
        (residual + box["out"]).astype(bf16),
        input_grad,
        gain_terms[0],
        placed["query"],
        placed["key"],
        placed["value"],
        placed["output"],
        gain_terms[1],
        placed["gate"],
        placed["up"],
        placed["down"],
    )


def solution(mesh):
    shards = mesh.shape["wshard"]
    halves = KVH // shards
    fine = Mesh(
        mesh.devices.reshape(mesh.shape["ctx"] // halves, halves, shards),
        ("line", "xpart", "wshard"),
    )
    every = ("line", "xpart", "wshard")
    in_specs = (
        P(every, None),
        P(),
        P("wshard"),
        P("wshard", None),
        P("wshard", None),
        P("wshard", None),
        P("wshard", None),
        P("wshard"),
        P("wshard", None),
        P("wshard", None),
        P("wshard", None),
        P(every, None),
    )
    out_specs = (
        P(every, None),
        P(every, None),
        P("wshard"),
        P("wshard", None),
        P("wshard", None),
        P("wshard", None),
        P("wshard", None),
        P("wshard"),
        P("wshard", None),
        P("wshard", None),
        P("wshard", None),
    )
    return jax.shard_map(local, mesh=fine, in_specs=in_specs, out_specs=out_specs, check_vma=False)
```

```python
import functools

import jax
import jax.numpy as jnp
from jax import lax
from jax.experimental import pallas as pl
from jax.experimental.pallas import tpu as pltpu
from jax.sharding import Mesh
from jax.sharding import PartitionSpec as P

H = 32
KVH = 8
HD = 64
GROUP = H // KVH

epsilon = 1e-05
rope_base = 500000.0
masked_score = -1e30
f32 = jnp.float32
bf16 = jnp.bfloat16


def rotary_tables(positions, width):
    half_width = width // 2
    frequency = jnp.power(rope_base, -jnp.arange(half_width, dtype=f32) * 2.0 / width)
    angles = frequency[:, None] * positions.astype(f32)[None, :]
    return (jnp.cos(angles), jnp.sin(angles))


def rotate(vector, cosine, sine):
    half_width = vector.shape[-2] // 2
    first = vector[..., :half_width, :]
    second = vector[..., half_width:, :]
    return jnp.concatenate(
        [first * cosine - second * sine, second * cosine + first * sine], axis=-2
    )


def contract(left, right, left_dim, right_dim):
    return lax.dot_general(
        left, right, (((left_dim,), (right_dim,)), ((), ())), preferred_element_type=f32
    )


SLAB = ("xpart", "wshard")


def swap(value, flip):
    return lax.ppermute(value, SLAB, [(i, i ^ flip) for i in range(KVH)])


FLIPS = (0, 2, 4, 6, 1, 3, 5, 7)


def slab_gather(block, turns=False):
    rows = block.shape[0]
    half = rows // 2
    total = jnp.zeros((KVH * rows,) + block.shape[1:], block.dtype)

    def put(total, pieces):
        for index, piece in pieces:
            total = lax.dynamic_update_slice(total, piece, (index * half,) + (0,) * (block.ndim - 1))
        return total

    total = put(total, [(0, block)])
    row, column, other = yield [swap(block, 2), swap(block, 4), swap(block, 1)]
    total = put(total, [(2, row), (4, column), (8, other)])
    if turns:
        far, other_row, other_column = yield [swap(row, 4), swap(row, 1), swap(column, 1)]
        total = put(total, [(6, far), (10, other_row), (12, other_column)])
        far, total = yield [swap(far, 1), total]
        return put(total, [(14, far)])
    far_low, far_high, other_row, other_column = yield [
        swap(row[:half], 4),
        swap(column[half:], 2),
        swap(row, 1),
        swap(column, 1),
    ]
    total = put(total, [(6, far_low), (7, far_high), (10, other_row), (12, other_column)])
    far_low, far_high, total = yield [swap(far_low, 1), swap(far_high, 1), total]
    return put(total, [(14, far_low), (15, far_high)])


def slab_reduce(rows_of, rows):
    (got,) = yield [swap(rows_of(4 * rows, 8 * rows).astype(bf16), 1)]
    own = (rows_of(0, 4 * rows) + got.astype(f32)).reshape(4, rows, -1)
    half = own.shape[-1] // 2
    left, right = own[..., :half], own[..., half:]
    left_got, right_got = yield [
        swap(left[2:].astype(bf16), 4),
        swap(right[1::2].astype(bf16), 2),
    ]
    left = left[:2] + left_got.astype(f32)
    right = right[0::2] + right_got.astype(f32)
    left_got, right_got = yield [
        swap(left[1].astype(bf16), 2),
        swap(right[1].astype(bf16), 4),
    ]
    return jnp.concatenate(
        [left[0] + left_got.astype(f32), right[0] + right_got.astype(f32)], axis=1
    )


def alone(task):
    try:
        transfers = next(task)
        while True:
            transfers = task.send(transfers)
    except StopIteration as stop:
        return stop.value


def after(value, *others):
    return lax.optimization_barrier((value,) + others)[0]


def run_tasks(tasks, box):
    running, stage, last = {}, 0, ()
    tasks = list(tasks)
    while tasks or running:
        for entry in list(tasks):
            name, ready, make, *turn = entry
            if ready(stage, box) and turn in ([], [stage % 2]):
                tasks.remove(entry)
                running[name] = (make(last), None, turn)
        moving = {}
        for name, (task, got, turn) in list(running.items()):
            if turn in ([], [stage % 2]):
                try:
                    moving[name] = task.send(got)
                except StopIteration as stop:
                    del running[name]
                    box[name] = stop.value
        held = lax.optimization_barrier(tuple(v for values in moving.values() for v in values))
        last = held[:1] or last
        box["now"] = last
        box["stage", stage] = last
        done = 0
        for name, values in moving.items():
            task, unused, turn = running[name]
            running[name] = (task, held[done : done + len(values)], turn)
            done += len(values)
        stage += 1


def mix_kernel(names, block, flag_ref, *refs):
    refs = dict(zip(names, refs))

    def read(name):
        return refs[name][...].reshape(block)

    @pl.when(flag_ref[0] == 0)
    def middle():
        if "sum" in refs:
            refs["sum"][...] = (read("now").astype(f32) + read("got").astype(f32)).astype(bf16)
        if "outer" in refs and "kept" in refs:
            refs["outer"][...] = (read("kept").astype(f32) + read("across").astype(f32)).astype(
                bf16
            )
        if "own" in refs:
            refs["own"][...] = read("before")

    @pl.when(flag_ref[0] == 1)
    def end():
        if "outer" in refs and "next" in refs:
            refs["outer"][...] = read("next")
        if "own" in refs:
            refs["own"][...] = read("got")


def mix(outer, sources, arrays, results, block):
    at_end = {"now": 0, "next": 1, "got": None, "kept": 0, "across": 0, "before": 0}
    names, operands, specs = [], [], []
    for name in at_end:
        if name in sources:
            array, shape, index, blocks = sources[name]
        elif name in arrays:
            array, blocks = arrays[name]
            shape, index = block, lambda i: (i, 0)
        else:
            continue
        if name == "got" and "sum" not in results:
            used = 1
        elif name == "got" and "own" not in results:
            used = 0
        else:
            used = at_end[name]

        def where(i, flag, index=index, used=used, blocks=blocks):
            i = jnp.minimum(i, blocks - 1)
            return index(i if used is None else jnp.where(flag[0] == used, i, 0))

        names.append(name)
        operands.append(array)
        specs.append(pl.BlockSpec(shape, where))
    got = pl.pallas_call(
        functools.partial(mix_kernel, tuple(names) + tuple(results), block),
        grid_spec=pltpu.PrefetchScalarGridSpec(
            num_scalar_prefetch=1,
            grid=(max(results.values()),),
            in_specs=specs,
            out_specs=[
                pl.BlockSpec(block, lambda i, flag, blocks=blocks: (jnp.minimum(i, blocks - 1), 0))
                for blocks in results.values()
            ],
        ),
        out_shape=[
            jax.ShapeDtypeStruct((blocks * block[0], block[1]), bf16)
            for blocks in results.values()
        ],
        compiler_params=pltpu.CompilerParams(vmem_limit_bytes=32 * 1024 * 1024),
        cost_estimate=pl.CostEstimate(
            flops=0,
            transcendentals=0,
            bytes_accessed=10 * max(results.values()) * block[0] * block[1],
        ),
        name="mix",
    )(outer, *operands)
    return dict(zip(results, got))


def finish(tasks):
    results, running = [None] * len(tasks), dict(enumerate(tasks))
    while running:
        held = lax.optimization_barrier(
            tuple(value for task, sent in running.values() for value in sent)
        )
        done = 0
        for number, (task, sent) in list(running.items()):
            try:
                running[number] = (task, task.send(held[done : done + len(sent)]))
            except StopIteration as stop:
                del running[number]
                results[number] = stop.value
            done += len(sent)
    return results


def stream(chunks, placed, box, block):
    count, halves = lax.axis_size("line"), lax.axis_size("xpart")
    place, side = lax.axis_index("line"), lax.axis_index("xpart")
    sides = [lax.rem(side + halves - turn, halves) for turn in range(halves)]
    split = count == 4
    outer = jnp.logical_and(split, jnp.logical_or(place == 0, place == count - 1))
    outer = outer.astype(jnp.int32).reshape(1)
    inward, outward, across = [(0, 1), (3, 2)], [(1, 0), (2, 3)], [(1, 2), (2, 1)]
    last = len(chunks)
    sizes = [blocks for source, put, blocks in chunks]

    def is_chunk(number):
        return 0 <= number < last

    def chunk(number):
        return chunks[number][0]() + (sizes[number],)

    def first(number):
        return mix(
            outer * 0 + 1, {"next": chunk(number)}, {}, {"outer": sizes[number]}, block
        )

    sending, width = first(0)["outer"], sizes[0]
    sums, owns, fresh = {}, {}, []
    for stage in range(last + 3):
        moves = {}
        if not split:
            if is_chunk(stage):
                moves["all"] = lax.psum(first(stage)["outer"], "line")
        else:
            pairs = (inward if is_chunk(stage) else []) + (outward if is_chunk(stage - 2) else [])
            if pairs:
                moves["got"] = lax.ppermute(sending, "line", pairs)
            if is_chunk(stage - 1):
                moves["across"] = lax.ppermute(sums[stage - 1], "line", across)
        if is_chunk(stage - 3):
            for turn in range(1, halves):
                moves[turn] = lax.ppermute(
                    owns[stage - 3], "xpart", [(i, (i + turn) % halves) for i in range(halves)]
                )
        held = yield list(moves.values()) + [placed[key] for key in fresh]
        moves = dict(zip(moves, held))
        placed.update(zip(fresh, held[len(moves) :]))
        if split:
            sources, arrays, results = {}, {}, {}
            if is_chunk(stage):
                sources["now"] = chunk(stage)
                results["sum"] = sizes[stage]
            if is_chunk(stage + 1):
                sources["next"] = chunk(stage + 1)
            if is_chunk(stage - 1):
                arrays["kept"] = (sums.pop(stage - 1), sizes[stage - 1])
                arrays["across"] = (moves["across"], sizes[stage - 1])
            if is_chunk(stage + 1) or is_chunk(stage - 1):
                results["outer"] = max(sizes[n] for n in (stage - 1, stage + 1) if is_chunk(n))
            if is_chunk(stage - 2):
                arrays["before"] = (sending, sizes[stage - 2])
                results["own"] = sizes[stage - 2]
            if is_chunk(stage) or is_chunk(stage - 2):
                arrays["got"] = (moves["got"], width)
            if results:
                made = mix(outer, sources, arrays, results, block)
                sending, width = made.get("outer"), results.get("outer")
                if is_chunk(stage):
                    sums[stage] = made["sum"]
                if is_chunk(stage - 2):
                    owns[stage - 2] = made["own"]
                box["mixed"] = (next(iter(made.values())),)
        elif is_chunk(stage):
            owns[stage] = moves["all"]
        fresh = []
        if is_chunk(stage - 3):
            pieces = [owns.pop(stage - 3)] + [moves[turn] for turn in range(1, halves)]
            before = dict(placed)
            chunks[stage - 3][1](placed, pieces, sides)
            fresh = [key for key in placed if placed[key] is not before.get(key)]
    return None


def place_kernel(spots_ref, *refs):
    out_ref = refs[-1]
    halves = spots_ref.shape[0] - 1
    columns = refs[0].shape[-1]
    for turn in range(halves):
        for spot in range(halves):

            @pl.when(spots_ref[1 + turn] == spot)
            def put(turn=turn, spot=spot):
                out_ref[:, spot * columns : (spot + 1) * columns] = refs[turn][0].astype(f32)


def place_columns(total, pieces, spot, sides, count):
    shards, rows, columns = pieces[0].shape
    halves = len(pieces)
    operands = [jnp.stack([spot] + sides).astype(jnp.int32)] + list(pieces)
    specs = [pl.BlockSpec((1, rows, columns), lambda w, spots: (w, 0, 0))] * halves
    aliases = {}
    if total is not None:
        aliases = {len(operands): 0}
        operands.append(total)
        specs.append(pl.BlockSpec(memory_space=pl.ANY))
    return pl.pallas_call(
        place_kernel,
        grid_spec=pltpu.PrefetchScalarGridSpec(
            num_scalar_prefetch=1,
            grid=(shards,),
            in_specs=specs,
            out_specs=pl.BlockSpec((rows, halves * columns), lambda w, spots: (spots[0], w)),
        ),
        out_shape=jax.ShapeDtypeStruct((count * rows, shards * halves * columns), f32),
        input_output_aliases=aliases,
        compiler_params=pltpu.CompilerParams(vmem_limit_bytes=32 * 1024 * 1024),
        cost_estimate=pl.CostEstimate(
            flops=0, transcendentals=0, bytes_accessed=6 * halves * shards * rows * columns
        ),
        name="place_columns",
    )(*operands)


def blocks_kernel(sides_ref, *refs):
    out_ref = refs[-1]
    for turn in range(sides_ref.shape[0]):

        @pl.when(pl.program_id(0) == turn)
        def put(turn=turn):
            out_ref[...] = refs[turn][...].astype(f32)


def place_blocks(total, pieces, sides, shape, block, spot):
    halves = len(pieces)
    steps = pieces[0].shape[0] // block[0]

    def source(turn):
        def index(t, i, sides_ref):
            return (jnp.where(t == turn, i, jnp.where(t < turn, 0, steps - 1)), 0)

        return pl.BlockSpec(block, index)

    operands = [jnp.stack(sides).astype(jnp.int32)] + list(pieces)
    specs = [source(turn) for turn in range(halves)]
    aliases = {}
    if total is not None:
        aliases = {len(operands): 0}
        operands.append(total)
        specs.append(pl.BlockSpec(memory_space=pl.ANY))
    return pl.pallas_call(
        blocks_kernel,
        grid_spec=pltpu.PrefetchScalarGridSpec(
            num_scalar_prefetch=1,
            grid=(halves, steps),
            in_specs=specs,
            out_specs=pl.BlockSpec(block, lambda t, i, sides_ref: spot(sides_ref[t], i)),
        ),
        out_shape=jax.ShapeDtypeStruct(shape, f32),
        input_output_aliases=aliases,
        compiler_params=pltpu.CompilerParams(vmem_limit_bytes=32 * 1024 * 1024),
        cost_estimate=pl.CostEstimate(
            flops=0, transcendentals=0, bytes_accessed=6 * halves * pieces[0].size
        ),
        name="place_blocks",
    )(*operands)


def attn_kernel(deep, heads, sides_ref, *refs):
    *others, query_ref, key_ref, value_ref = refs
    halves = sides_ref.shape[0]
    pieces = others[:halves]
    across = pieces[0].shape[1] // 128
    kinds = heads // 128
    count = query_ref.shape[1] // heads
    first = lax.broadcasted_iota(jnp.int32, (1, 128), 1) < HD

    def square(order, number, kind, high):
        spot = ((number // halves) * (kinds + 1) + kind) * deep + high
        down, right = spot // across * 128, spot % across * 128
        piece = pieces[order[number % halves]]
        return piece[down : down + 128, right : right + 128].astype(f32)

    for turn in range(halves):

        @pl.when(sides_ref[0] == turn)
        def put(turn=turn):
            order = [(side + turn) % halves for side in range(halves)]
            for high in range(deep):
                rows = slice(high * 128, (high + 1) * 128)
                for number in range(count):
                    for kind in range(kinds):
                        left = number * heads + kind * 128
                        query_ref[rows, left : left + 128] = square(order, number, kind, high)
                for pair in range(count // 2):
                    even = square(order, 2 * pair, kinds, high)
                    odd = square(order, 2 * pair + 1, kinds, high)
                    here = slice(pair * 128, (pair + 1) * 128)
                    key_ref[rows, here] = jnp.where(first, even, pltpu.roll(odd, HD, 1))
                    value_ref[rows, here] = jnp.where(first, pltpu.roll(even, HD, 1), odd)


def place_attn(totals, pieces, spot, sides, size, heads, shards, count):
    halves = len(pieces)
    columns = [shards * halves * width for width in (heads, HD, HD)]
    operands = [jnp.stack(sides).astype(jnp.int32)] + list(pieces)
    specs = [pl.BlockSpec(memory_space=pltpu.VMEM)] * halves
    aliases = {}
    if totals is not None:
        aliases = {len(operands) + i: i for i in range(3)}
        operands += totals
        specs += [pl.BlockSpec(memory_space=pl.ANY)] * 3

    def kernel(sides_ref, *refs):
        attn_kernel(size // 128, heads, sides_ref, *refs[:halves], *refs[-3:])

    return pl.pallas_call(
        kernel,
        grid_spec=pltpu.PrefetchScalarGridSpec(
            num_scalar_prefetch=1,
            grid=(1,),
            in_specs=specs,
            out_specs=[
                pl.BlockSpec((size, width), lambda i, sides_ref: (spot, 0)) for width in columns
            ],
        ),
        out_shape=[jax.ShapeDtypeStruct((count * size, width), f32) for width in columns],
        input_output_aliases=aliases,
        compiler_params=pltpu.CompilerParams(vmem_limit_bytes=32 * 1024 * 1024),
        cost_estimate=pl.CostEstimate(
            flops=0, transcendentals=0, bytes_accessed=6 * size * sum(columns)
        ),
        name="place_attn",
    )(*operands)


def sum_everywhere(vector, stages):
    for unused in range(stages):
        yield []
    got = yield [swap(vector, flip) for flip in range(1, KVH)]
    vector = sum(got, vector)
    count = lax.axis_size("line")
    got = yield [
        lax.ppermute(vector, "line", [(i, (i + turn) % count) for i in range(count)])
        for turn in range(1, count)
    ]
    return sum(got, vector)


def move_spans(load, store, order_ref, tiles, span):
    lane = lax.broadcasted_iota(jnp.int32, (1, 2 * span), 1)

    def step(t, unused):
        first, second = order_ref[2 * t], order_ref[2 * t + 1]
        left = load(first // 2).astype(f32)
        right = load(second // 2).astype(f32)
        left = jnp.where(first % 2 == 1, pltpu.roll(left, span, 1), left)
        right = jnp.where(second % 2 == 0, pltpu.roll(right, span, 1), right)
        store(t, jnp.where(lane < span, left, right))
        return unused

    lax.fori_loop(0, tiles, step, 0, unroll=min(8, tiles))


def tile_at(index, tile):
    return pl.ds(pl.multiple_of(index * tile, tile), tile)


def rows_at(start, amount, align):
    return pl.ds(pl.multiple_of(start, align), amount)


def causal(scores, offset, other):
    key = lax.broadcasted_iota(jnp.int32, scores.shape, 0)
    query = lax.broadcasted_iota(jnp.int32, scores.shape, 1)
    return jnp.where(key <= query + offset, scores, other)


def forward_kernel(
    size, span, sort_ref, back_ref, range_ref, blocks_ref, out_ref, sorted_ref, float_ref, log_ref, keys_ref
):
    count, unused, width = blocks_ref.shape
    tile = 2 * span
    per = width // tile
    tiles = count * per

    def load(t):
        return blocks_ref[t // per, :, tile_at(t % per, tile)]

    def store(t, value):
        sorted_ref[:, tile_at(t, tile)] = value.astype(bf16)
        keys_ref[tile_at(t, tile), :] = jnp.transpose(value[HD : 2 * HD, :]).astype(bf16)

    move_spans(load, store, sort_ref, tiles, span)
    half = size // 2

    def query_block(i, unused):
        def part(start, amount, key_start, keys, carried, offset=None):
            accum, running_max, running_sum = carried
            there = rows_at(key_start, keys, size)
            queries = sorted_ref[0:HD, rows_at(start, amount, half)]
            scores = jnp.dot(keys_ref[there, :], queries, preferred_element_type=f32)
            if offset is not None:
                scores = causal(scores, offset, masked_score)
            new_max = jnp.maximum(running_max, jnp.max(scores, axis=0, keepdims=True))
            weights = jnp.exp(scores - new_max)
            shrink = jnp.exp(running_max - new_max)
            running_sum = running_sum * shrink + jnp.sum(weights, axis=0, keepdims=True)
            accum = accum * shrink + jnp.dot(
                sorted_ref[2 * HD : 3 * HD, there],
                weights.astype(bf16),
                preferred_element_type=f32,
            )
            return (accum, new_max, running_sum)

        carried = (
            jnp.zeros((HD, size), f32),
            jnp.full((1, size), masked_score, f32),
            jnp.zeros((1, size), f32),
        )
        first = i * size
        carried = lax.fori_loop(
            0, i, lambda j, carried: part(first, size, j * size, size, carried), carried
        )
        for side in range(2):
            start = first + side * half
            own = tuple(c[:, side * half : (side + 1) * half] for c in carried)
            accum, running_max, running_sum = part(
                start, half, first, (side + 1) * half, own, side * half
            )
            here = rows_at(start, half, half)
            float_ref[:, here] = accum / running_sum
            log_ref[:, here] = running_max + jnp.log(running_sum)
        return unused

    float_ref[...] = jnp.zeros_like(float_ref)
    log_ref[...] = jnp.zeros_like(log_ref)
    lax.fori_loop(range_ref[0], range_ref[1], query_block, 0)

    def store_back(t, value):
        out_ref[t // per, :, tile_at(t % per, tile)] = value.astype(bf16)

    move_spans(lambda t: float_ref[:, tile_at(t, tile)], store_back, back_ref, tiles, span)


def backward_kernel(
    size,
    span,
    sort_ref,
    back_ref,
    range_ref,
    sorted_ref,
    float_ref,
    log_ref,
    blocks_ref,
    out_ref,
    keys_ref,
    values_ref,
    given_ref,
    delta_ref,
    grads_ref,
):
    count, unused, width = blocks_ref.shape
    tile = 2 * span
    per = width // tile
    tiles = count * per

    def load(t):
        return blocks_ref[t // per, :, tile_at(t % per, tile)]

    def store(t, value):
        here = tile_at(t, tile)
        given_ref[:, here] = value.astype(bf16)
        delta_ref[:, here] = jnp.sum(value * float_ref[:, here], axis=0, keepdims=True)
        keys_ref[here, :] = jnp.transpose(sorted_ref[HD : 2 * HD, here].astype(f32)).astype(bf16)
        values_ref[here, :] = jnp.transpose(sorted_ref[2 * HD :, here].astype(f32)).astype(bf16)

    move_spans(load, store, sort_ref, tiles, span)
    half = size // 2
    grads_ref[...] = jnp.zeros_like(grads_ref)

    def key_block(j, unused):
        first_key = j * size
        there = rows_at(first_key, size, size)

        def part(start, amount, keys, carried, offset=None):
            key_acc, value_acc = carried
            here = rows_at(start, amount, half)
            near = rows_at(first_key, keys, size)
            queries = sorted_ref[0:HD, here]
            given = given_ref[:, here]
            scores = jnp.dot(keys_ref[near, :], queries, preferred_element_type=f32)
            probs = jnp.exp(scores - log_ref[:, here])
            if offset is not None:
                probs = causal(probs, offset, 0.0)
            probs_grad = jnp.dot(values_ref[near, :], given, preferred_element_type=f32)
            score_low = (probs * (probs_grad - delta_ref[:, here])).astype(bf16)
            value_acc = value_acc + contract(given, probs.astype(bf16), 1, 1)
            key_acc = key_acc + contract(queries, score_low, 1, 1)
            grads_ref[0:HD, here] += jnp.dot(
                sorted_ref[HD : 2 * HD, near], score_low, preferred_element_type=f32
            ) * (HD**-0.5)
            return (key_acc, value_acc)

        def diagonal(carried):
            near = part(first_key, half, half, tuple(c[:, :half] for c in carried), 0)
            carried = tuple(
                jnp.concatenate([n, c[:, half:]], axis=1) for n, c in zip(near, carried)
            )
            return part(first_key + half, half, size, carried, half)

        carried = (jnp.zeros((HD, size), f32), jnp.zeros((HD, size), f32))
        first, last = range_ref[0], range_ref[1]
        carried = lax.cond(
            jnp.logical_and(j >= first, j < last), diagonal, lambda c: c, carried
        )
        carried = lax.fori_loop(
            jnp.maximum(j + 1, first),
            last,
            lambda i, carried: part(i * size, size, size, carried),
            carried,
        )
        grads_ref[HD : 2 * HD, there] = carried[0]
        grads_ref[2 * HD :, there] = carried[1]
        return unused

    lax.fori_loop(0, range_ref[1], key_block, 0)

    def store_back(t, value):
        out_ref[t // per, :, tile_at(t % per, tile)] = value.astype(bf16)

    move_spans(lambda t: grads_ref[:, tile_at(t, tile)], store_back, back_ref, tiles, span)


def attend_forward(blocks, sort_order, back_order, query_range, span, size):
    count, unused, width = blocks.shape
    total = count * width
    smem = pl.BlockSpec(memory_space=pltpu.SMEM)
    vmem = pl.BlockSpec(memory_space=pltpu.VMEM)
    return pl.pallas_call(
        functools.partial(forward_kernel, size, span),
        out_shape=(
            jax.ShapeDtypeStruct((count, HD, width), bf16),
            jax.ShapeDtypeStruct((3 * HD, total), bf16),
            jax.ShapeDtypeStruct((HD, total), f32),
            jax.ShapeDtypeStruct((1, total), f32),
        ),
        in_specs=[smem, smem, smem, vmem],
        out_specs=(vmem, vmem, vmem, vmem),
        scratch_shapes=[pltpu.VMEM((total, HD), bf16)],
        compiler_params=pltpu.CompilerParams(vmem_limit_bytes=56 * 1024 * 1024),
        cost_estimate=pl.CostEstimate(
            flops=30 * 10**9, transcendentals=0, bytes_accessed=8 * 10**6
        ),
        name="attend_forward",
    )(sort_order, back_order, query_range, blocks)


def attend_backward(
    ordered, floats, logs, blocks, sort_order, back_order, query_range, span, size
):
    count, unused, width = blocks.shape
    total = count * width
    smem = pl.BlockSpec(memory_space=pltpu.SMEM)
    vmem = pl.BlockSpec(memory_space=pltpu.VMEM)
    return pl.pallas_call(
        functools.partial(backward_kernel, size, span),
        out_shape=jax.ShapeDtypeStruct((count, 3 * HD, width), bf16),
        in_specs=[smem, smem, smem, vmem, vmem, vmem, vmem],
        out_specs=vmem,
        scratch_shapes=[
            pltpu.VMEM((total, HD), bf16),
            pltpu.VMEM((total, HD), bf16),
            pltpu.VMEM((HD, total), bf16),
            pltpu.VMEM((1, total), f32),
            pltpu.VMEM((3 * HD, total), f32),
        ],
        compiler_params=pltpu.CompilerParams(vmem_limit_bytes=56 * 1024 * 1024),
        cost_estimate=pl.CostEstimate(
            flops=36 * 10**9, transcendentals=0, bytes_accessed=8 * 10**6
        ),
        name="attend_backward",
    )(sort_order, back_order, query_range, ordered, floats, logs, blocks)


def norm_parts(vector):
    inverse = lax.rsqrt(jnp.mean(vector * vector, axis=-1, keepdims=True) + epsilon)
    return inverse, vector * inverse


def norm_back(vector, scale_gain, gradient):
    inverse, normed = norm_parts(vector)
    gain_term = jnp.sum(gradient * normed, axis=0)
    scaled = gradient * scale_gain
    return (
        inverse * (scaled - normed * jnp.mean(scaled * normed, axis=-1, keepdims=True)),
        gain_term,
    )


def local(
    inputs,
    span_order,
    attn_gain,
    query_weight,
    key_weight,
    value_weight,
    output_weight,
    ffn_gain,
    gate_weight,
    up_weight,
    down_weight,
    cotangent,
):
    tok_dev, width = inputs.shape
    span = tok_dev // 2
    tokens = KVH * tok_dev
    line = lax.axis_size("line")
    halves = lax.axis_size("xpart")
    shards = lax.axis_size("wshard")
    place = lax.axis_index("line")
    side = lax.axis_index("xpart")
    slab_place = side * shards + lax.axis_index("wshard")
    copies = line // GROUP
    rows = width // shards

    flips = jnp.array(FLIPS, jnp.int32)
    devices = jnp.arange(line, dtype=jnp.int32)[:, None] * KVH + (flips ^ slab_place)[None, :]
    slots = (2 * devices[..., None] + jnp.arange(2, dtype=jnp.int32)).reshape(-1)
    spans = span_order.shape[0]
    numbers = jnp.arange(spans, dtype=jnp.int32)
    back_order = jnp.sum(
        jnp.where(slots[:, None] == numbers[None, :], span_order[None, :], 0), axis=1
    )
    sort_order = jnp.sum(
        jnp.where(back_order[None, :] == numbers[:, None], numbers[None, :], 0), axis=1
    )
    total = line * tokens
    size = min(1024, total // copies)
    blocks_each = total // size // copies
    first_block = (place // GROUP) * blocks_each
    query_range = jnp.stack([first_block, first_block + blocks_each]).astype(jnp.int32)
    slab_spans = lax.dynamic_slice_in_dim(back_order, place * 2 * KVH, 2 * KVH, 0)
    positions = (slab_spans[:, None] * span + jnp.arange(span, dtype=jnp.int32)).reshape(-1)
    cosine, sine = rotary_tables(positions, HD)

    shard = lax.axis_index("wshard")

    def pass_on(block, flip):
        return lax.ppermute(block, "wshard", [(i, i ^ flip) for i in range(shards)])

    def in_order(blocks):
        first = blocks[0]
        total = jnp.zeros((shards,) + first.shape, first.dtype)
        for flip, block in enumerate(blocks):
            total = lax.dynamic_update_slice(
                total, block[None], (shard ^ flip,) + (0,) * first.ndim
            )
        return total

    def side_columns(weight, flip):
        units = weight.shape[1] // KVH
        if units % 128 == 0 or halves == 1:
            start = ((shard ^ flip) * halves + side) * units
            return lax.dynamic_slice_in_dim(weight, start, units, 1)
        pair = lax.dynamic_slice_in_dim(weight, (shard ^ flip) * halves * units, halves * units, 1)
        return jnp.where(side == 0, pair[:, :units], pair[:, units:])

    heads = query_weight.shape[1] // KVH
    units = gate_weight.shape[1] // KVH

    def side_block(weights, flip):
        return jnp.concatenate([side_columns(weight, flip) for weight in weights], axis=1)

    box = {}

    def exchange(weights, flips):
        weights = after(weights, *box["now"])
        return [pass_on(side_block(weights, flip), flip) for flip in flips]

    near, middle, far = (1,), range(2, shards // 2 + 1), range(shards // 2 + 1, shards)
    near, middle, far = (
        [flip for flip in flips if flip < shards] for flips in (near, middle, far)
    )

    projections = (query_weight, key_weight, value_weight)
    ffn_weights = (gate_weight, up_weight)

    def weights_task():
        blocks = [side_block(projections, 0)]
        blocks += yield [pass_on(side_block(projections, flip), flip) for flip in near]
        gains = jnp.stack([attn_gain, ffn_gain])
        gains = after(gains, *box["now"])
        got = yield exchange(projections, middle) + [
            pass_on(gains, flip) for flip in range(1, shards)
        ]
        blocks += got[: len(middle)]
        gains = in_order([gains] + list(got[len(middle) :])).astype(f32)
        blocks += yield exchange(projections, far)
        attn_weight = in_order(blocks).reshape(width, -1)
        return (gains[:, 0].reshape(width), gains[:, 1].reshape(width), attn_weight)

    run_tasks(
        [
            ("inputs", lambda t, b: True, lambda last: slab_gather(inputs)),
            ("weights", lambda t, b: True, lambda last: weights_task()),
        ],
        box,
    )
    gain_one, gain_two, attn_weight = box["weights"]
    normed_one = (norm_parts(box["inputs"].astype(f32))[1] * gain_one).astype(bf16)

    own_down = lax.dynamic_slice_in_dim(down_weight, side * units, units, 0)

    projected = contract(attn_weight, normed_one, 0, 1)
    queries = rotate(projected[:heads].reshape(GROUP, HD, tokens), cosine, sine).astype(bf16)
    queries = queries * jnp.asarray(HD**-0.5, bf16)
    keys = rotate(projected[heads : heads + HD], cosine, sine).astype(bf16)
    values = projected[heads + HD :].astype(bf16)
    blocks = jnp.concatenate(
        [queries, jnp.broadcast_to(jnp.concatenate([keys, values]), (GROUP, 2 * HD, tokens))],
        axis=1,
    )
    blocks = lax.all_to_all(jnp.tile(blocks, (copies, 1, 1)), "line", 0, 0, tiled=True)
    def ffn_pass(flips, parts, *now):
        weights = after([ffn_weights[part] for part in parts], *now)
        return [
            (flip, part, pass_on(side_columns(weight, flip), flip))
            for part, weight in zip(parts, weights)
            for flip in flips
        ]

    def held(moves, *others):
        values = lax.optimization_barrier(tuple(value for f, p, value in moves) + others)
        return [(f, p, v) for (f, p, unused), v in zip(moves, values)], values[len(moves) :]

    gathering = slab_gather(after(cotangent, *box["now"]), True)
    first = next(gathering)
    ffn_moves = ffn_pass(near + middle, (0,), first[0])
    ffn_moves, (blocks, *first) = held(ffn_moves, blocks, *first)
    late_moves = ffn_pass(near + middle, (1,), ffn_moves[-1][2])
    second = gathering.send(first)
    attended, ordered, floats, logs = attend_forward(
        blocks, sort_order, back_order, query_range, span, size
    )

    def from_heads(blocks):
        got = lax.all_to_all(blocks, "line", 0, 0, tiled=True)
        return got.reshape((copies, GROUP) + got.shape[1:])

    def add_copies(got):
        return got[0] if copies == 1 else jnp.sum(got.astype(f32), axis=0).astype(bf16)

    own_output = lax.dynamic_slice_in_dim(output_weight, side * heads, heads, 0)
    late_moves, (attended, *second) = held(late_moves, attended, *second)
    ffn_moves += late_moves
    third = gathering.send(second)
    late_moves = ffn_pass(far, (0,), attended)

    def attended_task():
        (blocks,) = yield [from_heads(attended)]
        heads_out = add_copies(blocks).reshape(heads, tokens)
        added = yield from slab_reduce(
            lambda start, stop: contract(heads_out[:, start:stop], own_output, 0, 0), tok_dev
        )
        return (heads_out, inputs.astype(f32) + added)

    def rest_task():
        got = yield [v for f, p, v in late_moves] + third
        moves = [(f, p, v) for (f, p, unused), v in zip(late_moves, got)]
        try:
            gathering.send(got[len(late_moves) :])
        except StopIteration as stop:
            box["cotangent"] = stop.value
        more = ffn_pass(far, (1,), *box["now"])
        yield []
        got = yield [v for f, p, v in more]
        return moves + [(f, p, v) for (f, p, unused), v in zip(more, got)]

    run_tasks(
        [
            ("attended", lambda t, b: True, lambda last: attended_task()),
            ("moves", lambda t, b: True, lambda last: rest_task()),
        ],
        box,
    )
    attended, residual = box["attended"]
    slab_cotangent = box["cotangent"]

    ffn_full = jnp.zeros((shards, rows, 2 * units), bf16)
    moves = [(0, part, side_columns(ffn_weights[part], 0)) for part in range(2)]
    for flip, part, block in moves + ffn_moves + box["moves"]:
        ffn_full = lax.dynamic_update_slice(
            ffn_full, block[None], (shard ^ flip, 0, part * units)
        )
    ffn_full = ffn_full.reshape(width, 2 * units)

    normed_two = alone(
        slab_gather((norm_parts(residual)[1] * gain_two).astype(bf16))
    )
    hidden_grad = contract(slab_cotangent, own_down, 1, 1)
    normed_two, hidden_grad = lax.optimization_barrier((normed_two, hidden_grad))
    ffn_pre = contract(normed_two, ffn_full, 1, 0)
    gate_pre, up_pre = ffn_pre[:, :units], ffn_pre[:, units:]
    sigmoid_gate = jax.nn.sigmoid(gate_pre)
    hidden = (gate_pre * sigmoid_gate * up_pre).astype(bf16)
    down_parts = contract(hidden, slab_cotangent, 0, 0).astype(bf16)
    gate_low = (
        hidden_grad * up_pre * sigmoid_gate * (1.0 + gate_pre * (1.0 - sigmoid_gate))
    ).astype(bf16)
    up_low = (hidden_grad * gate_pre * sigmoid_gate).astype(bf16)

    def to_shards(partial):
        return lax.all_to_all(partial, "wshard", 0, 0, tiled=True)

    gate_partial = contract(normed_two, gate_low, 0, 0).astype(bf16).reshape(shards, rows, units)

    def attention_back(last):
        ffn_low = after(jnp.concatenate([gate_low, up_low], axis=1), gate_partial, *box.get("mixed", ()))
        normed_two_grad = yield from slab_reduce(
            lambda start, stop: contract(ffn_low[start:stop], ffn_full, 1, 1), tok_dev
        )
        residual_part, box["ffn_gain"] = norm_back(residual, gain_two, normed_two_grad)
        residual_grad = cotangent.astype(f32) + residual_part
        branch_low = yield from slab_gather(residual_grad.astype(bf16))
        attended_grad = contract(own_output, branch_low, 1, 1).astype(bf16)
        given = jnp.tile(attended_grad.reshape(GROUP, HD, tokens), (copies, 1, 1))
        (given,) = yield [lax.all_to_all(given, "line", 0, 0, tiled=True)]
        box["output_parts"] = contract(attended, branch_low, 1, 0).astype(bf16)
        raw = attend_backward(
            ordered, floats, logs, given, sort_order, back_order, query_range, span, size
        )
        raw, box["output_parts"] = yield [raw, box["output_parts"]]
        (pair_raw,) = yield [from_heads(raw[:, HD:])]
        (query_raw,) = yield [from_heads(after(raw[:, :HD], pair_raw))]
        query_low = rotate(add_copies(query_raw).astype(f32), cosine, -sine).astype(bf16)
        pair_raw = jnp.sum(pair_raw.astype(f32), axis=(0, 1))
        key_low = rotate(pair_raw[:HD], cosine, -sine).astype(bf16)
        value_low = pair_raw[HD:].astype(bf16)
        low = jnp.concatenate([query_low.reshape(heads, tokens), key_low, value_low], axis=0)
        attn_partial = contract(normed_one, low, 0, 1).astype(bf16)
        (box["attn"],) = yield [to_shards(attn_partial.reshape(shards, rows, -1))]
        normed_one_grad = yield from slab_reduce(
            lambda start, stop: contract(low[:, start:stop], attn_weight, 0, 1), tok_dev
        )
        input_part, attn_gain_term = norm_back(inputs.astype(f32), gain_one, normed_one_grad)
        input_grad = residual_grad + input_part
        return (input_grad, jnp.stack([attn_gain_term, box["ffn_gain"]]))

    half_rows = rows // 2

    def feed_forward_back(last):
        gate0 = to_shards(gate_partial[:, :half_rows])
        yield []
        up_partial = contract(normed_two, after(up_low, *box["now"]), 0, 0).astype(bf16)
        (up_partial,) = yield [up_partial.reshape(shards, rows, units)]
        box["gate0"], gate_now = yield [gate0, gate_partial]
        gate1 = to_shards(gate_now[:, half_rows:])
        yield []
        (box["gate1"],) = yield [gate1]
        yield []
        up_now = after(up_partial, *box["now"])
        (box["up0"],) = yield [to_shards(up_now[:, :half_rows])]
        up_now = after(up_partial, *box["now"])
        (box["up1"],) = yield [to_shards(up_now[:, half_rows:])]
        return None

    def feed_forward_out(last):
        low = after(hidden, *box["stage", 1])
        return (
            yield from slab_reduce(
                lambda start, stop: contract(low[start:stop], own_down, 1, 0), tok_dev
            )
        )

    half_width, half_units = width // 2, units // 2

    steps, block = 4, (half_units // 4, half_width)

    def down_chunk(c):
        high, right = c // 2, c % 2

        def source():
            return down_parts, block, lambda i: (high * steps + i, right)

        def put(placed, pieces, sides):
            placed["down"] = place_blocks(
                placed.get("down"),
                pieces,
                sides,
                (halves * units, width),
                (half_units // 2, half_width),
                lambda on, i: (on * 4 + high * 2 + i, right),
            )

        return (source, put, steps)

    def column_chunk(name, c):
        size = rows // 4
        each = shards // steps

        def source():
            return (
                box[name + str(c // 2)],
                (each, size, units),
                lambda i: (i, c % 2, 0),
            )

        def put(placed, pieces, sides):
            pieces = [piece.reshape(shards, size, units) for piece in pieces]
            placed[name] = place_columns(placed.get(name), pieces, c, sides, 4)

        return (source, put, steps)

    def output_chunk():
        def source():
            return box["output_parts"], block, lambda i: (i % 2, i // 2)

        def put(placed, pieces, sides):
            placed["output"] = place_blocks(
                placed.get("output"),
                pieces,
                sides,
                (halves * heads, width),
                (heads, half_width),
                lambda on, i: (on, i),
            )

        return (source, put, steps)

    def attn_chunk(c):
        size, columns = rows // 2, heads + 2 * HD
        deep, wide, across = size // 128, columns // 128, half_width // 128
        blocks = shards * deep * wide // across

        def source():
            part = box["attn"][:, c * size : (c + 1) * size]
            squares = [
                part[w, h * 128 : (h + 1) * 128, b * 128 : (b + 1) * 128]
                for w in range(shards)
                for b in range(wide)
                for h in range(deep)
            ]
            lines = [
                jnp.concatenate(squares[g * across : (g + 1) * across], axis=1)
                for g in range(blocks)
            ]
            return jnp.concatenate(lines, axis=0), block, lambda i: (i, 0)

        def put(placed, pieces, sides):
            names = ("query", "key", "value")
            totals = [placed[name] for name in names] if "query" in placed else None
            totals = place_attn(totals, pieces, c, sides, size, heads, shards, 2)
            placed.update(zip(names, totals))

        return (source, put, blocks)

    chunks = [down_chunk(c) for c in range(4)]
    chunks += [column_chunk(name, c) for name in ("gate", "up") for c in range(4)]
    chunks += [output_chunk()] + [attn_chunk(c) for c in range(2)]
    placed = {}
    gradients = stream(chunks, placed, box, block)
    sent = gradients.send(lax.optimization_barrier(tuple(next(gradients))))
    run_tasks(
        [
            ("attention", lambda t, b: True, attention_back),
            ("parts", lambda t, b: True, feed_forward_back),
        ],
        box,
    )
    run_tasks([("out", lambda t, b: True, feed_forward_out)], box)
    input_grad, gain_terms = box["attention"]
    gain_sums = sum_everywhere(gain_terms, len(chunks) - 1)
    gain_terms = finish([(gradients, sent), (gain_sums, next(gain_sums))])[1]
    gain_terms = lax.dynamic_slice_in_dim(gain_terms, shard * rows, rows, 1)
    return (
        (residual + box["out"]).astype(bf16),
        input_grad,
        gain_terms[0],
        placed["query"],
        placed["key"],
        placed["value"],
        placed["output"],
        gain_terms[1],
        placed["gate"],
        placed["up"],
        placed["down"],
    )


def solution(mesh):
    shards = mesh.shape["wshard"]
    halves = KVH // shards
    fine = Mesh(
        mesh.devices.reshape(mesh.shape["ctx"] // halves, halves, shards),
        ("line", "xpart", "wshard"),
    )
    every = ("line", "xpart", "wshard")
    in_specs = (
        P(every, None),
        P(),
        P("wshard"),
        P("wshard", None),
        P("wshard", None),
        P("wshard", None),
        P("wshard", None),
        P("wshard"),
        P("wshard", None),
        P("wshard", None),
        P("wshard", None),
        P(every, None),
    )
    out_specs = (
        P(every, None),
        P(every, None),
        P("wshard"),
        P("wshard", None),
        P("wshard", None),
        P("wshard", None),
        P("wshard", None),
        P("wshard"),
        P("wshard", None),
        P("wshard", None),
        P("wshard", None),
    )
    return jax.shard_map(local, mesh=fine, in_specs=in_specs, out_specs=out_specs, check_vma=False)
```

```python
import functools

import jax
import jax.numpy as jnp
from jax import lax
from jax.experimental import pallas as pl
from jax.experimental.pallas import tpu as pltpu
from jax.sharding import Mesh
from jax.sharding import PartitionSpec as P

H = 32
KVH = 8
HD = 64
GROUP = H // KVH

epsilon = 1e-05
rope_base = 500000.0
masked_score = -1e30
f32 = jnp.float32
bf16 = jnp.bfloat16


def rotary_tables(positions, width):
    half_width = width // 2
    frequency = jnp.power(rope_base, -jnp.arange(half_width, dtype=f32) * 2.0 / width)
    angles = frequency[:, None] * positions.astype(f32)[None, :]
    return (jnp.cos(angles), jnp.sin(angles))


def rotate(vector, cosine, sine):
    half_width = vector.shape[-2] // 2
    first = vector[..., :half_width, :]
    second = vector[..., half_width:, :]
    return jnp.concatenate(
        [first * cosine - second * sine, second * cosine + first * sine], axis=-2
    )


def contract(left, right, left_dim, right_dim):
    return lax.dot_general(
        left, right, (((left_dim,), (right_dim,)), ((), ())), preferred_element_type=f32
    )


SLAB = ("xpart", "wshard")


def swap(value, flip):
    return lax.ppermute(value, SLAB, [(i, i ^ flip) for i in range(KVH)])


FLIPS = (0, 2, 4, 6, 1, 3, 5, 7)


def slab_gather(block, turns=False):
    rows = block.shape[0]
    half = rows // 2
    total = jnp.zeros((KVH * rows,) + block.shape[1:], block.dtype)

    def put(total, pieces):
        for index, piece in pieces:
            total = lax.dynamic_update_slice(total, piece, (index * half,) + (0,) * (block.ndim - 1))
        return total

    total = put(total, [(0, block)])
    row, column, other = yield [swap(block, 2), swap(block, 4), swap(block, 1)]
    total = put(total, [(2, row), (4, column), (8, other)])
    if turns:
        far, other_row, other_column = yield [swap(row, 4), swap(row, 1), swap(column, 1)]
        total = put(total, [(6, far), (10, other_row), (12, other_column)])
        far, total = yield [swap(far, 1), total]
        return put(total, [(14, far)])
    far_low, far_high, other_row, other_column = yield [
        swap(row[:half], 4),
        swap(column[half:], 2),
        swap(row, 1),
        swap(column, 1),
    ]
    total = put(total, [(6, far_low), (7, far_high), (10, other_row), (12, other_column)])
    far_low, far_high, total = yield [swap(far_low, 1), swap(far_high, 1), total]
    return put(total, [(14, far_low), (15, far_high)])


def slab_reduce(rows_of, rows):
    (got,) = yield [swap(rows_of(4 * rows, 8 * rows).astype(bf16), 1)]
    own = (rows_of(0, 4 * rows) + got.astype(f32)).reshape(4, rows, -1)
    half = own.shape[-1] // 2
    left, right = own[..., :half], own[..., half:]
    left_got, right_got = yield [
        swap(left[2:].astype(bf16), 4),
        swap(right[1::2].astype(bf16), 2),
    ]
    left = left[:2] + left_got.astype(f32)
    right = right[0::2] + right_got.astype(f32)
    left_got, right_got = yield [
        swap(left[1].astype(bf16), 2),
        swap(right[1].astype(bf16), 4),
    ]
    return jnp.concatenate(
        [left[0] + left_got.astype(f32), right[0] + right_got.astype(f32)], axis=1
    )


def alone(task):
    try:
        transfers = next(task)
        while True:
            transfers = task.send(transfers)
    except StopIteration as stop:
        return stop.value


def after(value, *others):
    return lax.optimization_barrier((value,) + others)[0]


def run_tasks(tasks, box):
    running, stage, last = {}, 0, ()
    tasks = list(tasks)
    while tasks or running:
        for entry in list(tasks):
            name, ready, make, *turn = entry
            if ready(stage, box) and turn in ([], [stage % 2]):
                tasks.remove(entry)
                running[name] = (make(last), None, turn)
        moving = {}
        for name, (task, got, turn) in list(running.items()):
            if turn in ([], [stage % 2]):
                try:
                    moving[name] = task.send(got)
                except StopIteration as stop:
                    del running[name]
                    box[name] = stop.value
        held = lax.optimization_barrier(tuple(v for values in moving.values() for v in values))
        last = held[:1] or last
        box["now"] = last
        box["stage", stage] = last
        done = 0
        for name, values in moving.items():
            task, unused, turn = running[name]
            running[name] = (task, held[done : done + len(values)], turn)
            done += len(values)
        stage += 1


def mix_kernel(names, block, flag_ref, *refs):
    refs = dict(zip(names, refs))

    def read(name):
        return refs[name][...].reshape(block)

    @pl.when(flag_ref[0] == 0)
    def middle():
        if "sum" in refs:
            refs["sum"][...] = (read("now").astype(f32) + read("got").astype(f32)).astype(bf16)
        if "outer" in refs and "kept" in refs:
            refs["outer"][...] = (read("kept").astype(f32) + read("across").astype(f32)).astype(
                bf16
            )
        if "own" in refs:
            refs["own"][...] = read("before")

    @pl.when(flag_ref[0] == 1)
    def end():
        if "outer" in refs and "next" in refs:
            refs["outer"][...] = read("next")
        if "own" in refs:
            refs["own"][...] = read("got")


def mix(outer, sources, arrays, results, block):
    at_end = {"now": 0, "next": 1, "got": None, "kept": 0, "across": 0, "before": 0}
    names, operands, specs = [], [], []
    for name in at_end:
        if name in sources:
            array, shape, index, blocks = sources[name]
        elif name in arrays:
            array, blocks = arrays[name]
            shape, index = block, lambda i: (i, 0)
        else:
            continue
        if name == "got" and "sum" not in results:
            used = 1
        elif name == "got" and "own" not in results:
            used = 0
        else:
            used = at_end[name]

        def where(i, flag, index=index, used=used, blocks=blocks):
            i = jnp.minimum(i, blocks - 1)
            return index(i if used is None else jnp.where(flag[0] == used, i, 0))

        names.append(name)
        operands.append(array)
        specs.append(pl.BlockSpec(shape, where))
    got = pl.pallas_call(
        functools.partial(mix_kernel, tuple(names) + tuple(results), block),
        grid_spec=pltpu.PrefetchScalarGridSpec(
            num_scalar_prefetch=1,
            grid=(max(results.values()),),
            in_specs=specs,
            out_specs=[
                pl.BlockSpec(block, lambda i, flag, blocks=blocks: (jnp.minimum(i, blocks - 1), 0))
                for blocks in results.values()
            ],
        ),
        out_shape=[
            jax.ShapeDtypeStruct((blocks * block[0], block[1]), bf16)
            for blocks in results.values()
        ],
        compiler_params=pltpu.CompilerParams(vmem_limit_bytes=32 * 1024 * 1024),
        cost_estimate=pl.CostEstimate(
            flops=0,
            transcendentals=0,
            bytes_accessed=10 * max(results.values()) * block[0] * block[1],
        ),
        name="mix",
    )(outer, *operands)
    return dict(zip(results, got))


def finish(tasks):
    results, running = [None] * len(tasks), dict(enumerate(tasks))
    while running:
        held = lax.optimization_barrier(
            tuple(value for task, sent in running.values() for value in sent)
        )
        done = 0
        for number, (task, sent) in list(running.items()):
            try:
                running[number] = (task, task.send(held[done : done + len(sent)]))
            except StopIteration as stop:
                del running[number]
                results[number] = stop.value
            done += len(sent)
    return results


def stream(chunks, placed, box, block):
    count, halves = lax.axis_size("line"), lax.axis_size("xpart")
    place, side = lax.axis_index("line"), lax.axis_index("xpart")
    sides = [lax.rem(side + halves - turn, halves) for turn in range(halves)]
    split = count == 4
    outer = jnp.logical_and(split, jnp.logical_or(place == 0, place == count - 1))
    outer = outer.astype(jnp.int32).reshape(1)
    inward, outward, across = [(0, 1), (3, 2)], [(1, 0), (2, 3)], [(1, 2), (2, 1)]
    last = len(chunks)
    sizes = [blocks for source, put, blocks in chunks]

    def is_chunk(number):
        return 0 <= number < last

    def chunk(number):
        return chunks[number][0]() + (sizes[number],)

    def first(number):
        return mix(
            outer * 0 + 1, {"next": chunk(number)}, {}, {"outer": sizes[number]}, block
        )

    sending, width = first(0)["outer"], sizes[0]
    sums, owns, fresh = {}, {}, []
    for stage in range(last + 3):
        moves = {}
        if not split:
            if is_chunk(stage):
                moves["all"] = lax.psum(first(stage)["outer"], "line")
        else:
            pairs = (inward if is_chunk(stage) else []) + (outward if is_chunk(stage - 2) else [])
            if pairs:
                moves["got"] = lax.ppermute(sending, "line", pairs)
            if is_chunk(stage - 1):
                moves["across"] = lax.ppermute(sums[stage - 1], "line", across)
        if is_chunk(stage - 3):
            for turn in range(1, halves):
                moves[turn] = lax.ppermute(
                    owns[stage - 3], "xpart", [(i, (i + turn) % halves) for i in range(halves)]
                )
        held = yield list(moves.values()) + [placed[key] for key in fresh]
        moves = dict(zip(moves, held))
        placed.update(zip(fresh, held[len(moves) :]))
        if split:
            sources, arrays, results = {}, {}, {}
            if is_chunk(stage):
                sources["now"] = chunk(stage)
                results["sum"] = sizes[stage]
            if is_chunk(stage + 1):
                sources["next"] = chunk(stage + 1)
            if is_chunk(stage - 1):
                arrays["kept"] = (sums.pop(stage - 1), sizes[stage - 1])
                arrays["across"] = (moves["across"], sizes[stage - 1])
            if is_chunk(stage + 1) or is_chunk(stage - 1):
                results["outer"] = max(sizes[n] for n in (stage - 1, stage + 1) if is_chunk(n))
            if is_chunk(stage - 2):
                arrays["before"] = (sending, sizes[stage - 2])
                results["own"] = sizes[stage - 2]
            if is_chunk(stage) or is_chunk(stage - 2):
                arrays["got"] = (moves["got"], width)
            if results:
                made = mix(outer, sources, arrays, results, block)
                sending, width = made.get("outer"), results.get("outer")
                if is_chunk(stage):
                    sums[stage] = made["sum"]
                if is_chunk(stage - 2):
                    owns[stage - 2] = made["own"]
                box["mixed"] = (next(iter(made.values())),)
        elif is_chunk(stage):
            owns[stage] = moves["all"]
        fresh = []
        if is_chunk(stage - 3):
            pieces = [owns.pop(stage - 3)] + [moves[turn] for turn in range(1, halves)]
            before = dict(placed)
            chunks[stage - 3][1](placed, pieces, sides)
            fresh = [key for key in placed if placed[key] is not before.get(key)]
    return None


def place_kernel(spots_ref, *refs):
    out_ref = refs[-1]
    halves = spots_ref.shape[0] - 1
    columns = refs[0].shape[-1]
    for turn in range(halves):
        for spot in range(halves):

            @pl.when(spots_ref[1 + turn] == spot)
            def put(turn=turn, spot=spot):
                out_ref[:, spot * columns : (spot + 1) * columns] = refs[turn][0].astype(f32)


def place_columns(total, pieces, spot, sides, count):
    shards, rows, columns = pieces[0].shape
    halves = len(pieces)
    operands = [jnp.stack([spot] + sides).astype(jnp.int32)] + list(pieces)
    specs = [pl.BlockSpec((1, rows, columns), lambda w, spots: (w, 0, 0))] * halves
    aliases = {}
    if total is not None:
        aliases = {len(operands): 0}
        operands.append(total)
        specs.append(pl.BlockSpec(memory_space=pl.ANY))
    return pl.pallas_call(
        place_kernel,
        grid_spec=pltpu.PrefetchScalarGridSpec(
            num_scalar_prefetch=1,
            grid=(shards,),
            in_specs=specs,
            out_specs=pl.BlockSpec((rows, halves * columns), lambda w, spots: (spots[0], w)),
        ),
        out_shape=jax.ShapeDtypeStruct((count * rows, shards * halves * columns), f32),
        input_output_aliases=aliases,
        compiler_params=pltpu.CompilerParams(vmem_limit_bytes=32 * 1024 * 1024),
        cost_estimate=pl.CostEstimate(
            flops=0, transcendentals=0, bytes_accessed=6 * halves * shards * rows * columns
        ),
        name="place_columns",
    )(*operands)


def blocks_kernel(sides_ref, *refs):
    out_ref = refs[-1]
    for turn in range(sides_ref.shape[0]):

        @pl.when(pl.program_id(0) == turn)
        def put(turn=turn):
            out_ref[...] = refs[turn][...].astype(f32)


def place_blocks(total, pieces, sides, shape, block, spot):
    halves = len(pieces)
    steps = pieces[0].shape[0] // block[0]

    def source(turn):
        def index(t, i, sides_ref):
            return (jnp.where(t == turn, i, jnp.where(t < turn, 0, steps - 1)), 0)

        return pl.BlockSpec(block, index)

    operands = [jnp.stack(sides).astype(jnp.int32)] + list(pieces)
    specs = [source(turn) for turn in range(halves)]
    aliases = {}
    if total is not None:
        aliases = {len(operands): 0}
        operands.append(total)
        specs.append(pl.BlockSpec(memory_space=pl.ANY))
    return pl.pallas_call(
        blocks_kernel,
        grid_spec=pltpu.PrefetchScalarGridSpec(
            num_scalar_prefetch=1,
            grid=(halves, steps),
            in_specs=specs,
            out_specs=pl.BlockSpec(block, lambda t, i, sides_ref: spot(sides_ref[t], i)),
        ),
        out_shape=jax.ShapeDtypeStruct(shape, f32),
        input_output_aliases=aliases,
        compiler_params=pltpu.CompilerParams(vmem_limit_bytes=32 * 1024 * 1024),
        cost_estimate=pl.CostEstimate(
            flops=0, transcendentals=0, bytes_accessed=6 * halves * pieces[0].size
        ),
        name="place_blocks",
    )(*operands)


def attn_kernel(deep, heads, sides_ref, *refs):
    *others, query_ref, key_ref, value_ref = refs
    halves = sides_ref.shape[0]
    pieces = others[:halves]
    across = pieces[0].shape[1] // 128
    kinds = heads // 128
    count = query_ref.shape[1] // heads
    first = lax.broadcasted_iota(jnp.int32, (1, 128), 1) < HD

    def square(order, number, kind, high):
        spot = ((number // halves) * (kinds + 1) + kind) * deep + high
        down, right = spot // across * 128, spot % across * 128
        piece = pieces[order[number % halves]]
        return piece[down : down + 128, right : right + 128].astype(f32)

    for turn in range(halves):

        @pl.when(sides_ref[0] == turn)
        def put(turn=turn):
            order = [(side + turn) % halves for side in range(halves)]
            for high in range(deep):
                rows = slice(high * 128, (high + 1) * 128)
                for number in range(count):
                    for kind in range(kinds):
                        left = number * heads + kind * 128
                        query_ref[rows, left : left + 128] = square(order, number, kind, high)
                for pair in range(count // 2):
                    even = square(order, 2 * pair, kinds, high)
                    odd = square(order, 2 * pair + 1, kinds, high)
                    here = slice(pair * 128, (pair + 1) * 128)
                    key_ref[rows, here] = jnp.where(first, even, pltpu.roll(odd, HD, 1))
                    value_ref[rows, here] = jnp.where(first, pltpu.roll(even, HD, 1), odd)


def place_attn(totals, pieces, spot, sides, size, heads, shards, count):
    halves = len(pieces)
    columns = [shards * halves * width for width in (heads, HD, HD)]
    operands = [jnp.stack(sides).astype(jnp.int32)] + list(pieces)
    specs = [pl.BlockSpec(memory_space=pltpu.VMEM)] * halves
    aliases = {}
    if totals is not None:
        aliases = {len(operands) + i: i for i in range(3)}
        operands += totals
        specs += [pl.BlockSpec(memory_space=pl.ANY)] * 3

    def kernel(sides_ref, *refs):
        attn_kernel(size // 128, heads, sides_ref, *refs[:halves], *refs[-3:])

    return pl.pallas_call(
        kernel,
        grid_spec=pltpu.PrefetchScalarGridSpec(
            num_scalar_prefetch=1,
            grid=(1,),
            in_specs=specs,
            out_specs=[
                pl.BlockSpec((size, width), lambda i, sides_ref: (spot, 0)) for width in columns
            ],
        ),
        out_shape=[jax.ShapeDtypeStruct((count * size, width), f32) for width in columns],
        input_output_aliases=aliases,
        compiler_params=pltpu.CompilerParams(vmem_limit_bytes=32 * 1024 * 1024),
        cost_estimate=pl.CostEstimate(
            flops=0, transcendentals=0, bytes_accessed=6 * size * sum(columns)
        ),
        name="place_attn",
    )(*operands)


def sum_everywhere(vector, stages):
    for unused in range(stages):
        yield []
    got = yield [swap(vector, flip) for flip in range(1, KVH)]
    vector = sum(got, vector)
    count = lax.axis_size("line")
    got = yield [
        lax.ppermute(vector, "line", [(i, (i + turn) % count) for i in range(count)])
        for turn in range(1, count)
    ]
    return sum(got, vector)


def move_spans(load, store, order_ref, tiles, span):
    lane = lax.broadcasted_iota(jnp.int32, (1, 2 * span), 1)

    def step(t, unused):
        first, second = order_ref[2 * t], order_ref[2 * t + 1]
        left = load(first // 2).astype(f32)
        right = load(second // 2).astype(f32)
        left = jnp.where(first % 2 == 1, pltpu.roll(left, span, 1), left)
        right = jnp.where(second % 2 == 0, pltpu.roll(right, span, 1), right)
        store(t, jnp.where(lane < span, left, right))
        return unused

    lax.fori_loop(0, tiles, step, 0, unroll=min(8, tiles))


def tile_at(index, tile):
    return pl.ds(pl.multiple_of(index * tile, tile), tile)


def rows_at(start, amount, align):
    return pl.ds(pl.multiple_of(start, align), amount)


def causal(scores, offset, other):
    key = lax.broadcasted_iota(jnp.int32, scores.shape, 0)
    query = lax.broadcasted_iota(jnp.int32, scores.shape, 1)
    return jnp.where(key <= query + offset, scores, other)


def forward_kernel(
    size, span, sort_ref, back_ref, range_ref, blocks_ref, out_ref, sorted_ref, float_ref, log_ref, keys_ref
):
    count, unused, width = blocks_ref.shape
    tile = 2 * span
    per = width // tile
    tiles = count * per

    def load(t):
        return blocks_ref[t // per, :, tile_at(t % per, tile)]

    def store(t, value):
        sorted_ref[:, tile_at(t, tile)] = value.astype(bf16)
        keys_ref[tile_at(t, tile), :] = jnp.transpose(value[HD : 2 * HD, :]).astype(bf16)

    move_spans(load, store, sort_ref, tiles, span)
    half = size // 2

    def query_block(i, unused):
        def part(start, amount, key_start, keys, carried, offset=None):
            accum, running_max, running_sum = carried
            there = rows_at(key_start, keys, size)
            queries = sorted_ref[0:HD, rows_at(start, amount, half)]
            scores = jnp.dot(keys_ref[there, :], queries, preferred_element_type=f32)
            if offset is not None:
                scores = causal(scores, offset, masked_score)
            new_max = jnp.maximum(running_max, jnp.max(scores, axis=0, keepdims=True))
            weights = jnp.exp(scores - new_max)
            shrink = jnp.exp(running_max - new_max)
            running_sum = running_sum * shrink + jnp.sum(weights, axis=0, keepdims=True)
            accum = accum * shrink + jnp.dot(
                sorted_ref[2 * HD : 3 * HD, there],
                weights.astype(bf16),
                preferred_element_type=f32,
            )
            return (accum, new_max, running_sum)

        carried = (
            jnp.zeros((HD, size), f32),
            jnp.full((1, size), masked_score, f32),
            jnp.zeros((1, size), f32),
        )
        first = i * size
        carried = lax.fori_loop(
            0, i, lambda j, carried: part(first, size, j * size, size, carried), carried
        )
        for side in range(2):
            start = first + side * half
            own = tuple(c[:, side * half : (side + 1) * half] for c in carried)
            accum, running_max, running_sum = part(
                start, half, first, (side + 1) * half, own, side * half
            )
            here = rows_at(start, half, half)
            float_ref[:, here] = accum / running_sum
            log_ref[:, here] = running_max + jnp.log(running_sum)
        return unused

    float_ref[...] = jnp.zeros_like(float_ref)
    log_ref[...] = jnp.zeros_like(log_ref)
    lax.fori_loop(range_ref[0], range_ref[1], query_block, 0)

    def store_back(t, value):
        out_ref[t // per, :, tile_at(t % per, tile)] = value.astype(bf16)

    move_spans(lambda t: float_ref[:, tile_at(t, tile)], store_back, back_ref, tiles, span)


def backward_kernel(
    size,
    span,
    sort_ref,
    back_ref,
    range_ref,
    sorted_ref,
    float_ref,
    log_ref,
    blocks_ref,
    out_ref,
    keys_ref,
    values_ref,
    given_ref,
    delta_ref,
    grads_ref,
):
    count, unused, width = blocks_ref.shape
    tile = 2 * span
    per = width // tile
    tiles = count * per

    def load(t):
        return blocks_ref[t // per, :, tile_at(t % per, tile)]

    def store(t, value):
        here = tile_at(t, tile)
        given_ref[:, here] = value.astype(bf16)
        delta_ref[:, here] = jnp.sum(value * float_ref[:, here], axis=0, keepdims=True)
        keys_ref[here, :] = jnp.transpose(sorted_ref[HD : 2 * HD, here].astype(f32)).astype(bf16)
        values_ref[here, :] = jnp.transpose(sorted_ref[2 * HD :, here].astype(f32)).astype(bf16)

    move_spans(load, store, sort_ref, tiles, span)
    half = size // 2
    grads_ref[...] = jnp.zeros_like(grads_ref)

    def key_block(j, unused):
        first_key = j * size
        there = rows_at(first_key, size, size)

        def part(start, amount, keys, carried, offset=None):
            key_acc, value_acc = carried
            here = rows_at(start, amount, half)
            near = rows_at(first_key, keys, size)
            queries = sorted_ref[0:HD, here]
            given = given_ref[:, here]
            scores = jnp.dot(keys_ref[near, :], queries, preferred_element_type=f32)
            probs = jnp.exp(scores - log_ref[:, here])
            if offset is not None:
                probs = causal(probs, offset, 0.0)
            probs_grad = jnp.dot(values_ref[near, :], given, preferred_element_type=f32)
            score_low = (probs * (probs_grad - delta_ref[:, here])).astype(bf16)
            value_acc = value_acc + contract(given, probs.astype(bf16), 1, 1)
            key_acc = key_acc + contract(queries, score_low, 1, 1)
            grads_ref[0:HD, here] += jnp.dot(
                sorted_ref[HD : 2 * HD, near], score_low, preferred_element_type=f32
            ) * (HD**-0.5)
            return (key_acc, value_acc)

        def diagonal(carried):
            near = part(first_key, half, half, tuple(c[:, :half] for c in carried), 0)
            carried = tuple(
                jnp.concatenate([n, c[:, half:]], axis=1) for n, c in zip(near, carried)
            )
            return part(first_key + half, half, size, carried, half)

        carried = (jnp.zeros((HD, size), f32), jnp.zeros((HD, size), f32))
        first, last = range_ref[0], range_ref[1]
        carried = lax.cond(
            jnp.logical_and(j >= first, j < last), diagonal, lambda c: c, carried
        )
        carried = lax.fori_loop(
            jnp.maximum(j + 1, first),
            last,
            lambda i, carried: part(i * size, size, size, carried),
            carried,
        )
        grads_ref[HD : 2 * HD, there] = carried[0]
        grads_ref[2 * HD :, there] = carried[1]
        return unused

    lax.fori_loop(0, range_ref[1], key_block, 0)

    def store_back(t, value):
        out_ref[t // per, :, tile_at(t % per, tile)] = value.astype(bf16)

    move_spans(lambda t: grads_ref[:, tile_at(t, tile)], store_back, back_ref, tiles, span)


def attend_forward(blocks, sort_order, back_order, query_range, span, size):
    count, unused, width = blocks.shape
    total = count * width
    smem = pl.BlockSpec(memory_space=pltpu.SMEM)
    vmem = pl.BlockSpec(memory_space=pltpu.VMEM)
    return pl.pallas_call(
        functools.partial(forward_kernel, size, span),
        out_shape=(
            jax.ShapeDtypeStruct((count, HD, width), bf16),
            jax.ShapeDtypeStruct((3 * HD, total), bf16),
            jax.ShapeDtypeStruct((HD, total), f32),
            jax.ShapeDtypeStruct((1, total), f32),
        ),
        in_specs=[smem, smem, smem, vmem],
        out_specs=(vmem, vmem, vmem, vmem),
        scratch_shapes=[pltpu.VMEM((total, HD), bf16)],
        compiler_params=pltpu.CompilerParams(vmem_limit_bytes=56 * 1024 * 1024),
        cost_estimate=pl.CostEstimate(
            flops=30 * 10**9, transcendentals=0, bytes_accessed=8 * 10**6
        ),
        name="attend_forward",
    )(sort_order, back_order, query_range, blocks)


def attend_backward(
    ordered, floats, logs, blocks, sort_order, back_order, query_range, span, size
):
    count, unused, width = blocks.shape
    total = count * width
    smem = pl.BlockSpec(memory_space=pltpu.SMEM)
    vmem = pl.BlockSpec(memory_space=pltpu.VMEM)
    return pl.pallas_call(
        functools.partial(backward_kernel, size, span),
        out_shape=jax.ShapeDtypeStruct((count, 3 * HD, width), bf16),
        in_specs=[smem, smem, smem, vmem, vmem, vmem, vmem],
        out_specs=vmem,
        scratch_shapes=[
            pltpu.VMEM((total, HD), bf16),
            pltpu.VMEM((total, HD), bf16),
            pltpu.VMEM((HD, total), bf16),
            pltpu.VMEM((1, total), f32),
            pltpu.VMEM((3 * HD, total), f32),
        ],
        compiler_params=pltpu.CompilerParams(vmem_limit_bytes=56 * 1024 * 1024),
        cost_estimate=pl.CostEstimate(
            flops=36 * 10**9, transcendentals=0, bytes_accessed=8 * 10**6
        ),
        name="attend_backward",
    )(sort_order, back_order, query_range, ordered, floats, logs, blocks)


def norm_parts(vector):
    inverse = lax.rsqrt(jnp.mean(vector * vector, axis=-1, keepdims=True) + epsilon)
    return inverse, vector * inverse


def norm_back(vector, scale_gain, gradient):
    inverse, normed = norm_parts(vector)
    gain_term = jnp.sum(gradient * normed, axis=0)
    scaled = gradient * scale_gain
    return (
        inverse * (scaled - normed * jnp.mean(scaled * normed, axis=-1, keepdims=True)),
        gain_term,
    )


def local(
    inputs,
    span_order,
    attn_gain,
    query_weight,
    key_weight,
    value_weight,
    output_weight,
    ffn_gain,
    gate_weight,
    up_weight,
    down_weight,
    cotangent,
):
    tok_dev, width = inputs.shape
    span = tok_dev // 2
    tokens = KVH * tok_dev
    line = lax.axis_size("line")
    halves = lax.axis_size("xpart")
    shards = lax.axis_size("wshard")
    place = lax.axis_index("line")
    side = lax.axis_index("xpart")
    slab_place = side * shards + lax.axis_index("wshard")
    copies = line // GROUP
    rows = width // shards

    flips = jnp.array(FLIPS, jnp.int32)
    devices = jnp.arange(line, dtype=jnp.int32)[:, None] * KVH + (flips ^ slab_place)[None, :]
    slots = (2 * devices[..., None] + jnp.arange(2, dtype=jnp.int32)).reshape(-1)
    spans = span_order.shape[0]
    numbers = jnp.arange(spans, dtype=jnp.int32)
    back_order = jnp.sum(
        jnp.where(slots[:, None] == numbers[None, :], span_order[None, :], 0), axis=1
    )
    sort_order = jnp.sum(
        jnp.where(back_order[None, :] == numbers[:, None], numbers[None, :], 0), axis=1
    )
    total = line * tokens
    size = min(1024, total // copies)
    blocks_each = total // size // copies
    first_block = (place // GROUP) * blocks_each
    query_range = jnp.stack([first_block, first_block + blocks_each]).astype(jnp.int32)
    slab_spans = lax.dynamic_slice_in_dim(back_order, place * 2 * KVH, 2 * KVH, 0)
    positions = (slab_spans[:, None] * span + jnp.arange(span, dtype=jnp.int32)).reshape(-1)
    cosine, sine = rotary_tables(positions, HD)

    shard = lax.axis_index("wshard")

    def pass_on(block, flip):
        return lax.ppermute(block, "wshard", [(i, i ^ flip) for i in range(shards)])

    def in_order(blocks):
        first = blocks[0]
        total = jnp.zeros((shards,) + first.shape, first.dtype)
        for flip, block in enumerate(blocks):
            total = lax.dynamic_update_slice(
                total, block[None], (shard ^ flip,) + (0,) * first.ndim
            )
        return total

    def side_columns(weight, flip):
        units = weight.shape[1] // KVH
        if units % 128 == 0 or halves == 1:
            start = ((shard ^ flip) * halves + side) * units
            return lax.dynamic_slice_in_dim(weight, start, units, 1)
        pair = lax.dynamic_slice_in_dim(weight, (shard ^ flip) * halves * units, halves * units, 1)
        return jnp.where(side == 0, pair[:, :units], pair[:, units:])

    heads = query_weight.shape[1] // KVH
    units = gate_weight.shape[1] // KVH

    def side_block(weights, flip):
        return jnp.concatenate([side_columns(weight, flip) for weight in weights], axis=1)

    box = {}

    def exchange(weights, flips):
        weights = after(weights, *box["now"])
        return [pass_on(side_block(weights, flip), flip) for flip in flips]

    near, middle, far = (1,), range(2, shards // 2 + 1), range(shards // 2 + 1, shards)
    near, middle, far = (
        [flip for flip in flips if flip < shards] for flips in (near, middle, far)
    )

    projections = (query_weight, key_weight, value_weight)
    ffn_weights = (gate_weight, up_weight)

    def weights_task():
        blocks = [side_block(projections, 0)]
        blocks += yield [pass_on(side_block(projections, flip), flip) for flip in near]
        gains = jnp.stack([attn_gain, ffn_gain])
        gains = after(gains, *box["now"])
        got = yield exchange(projections, middle) + [
            pass_on(gains, flip) for flip in range(1, shards)
        ]
        blocks += got[: len(middle)]
        gains = in_order([gains] + list(got[len(middle) :])).astype(f32)
        blocks += yield exchange(projections, far)
        attn_weight = in_order(blocks).reshape(width, -1)
        return (gains[:, 0].reshape(width), gains[:, 1].reshape(width), attn_weight)

    run_tasks(
        [
            ("inputs", lambda t, b: True, lambda last: slab_gather(inputs)),
            ("weights", lambda t, b: True, lambda last: weights_task()),
        ],
        box,
    )
    gain_one, gain_two, attn_weight = box["weights"]
    normed_one = (norm_parts(box["inputs"].astype(f32))[1] * gain_one).astype(bf16)

    own_down = lax.dynamic_slice_in_dim(down_weight, side * units, units, 0)

    projected = contract(attn_weight, normed_one, 0, 1)
    queries = rotate(projected[:heads].reshape(GROUP, HD, tokens), cosine, sine).astype(bf16)
    queries = queries * jnp.asarray(HD**-0.5, bf16)
    keys = rotate(projected[heads : heads + HD], cosine, sine).astype(bf16)
    values = projected[heads + HD :].astype(bf16)
    blocks = jnp.concatenate(
        [queries, jnp.broadcast_to(jnp.concatenate([keys, values]), (GROUP, 2 * HD, tokens))],
        axis=1,
    )
    blocks = lax.all_to_all(jnp.tile(blocks, (copies, 1, 1)), "line", 0, 0, tiled=True)
    def ffn_pass(flips, parts, *now):
        weights = after([ffn_weights[part] for part in parts], *now)
        return [
            (flip, part, pass_on(side_columns(weight, flip), flip))
            for part, weight in zip(parts, weights)
            for flip in flips
        ]

    def held(moves, *others):
        values = lax.optimization_barrier(tuple(value for f, p, value in moves) + others)
        return [(f, p, v) for (f, p, unused), v in zip(moves, values)], values[len(moves) :]

    gathering = slab_gather(after(cotangent, *box["now"]), True)
    first = next(gathering)
    ffn_moves = ffn_pass(near + middle, (0,), first[0])
    ffn_moves, (blocks, *first) = held(ffn_moves, blocks, *first)
    late_moves = ffn_pass(near + middle, (1,), ffn_moves[-1][2])
    second = gathering.send(first)
    attended, ordered, floats, logs = attend_forward(
        blocks, sort_order, back_order, query_range, span, size
    )

    def from_heads(blocks):
        got = lax.all_to_all(blocks, "line", 0, 0, tiled=True)
        return got.reshape((copies, GROUP) + got.shape[1:])

    def add_copies(got):
        return got[0] if copies == 1 else jnp.sum(got.astype(f32), axis=0).astype(bf16)

    own_output = lax.dynamic_slice_in_dim(output_weight, side * heads, heads, 0)
    late_moves, (attended, *second) = held(late_moves, attended, *second)
    ffn_moves += late_moves
    third = gathering.send(second)
    late_moves = ffn_pass(far, (0,), attended)

    def attended_task():
        (blocks,) = yield [from_heads(attended)]
        heads_out = add_copies(blocks).reshape(heads, tokens)
        added = yield from slab_reduce(
            lambda start, stop: contract(heads_out[:, start:stop], own_output, 0, 0), tok_dev
        )
        return (heads_out, inputs.astype(f32) + added)

    def rest_task():
        got = yield [v for f, p, v in late_moves] + third
        moves = [(f, p, v) for (f, p, unused), v in zip(late_moves, got)]
        try:
            gathering.send(got[len(late_moves) :])
        except StopIteration as stop:
            box["cotangent"] = stop.value
        more = ffn_pass(far, (1,), *box["now"])
        yield []
        got = yield [v for f, p, v in more]
        return moves + [(f, p, v) for (f, p, unused), v in zip(more, got)]

    run_tasks(
        [
            ("attended", lambda t, b: True, lambda last: attended_task()),
            ("moves", lambda t, b: True, lambda last: rest_task()),
        ],
        box,
    )
    attended, residual = box["attended"]
    slab_cotangent = box["cotangent"]

    ffn_full = jnp.zeros((shards, rows, 2 * units), bf16)
    moves = [(0, part, side_columns(ffn_weights[part], 0)) for part in range(2)]
    for flip, part, block in moves + ffn_moves + box["moves"]:
        ffn_full = lax.dynamic_update_slice(
            ffn_full, block[None], (shard ^ flip, 0, part * units)
        )
    ffn_full = ffn_full.reshape(width, 2 * units)

    normed_two = alone(
        slab_gather((norm_parts(residual)[1] * gain_two).astype(bf16))
    )
    hidden_grad = contract(slab_cotangent, own_down, 1, 1)
    normed_two, hidden_grad = lax.optimization_barrier((normed_two, hidden_grad))
    ffn_pre = contract(normed_two, ffn_full, 1, 0)
    gate_pre, up_pre = ffn_pre[:, :units], ffn_pre[:, units:]
    sigmoid_gate = jax.nn.sigmoid(gate_pre)
    hidden = (gate_pre * sigmoid_gate * up_pre).astype(bf16)
    down_parts = contract(hidden, slab_cotangent, 0, 0).astype(bf16)
    gate_low = (
        hidden_grad * up_pre * sigmoid_gate * (1.0 + gate_pre * (1.0 - sigmoid_gate))
    ).astype(bf16)
    up_low = (hidden_grad * gate_pre * sigmoid_gate).astype(bf16)

    def to_shards(partial):
        return lax.all_to_all(partial, "wshard", 0, 0, tiled=True)

    gate_partial = contract(normed_two, gate_low, 0, 0).astype(bf16).reshape(shards, rows, units)

    def attention_back(last):
        ffn_low = after(jnp.concatenate([gate_low, up_low], axis=1), gate_partial, *box.get("mixed", ()))
        normed_two_grad = yield from slab_reduce(
            lambda start, stop: contract(ffn_low[start:stop], ffn_full, 1, 1), tok_dev
        )
        residual_part, box["ffn_gain"] = norm_back(residual, gain_two, normed_two_grad)
        residual_grad = cotangent.astype(f32) + residual_part
        branch_low = yield from slab_gather(residual_grad.astype(bf16))
        attended_grad = contract(own_output, branch_low, 1, 1).astype(bf16)
        given = jnp.tile(attended_grad.reshape(GROUP, HD, tokens), (copies, 1, 1))
        (given,) = yield [lax.all_to_all(given, "line", 0, 0, tiled=True)]
        box["output_parts"] = contract(attended, branch_low, 1, 0).astype(bf16)
        raw = attend_backward(
            ordered, floats, logs, given, sort_order, back_order, query_range, span, size
        )
        raw, box["output_parts"] = yield [raw, box["output_parts"]]
        (pair_raw,) = yield [from_heads(raw[:, HD:])]
        (query_raw,) = yield [from_heads(after(raw[:, :HD], pair_raw))]
        query_low = rotate(add_copies(query_raw).astype(f32), cosine, -sine).astype(bf16)
        pair_raw = jnp.sum(pair_raw.astype(f32), axis=(0, 1))
        key_low = rotate(pair_raw[:HD], cosine, -sine).astype(bf16)
        value_low = pair_raw[HD:].astype(bf16)
        low = jnp.concatenate([query_low.reshape(heads, tokens), key_low, value_low], axis=0)
        attn_partial = contract(normed_one, low, 0, 1).astype(bf16)
        (box["attn"],) = yield [to_shards(attn_partial.reshape(shards, rows, -1))]
        normed_one_grad = yield from slab_reduce(
            lambda start, stop: contract(low[:, start:stop], attn_weight, 0, 1), tok_dev
        )
        input_part, attn_gain_term = norm_back(inputs.astype(f32), gain_one, normed_one_grad)
        input_grad = residual_grad + input_part
        return (input_grad, jnp.stack([attn_gain_term, box["ffn_gain"]]))

    half_rows = rows // 2

    def feed_forward_back(last):
        gate0 = to_shards(gate_partial[:, :half_rows])
        yield []
        up_partial = contract(normed_two, after(up_low, *box["now"]), 0, 0).astype(bf16)
        (up_partial,) = yield [up_partial.reshape(shards, rows, units)]
        box["gate0"], gate_now = yield [gate0, gate_partial]
        gate1 = to_shards(gate_now[:, half_rows:])
        yield []
        (box["gate1"],) = yield [gate1]
        up_all = to_shards(after(up_partial, *box["now"]))
        yield []
        (box["up"],) = yield [up_all]
        return None

    def feed_forward_out(last):
        low = after(hidden, *box["stage", 1])
        return (
            yield from slab_reduce(
                lambda start, stop: contract(low[start:stop], own_down, 1, 0), tok_dev
            )
        )

    half_width, half_units = width // 2, units // 2

    steps, block = 4, (half_units // 4, half_width)

    def down_chunk(c):
        high, right = c // 2, c % 2

        def source():
            return down_parts, block, lambda i: (high * steps + i, right)

        def put(placed, pieces, sides):
            placed["down"] = place_blocks(
                placed.get("down"),
                pieces,
                sides,
                (halves * units, width),
                (half_units // 2, half_width),
                lambda on, i: (on * 4 + high * 2 + i, right),
            )

        return (source, put, steps)

    def column_chunk(name, c):
        size = rows // 4
        each = shards // steps

        def source():
            if name in box:
                return box[name], (each, size, units), lambda i: (i, c, 0)
            return (
                box[name + str(c // 2)],
                (each, size, units),
                lambda i: (i, c % 2, 0),
            )

        def put(placed, pieces, sides):
            pieces = [piece.reshape(shards, size, units) for piece in pieces]
            placed[name] = place_columns(placed.get(name), pieces, c, sides, 4)

        return (source, put, steps)

    def output_chunk():
        def source():
            return box["output_parts"], block, lambda i: (i % 2, i // 2)

        def put(placed, pieces, sides):
            placed["output"] = place_blocks(
                placed.get("output"),
                pieces,
                sides,
                (halves * heads, width),
                (heads, half_width),
                lambda on, i: (on, i),
            )

        return (source, put, steps)

    def attn_chunk(c):
        size, columns = rows // 2, heads + 2 * HD
        deep, wide, across = size // 128, columns // 128, half_width // 128
        blocks = shards * deep * wide // across

        def source():
            part = box["attn"][:, c * size : (c + 1) * size]
            squares = [
                part[w, h * 128 : (h + 1) * 128, b * 128 : (b + 1) * 128]
                for w in range(shards)
                for b in range(wide)
                for h in range(deep)
            ]
            lines = [
                jnp.concatenate(squares[g * across : (g + 1) * across], axis=1)
                for g in range(blocks)
            ]
            return jnp.concatenate(lines, axis=0), block, lambda i: (i, 0)

        def put(placed, pieces, sides):
            names = ("query", "key", "value")
            totals = [placed[name] for name in names] if "query" in placed else None
            totals = place_attn(totals, pieces, c, sides, size, heads, shards, 2)
            placed.update(zip(names, totals))

        return (source, put, blocks)

    chunks = [down_chunk(c) for c in range(4)]
    chunks += [column_chunk(name, c) for name in ("gate", "up") for c in range(4)]
    chunks += [output_chunk()] + [attn_chunk(c) for c in range(2)]
    placed = {}
    gradients = stream(chunks, placed, box, block)
    sent = gradients.send(lax.optimization_barrier(tuple(next(gradients))))
    run_tasks(
        [
            ("attention", lambda t, b: True, attention_back),
            ("parts", lambda t, b: True, feed_forward_back),
        ],
        box,
    )
    run_tasks([("out", lambda t, b: True, feed_forward_out)], box)
    input_grad, gain_terms = box["attention"]
    gain_sums = sum_everywhere(gain_terms, len(chunks) - 1)
    gain_terms = finish([(gradients, sent), (gain_sums, next(gain_sums))])[1]
    gain_terms = lax.dynamic_slice_in_dim(gain_terms, shard * rows, rows, 1)
    return (
        (residual + box["out"]).astype(bf16),
        input_grad,
        gain_terms[0],
        placed["query"],
        placed["key"],
        placed["value"],
        placed["output"],
        gain_terms[1],
        placed["gate"],
        placed["up"],
        placed["down"],
    )


def solution(mesh):
    shards = mesh.shape["wshard"]
    halves = KVH // shards
    fine = Mesh(
        mesh.devices.reshape(mesh.shape["ctx"] // halves, halves, shards),
        ("line", "xpart", "wshard"),
    )
    every = ("line", "xpart", "wshard")
    in_specs = (
        P(every, None),
        P(),
        P("wshard"),
        P("wshard", None),
        P("wshard", None),
        P("wshard", None),
        P("wshard", None),
        P("wshard"),
        P("wshard", None),
        P("wshard", None),
        P("wshard", None),
        P(every, None),
    )
    out_specs = (
        P(every, None),
        P(every, None),
        P("wshard"),
        P("wshard", None),
        P("wshard", None),
        P("wshard", None),
        P("wshard", None),
        P("wshard"),
        P("wshard", None),
        P("wshard", None),
        P("wshard", None),
    )
    return jax.shard_map(local, mesh=fine, in_specs=in_specs, out_specs=out_specs, check_vma=False)
```
